32 devices in a mesh: ctx: 8 (over z, x), shard: 4 (over y, core).
Axes of the slice: x: 2, y: 2, z: 4, core: 2. Of those that a mesh axis runs over, the one named last changes fastest.
Arguments:
- block_input: bfloat16 [4, 1024, 576], P('shard', 'ctx'), may hold values from -6 to 6
- out_grad: bfloat16 [4, 1024, 576], P('shard', 'ctx'), may hold values from -6 to 6
- positions: int32 [1024], P('ctx'), may hold values from 0 to 1023, as said below
- norm_gains: bfloat16 [2, 576], P(None, 'shard'), may hold values from 0.25 to 1.75
- w_query: bfloat16 [576, 576], P('shard'), may hold values from -0.25 to 0.25
- w_kv: bfloat16 [2, 576, 192], P(None, 'shard'), may hold values from -0.25 to 0.25
- w_out: bfloat16 [576, 576], P('shard'), may hold values from -2 to 2
- w_gate_up: bfloat16 [2, 576, 1536], P(None, 'shard'), may hold values from -0.25 to 0.25
- w_down: bfloat16 [1536, 576], P('shard'), may hold values from -0.15625 to 0.15625
- mom_gains: float32 [2, 576], P(None, 'shard')
- mom_query: float32 [576, 576], P('shard')
- mom_kv: float32 [2, 576, 192], P(None, 'shard')
- mom_out: float32 [576, 576], P('shard')
- mom_gate_up: float32 [2, 576, 1536], P(None, 'shard')
- mom_down: float32 [1536, 576], P('shard')
Outputs:
- block_output: float32 [4, 1024, 576], P('shard', 'ctx')
- input_grad: float32 [4, 1024, 576], P('shard', 'ctx')
- grad_gains: float32 [2, 576], P(None, 'shard')
- grad_query: float32 [576, 576], P('shard')
- grad_kv: float32 [2, 576, 192], P(None, 'shard')
- grad_out: float32 [576, 576], P('shard')
- grad_gate_up: float32 [2, 576, 1536], P(None, 'shard')
- grad_down: float32 [1536, 576], P('shard')
- moment_gains: float32 [2, 576], P(None, 'shard')
- moment_query: float32 [576, 576], P('shard')
- moment_kv: float32 [2, 576, 192], P(None, 'shard')
- moment_out: float32 [576, 576], P('shard')
- moment_gate_up: float32 [2, 576, 1536], P(None, 'shard')
- moment_down: float32 [1536, 576], P('shard')
- momentum_norms: float32 [7], replicated
- new_gains: float32 [2, 576], P(None, 'shard')
- new_query: float32 [576, 576], P('shard')
- new_kv: float32 [2, 576, 192], P(None, 'shard')
- new_out: float32 [576, 576], P('shard')
- new_gate_up: float32 [2, 576, 1536], P(None, 'shard')
- new_down: float32 [1536, 576], P('shard')
The draws below stay inside these ranges and needn't reach their ends.
Inputs may be any that keep to these rules, and one draw needn't show every extreme that they name: Each device's 128 entries are consecutive positions in rising order; all entries together are 0 to 1023, each once.
All inputs are finite; a program needn't handle non-finite values.
Results may differ from the reference program's by a relative error of at most 0.023.
Values may be sent and summed in bfloat16 or wider, within the bound.
No kernel may reach another device: no remote copies, remote signals or barrier semaphores. Data moves between devices by JAX's collectives and lax.ppermute only.
A program may use at most 192 MiB of HBM per device.

```python
import math
import jax
import jax.numpy as jnp
from jax import lax

D = 576
FF = 1536
HEADS = 9
KV_HEADS = 3
HEAD_DIM = 64
TOK_DEV = 128
NS_STEPS = 5
SEQ = 1024
SEQS = 4
ALL_TOKENS = 4096
KEY_BLOCK = 512


def moment_values(key, shape, row_dim):
    base = jax.random.truncated_normal(key, -4.0, 4.0, shape, jnp.float32)
    top = 2.0
    count = shape[row_dim]
    ramp = 1.0 + top * jnp.arange(count, dtype=jnp.float32) / (count - 1)
    view = [1] * len(shape)
    view[row_dim] = count
    return base * ramp.reshape(view) * (0.5 * jnp.sqrt(jnp.float32(ALL_TOKENS)))


def draw_positions(key, part):
    blocks = SEQ // TOK_DEV
    order = jax.random.permutation(key, blocks)
    grid = order[:, None] * TOK_DEV + jnp.arange(TOK_DEV)[None, :]
    return grid.reshape(SEQ).astype(jnp.int32)


def draw_mom_gains(key, part):
    return moment_values(jax.random.fold_in(key, 11), (2, D), 1)


def draw_mom_query(key, part):
    return moment_values(jax.random.fold_in(key, 12), (D, D), 0)


def draw_mom_kv(key, part):
    return moment_values(jax.random.fold_in(key, 13), (2, D, KV_HEADS * HEAD_DIM), 1)


def draw_mom_out(key, part):
    return moment_values(jax.random.fold_in(key, 14), (D, D), 0)


def draw_mom_gate_up(key, part):
    return moment_values(jax.random.fold_in(key, 15), (2, D, FF), 1)


def draw_mom_down(key, part):
    return moment_values(jax.random.fold_in(key, 16), (FF, D), 0)


def level_of(key, shape, pieces, low, top_value):
    loudness, own = 1.0, jax.random.fold_in(key, 6)
    for position, blocks in pieces:
        steps = jnp.exp(jax.random.uniform(jax.random.fold_in(own, position), (blocks,), jnp.float32, low / len(pieces), top_value / len(pieces)))
        loudness = loudness * jnp.repeat(steps, shape[position] // blocks).reshape([-1 if axis == position else 1 for axis in range(len(shape))])
    return loudness


def bell_draw(own_key, dims, deviation, most, pieces=(), held_as=jnp.bfloat16):
    entries = jax.random.normal(own_key, dims, jnp.float32) * deviation
    if len(pieces) > 0:
        entries = level_of(own_key, dims, pieces, -0.22, 0.18) * entries
    return jnp.clip(entries, min=-most, max=most).astype(held_as)


def setup_inputs(seed: int = 0) -> dict:
    key_list = jax.random.split(jax.random.key(seed), 16)
    return {
        "block_input": bell_draw(key_list[0], (SEQS, SEQ, D), 1.0, 6.0, ((0, 4), (1, 8))),
        "out_grad": bell_draw(key_list[1], (SEQS, SEQ, D), 1.0, 6.0, ((0, 4), (1, 8))),
        "positions": draw_positions(jax.random.fold_in(key_list[15], 71), 0),
        "norm_gains": jnp.clip(1.0 + 0.15 * jax.random.normal(key_list[3], (2, D), jnp.float32), 0.25, 1.75).astype(jnp.bfloat16),
        "w_query": bell_draw(key_list[4], (D, D), D ** -0.5, 0.25, ((0, 4),)),
        "w_kv": bell_draw(key_list[5], (2, D, KV_HEADS * HEAD_DIM), D ** -0.5, 0.25, ((1, 4),)),
        "w_out": bell_draw(key_list[6], (D, D), (max(1, D * 16 // SEQ)) ** -0.5, 2.0, ((0, 4),)),
        "w_gate_up": bell_draw(key_list[7], (2, D, FF), D ** -0.5, 0.25, ((1, 4),)),
        "w_down": bell_draw(key_list[8], (FF, D), FF ** -0.5, 0.15625, ((0, 4),)),
        "mom_gains": draw_mom_gains(jax.random.fold_in(key_list[15], 71), 0),
        "mom_query": draw_mom_query(jax.random.fold_in(key_list[15], 71), 0),
        "mom_kv": draw_mom_kv(jax.random.fold_in(key_list[15], 71), 0),
        "mom_out": draw_mom_out(jax.random.fold_in(key_list[15], 71), 0),
        "mom_gate_up": draw_mom_gate_up(jax.random.fold_in(key_list[15], 71), 0),
        "mom_down": draw_mom_down(jax.random.fold_in(key_list[15], 71), 0),
    }


NS_A = 3.4445
NS_B = -4.775
NS_C = 2.0315
NORM_EPS = 1e-05
MOMENTUM = 0.95
RATE = 0.2
SHAPE_SCALE = 0.2
GAIN_RATE = 0.02
SCORE_SCALE = 0.125

@jax.custom_vjp
def low(v):
    return lax.optimization_barrier(v.astype(jnp.bfloat16)).astype(jnp.float32)

@jax.custom_vjp
def low_back(v):
    return v

def low_keep(v):
    return (low(v), None)

def low_pass(kept, grad):
    return (grad,)

def back_keep(v):
    return (v, None)

def back_low(kept, grad):
    return (low(grad),)
low.defvjp(low_keep, low_pass)
low_back.defvjp(back_keep, back_low)

def matmul_high(left, right):
    return jnp.dot(left, right, precision=lax.Precision.HIGHEST)

def rms_scale(values, gain):
    inverse = lax.rsqrt(lax.optimization_barrier(jnp.mean(values * values, axis=-1, keepdims=True)) + NORM_EPS)
    return values * inverse * gain

def rope_tables(positions):
    half = HEAD_DIM // 2
    inverse = 1.0 / 10000.0 ** (jnp.arange(half, dtype=jnp.float32) * 2.0 / HEAD_DIM)
    angles = positions.astype(jnp.float32)[:, None] * inverse[None, :]
    return (jnp.cos(angles)[:, None, :], jnp.sin(angles)[:, None, :])

def rotate(rows, cosine, sine):
    half = rows.shape[-1] // 2
    first = rows[..., :half]
    second = rows[..., half:]
    return jnp.concatenate([first * cosine - second * sine, second * cosine + first * sine], axis=-1)

def attend_rows(query_block, query_pos, keys, values, positions):
    scores = jnp.einsum('qhgd,khd->hgqk', query_block, keys, precision=lax.Precision.HIGHEST) * SCORE_SCALE
    scores = low_back(scores)
    allowed = positions[None, :] <= query_pos[:, None]
    scores = jnp.where(allowed[None, None], scores, -jnp.inf)
    peak = lax.optimization_barrier(jnp.max(scores, axis=-1, keepdims=True))
    weights = jnp.exp(scores - peak)
    probs = low(weights / lax.optimization_barrier(jnp.sum(weights, axis=-1, keepdims=True)))
    return jnp.einsum('hgqk,khd->qhgd', probs, values, precision=lax.Precision.HIGHEST)

def layer(tokens, norm_gains, w_query, w_kv, w_out, w_gate_up, w_down, positions):
    cosine, sine = rope_tables(positions)
    groups = HEADS // KV_HEADS
    normed = low(rms_scale(tokens, norm_gains[0]))
    query = low_back(matmul_high(normed, w_query)).reshape(SEQ, HEADS, HEAD_DIM)
    query = low(rotate(query, cosine, sine)).reshape(SEQ, KV_HEADS, groups, HEAD_DIM)
    keys = low_back(matmul_high(normed, w_kv[0])).reshape(SEQ, KV_HEADS, HEAD_DIM)
    keys = low(rotate(keys, cosine, sine))
    values = low(low_back(matmul_high(normed, w_kv[1]))).reshape(SEQ, KV_HEADS, HEAD_DIM)
    count = SEQ // KEY_BLOCK

    def attend_block(pair):
        return attend_rows(pair[0], pair[1], keys, values, positions)
    blocks = lax.map(jax.checkpoint(attend_block), (query.reshape(count, KEY_BLOCK, KV_HEADS, groups, HEAD_DIM), positions.reshape(count, KEY_BLOCK)))
    attn = low(low_back(blocks.reshape(SEQ, HEADS * HEAD_DIM)))
    middle = tokens + low_back(matmul_high(attn, w_out))
    normed_mid = low(rms_scale(middle, norm_gains[1]))
    gate = low_back(matmul_high(normed_mid, w_gate_up[0]))
    up_rows = low_back(matmul_high(normed_mid, w_gate_up[1]))
    hidden = low(gate * jax.nn.sigmoid(gate) * up_rows)
    return middle + matmul_high(hidden, w_down)

def orthogonalize(matrix):
    iterate = matrix / (jnp.sqrt(jnp.sum(matrix * matrix)) + 1e-07)
    flipped = matrix.shape[0] > matrix.shape[1]
    if flipped:
        iterate = iterate.T
    for sweep in range(NS_STEPS):
        gram = matmul_high(iterate, iterate.T)
        polynomial = NS_B * gram + NS_C * matmul_high(gram, gram)
        iterate = NS_A * iterate + matmul_high(polynomial, iterate)
    if flipped:
        iterate = iterate.T
    return iterate

def step_of(matrix):
    return -RATE * SHAPE_SCALE * math.sqrt(max(matrix.shape[0], matrix.shape[1])) * orthogonalize(matrix)

def root_mean(matrix):
    return jnp.sqrt(jnp.sum(matrix * matrix) / matrix.size)

def reference(block_input, out_grad, positions, norm_gains, w_query, w_kv, w_out, w_gate_up, w_down, mom_gains, mom_query, mom_kv, mom_out, mom_gate_up, mom_down):
    params = (norm_gains.astype(jnp.float32), w_query.astype(jnp.float32), w_kv.astype(jnp.float32), w_out.astype(jnp.float32), w_gate_up.astype(jnp.float32), w_down.astype(jnp.float32))

    def forward(tokens, gains, query_w, kv_w, out_w, gate_up_w, down_w):
        return layer(tokens, gains, query_w, kv_w, out_w, gate_up_w, down_w, positions)

    def sequence_step(totals, pair):
        output, pullback = jax.vjp(forward, pair[0].astype(jnp.float32), params[0], params[1], params[2], params[3], params[4], params[5])
        grads = pullback(pair[1].astype(jnp.float32))
        return (tuple((total + grad for total, grad in zip(totals, grads[1:]))), (output, grads[0]))
    zeros = tuple((jnp.zeros(param.shape, jnp.float32) for param in params))
    totals, outs = lax.scan(sequence_step, zeros, (block_input, out_grad))
    olds = (mom_gains, mom_query, mom_kv, mom_out, mom_gate_up, mom_down)
    moments = tuple((MOMENTUM * old + grad for old, grad in zip(olds, totals)))
    members = [moments[1], moments[2][0], moments[2][1], moments[3], moments[4][0], moments[4][1], moments[5]]
    momentum_norms = jnp.stack([root_mean(member) for member in members])
    new_gains = params[0] + -GAIN_RATE / math.sqrt(ALL_TOKENS) * moments[0]
    new_query = params[1] + step_of(moments[1])
    new_kv = params[2] + jnp.stack([step_of(moments[2][0]), step_of(moments[2][1])])
    new_out = params[3] + step_of(moments[3])
    new_gate_up = params[4] + jnp.stack([step_of(moments[4][0]), step_of(moments[4][1])])
    new_down = params[5] + step_of(moments[5])
    return (outs[0], outs[1], totals[0], totals[1], totals[2], totals[3], totals[4], totals[5], moments[0], moments[1], moments[2], moments[3], moments[4], moments[5], momentum_norms, new_gains, new_query, new_kv, new_out, new_gate_up, new_down)
```

```python
import functools
import math

import jax
import jax.numpy as jnp
from jax import lax
from jax.experimental import pallas as pl
from jax.experimental.pallas import tpu as pltpu
from jax.sharding import Mesh
from jax.sharding import PartitionSpec as P

D = 576
FF = 1536
HEAD_DIM = 64
HEADS = 9
KV_HEADS = 3
GROUPS = 3
KV_WIDTH = 192
NS_STEPS = 5
NS_A = 3.4445
NS_B = -4.775
NS_C = 2.0315
NORM_EPS = 1e-05
MOMENTUM = 0.95
RATE = 0.2
SHAPE_SCALE = 0.2
GAIN_RATE = 0.02
NEG_LARGE = -1e30

bf16 = jnp.bfloat16
f32 = jnp.float32
SHARD = ("y", "core")
CTX = ("hi", "lo")
ALL = ("hi", "lo", "y", "core")
TRADE = ((0, 1), (1, 0))


def dot(left, right):
    return jnp.dot(left, right, preferred_element_type=f32)


def dot_cols(left, right):
    return lax.dot_general(left, right, (((1,), (1,)), ((), ())), preferred_element_type=f32)


def dot_rows(left, right):
    return lax.dot_general(left, right, (((0,), (0,)), ((), ())), preferred_element_type=f32)


def call(body, outs, args, scratch=(), flops=0, smem=(), limit=56):
    moved = sum(a.size * a.dtype.itemsize for a in args)
    specs = [
        pl.BlockSpec(memory_space=pltpu.SMEM if i in smem else pltpu.VMEM)
        for i in range(len(args))
    ]
    return pl.pallas_call(
        body,
        out_shape=[jax.ShapeDtypeStruct(s, d) for s, d in outs],
        in_specs=specs,
        out_specs=[pl.BlockSpec(memory_space=pltpu.VMEM) for _ in outs],
        scratch_shapes=list(scratch),
        compiler_params=pltpu.CompilerParams(vmem_limit_bytes=limit * 2**20),
        cost_estimate=pl.CostEstimate(flops=flops, bytes_accessed=moved, transcendentals=0),
    )(*args)


def turn(chunk, cosine, sine):
    lane = lax.broadcasted_iota(jnp.int32, chunk.shape, 1)
    other = jnp.where(lane % 64 < 32, pltpu.roll(chunk, 96, 1), pltpu.roll(chunk, 32, 1))
    return chunk * cosine + other * sine


def turn_wide(rows, cosine, sine):
    width = rows.shape[1]
    parts = []
    for at in range(0, width, 128):
        if at + 128 <= width:
            parts.append(turn(rows[:, at : at + 128], cosine, sine))
        else:
            tail = rows[:, at:]
            parts.append(turn(jnp.concatenate([tail, tail], axis=1), cosine, sine)[:, :64])
    return jnp.concatenate(parts, axis=1)


def inverse_rms(rows):
    return lax.rsqrt(jnp.mean(rows * rows, axis=1, keepdims=True) + NORM_EPS)


def project_body(tok, xg_ref, w_ref, gains_ref, cos_ref, sin_ref, attn_in_ref, q_ref, kv_ref):
    x = xg_ref[0:tok, 0:D].astype(f32)
    attn_in = (x * inverse_rms(x) * gains_ref[0:1, :]).astype(bf16)
    attn_in_ref[...] = attn_in
    cosine, sine = cos_ref[...], sin_ref[...]
    keys_values = dot(attn_in, w_ref[:, 0 : 2 * KV_WIDTH])
    kv_ref[0:tok, 0:KV_WIDTH] = turn_wide(keys_values[:, 0:KV_WIDTH], cosine, sine).astype(bf16)
    kv_ref[0:tok, KV_WIDTH:] = keys_values[:, KV_WIDTH:].astype(bf16)
    kv_ref[tok:, :] = xg_ref[tok:, 0 : 2 * KV_WIDTH]
    query = dot(attn_in, w_ref[:, 2 * KV_WIDTH :])
    q_ref[...] = turn_wide(query, cosine, sine).astype(bf16) * jnp.asarray(0.125, bf16)


def group_rows(rows, group):
    return jnp.concatenate(
        [
            rows[:, (GROUPS * group + i) * HEAD_DIM : (GROUPS * group + i + 1) * HEAD_DIM]
            for i in range(GROUPS)
        ],
        axis=0,
    )


def ungroup(groups, tok):
    return jnp.concatenate(
        [g[i * tok : (i + 1) * tok, :] for g in groups for i in range(GROUPS)], axis=1
    )


def each_block(count, visit):
    if count <= 8:
        for j in range(count):
            visit(j)
    else:
        lax.fori_loop(0, count, lambda j, c: (visit(j), c)[1], 0)


def attend_body(
    tok, blocks, xg_ref, q_ref, kv_ref, wo_ref, gains_ref,
    attn_f_ref, both_ref, middle_ref, lse_ref, scores_ref, peak_ref, total_ref, mixed_ref,
):
    wide = GROUPS * tok
    x = xg_ref[0:tok, 0:D].astype(f32)
    query_base = xg_ref[tok : tok + 1, 0:1].astype(f32) * tok
    row = lax.broadcasted_iota(jnp.int32, (tok, wide), 0)
    col = lax.broadcasted_iota(jnp.int32, (tok, wide), 1) % tok
    ahead = (row - col).astype(f32)
    q = q_ref[...]
    queries = [group_rows(q, g) for g in range(KV_HEADS)]
    peak_ref[...] = jnp.full(peak_ref.shape, NEG_LARGE, f32)
    total_ref[...] = jnp.zeros(total_ref.shape, f32)
    mixed_ref[...] = jnp.zeros(mixed_ref.shape, f32)

    def first(j):
        allowed = ahead <= query_base - kv_ref[j, tok : tok + 1, 0:1].astype(f32) * tok
        for g in range(KV_HEADS):
            s = dot_cols(kv_ref[j, 0:tok, g * HEAD_DIM : (g + 1) * HEAD_DIM], queries[g])
            s = jnp.where(allowed, s, NEG_LARGE)
            scores_ref[g, pl.ds(j * tok, tok), :] = s
            peak_ref[g : g + 1, :] = jnp.maximum(
                peak_ref[g : g + 1, :], jnp.max(s, axis=0, keepdims=True)
            )

    each_block(blocks, first)

    def second(j):
        for g in range(KV_HEADS):
            p = jnp.exp(scores_ref[g, pl.ds(j * tok, tok), :] - peak_ref[g : g + 1, :])
            total_ref[g : g + 1, :] += jnp.sum(p, axis=0, keepdims=True)
            at = KV_WIDTH + g * HEAD_DIM
            mixed_ref[g] += dot_rows(kv_ref[j, 0:tok, at : at + HEAD_DIM], p.astype(bf16))

    each_block(blocks, second)
    lse_ref[...] = peak_ref[...] + jnp.log(total_ref[...])
    attn_f = ungroup(
        [(mixed_ref[g] / total_ref[g : g + 1, :]).T for g in range(KV_HEADS)], tok
    )
    attn_f_ref[...] = attn_f
    attn_rows = attn_f.astype(bf16)
    middle = x + dot(attn_rows, wo_ref[...])
    middle_ref[...] = middle
    both_ref[0] = (middle * inverse_rms(middle) * gains_ref[1:2, :]).astype(bf16)
    both_ref[1] = attn_rows


def feed_body(ffn_ref, g_ref, wgu_ref, wd_ref, out_ref, dffn_ref, grad_ref):
    part = wd_ref.shape[0]
    ffn_in = ffn_ref[...]
    cotangent = g_ref[...]
    wgu = wgu_ref[...]
    wd = wd_ref[...]
    gate_up = dot(ffn_in, wgu)
    gate, up = gate_up[:, :part], gate_up[:, part:]
    sigma = jax.nn.sigmoid(gate)
    swish = gate * sigma
    hidden = (swish * up).astype(bf16)
    d_hidden = dot_cols(cotangent, wd)
    d_gate = (d_hidden * up * sigma * (1.0 + gate * (1.0 - sigma))).astype(bf16)
    d_up = (d_hidden * swish).astype(bf16)
    both = jnp.concatenate([d_gate, d_up], axis=1)
    dffn_ref[...] = dot_cols(both, wgu).astype(bf16)
    grad_ref[:, 0 : 2 * part] = dot_rows(ffn_in, both).astype(bf16)
    grad_ref[:, 2 * part :] = dot_rows(cotangent, hidden).astype(bf16)
    out_ref[...] = dot(hidden, wd).astype(bf16)


def back_body(
    tok, blocks, dffn_ref, xg_ref, middle_ref, gains_ref, wo_ref, attn_f_ref, q_ref, kv_ref,
    lse_ref, cos_ref, sin_ref,
    dmid_ref, dq_ref, dbranch_ref, dkv_ref, gain_ref, dq_acc,
):
    wide = GROUPS * tok
    query_base = xg_ref[tok : tok + 1, 0:1].astype(f32) * tok
    middle = middle_ref[...]
    inverse = inverse_rms(middle)
    normed = middle * inverse
    d_in = dffn_ref[0].astype(f32)
    for i in range(1, dffn_ref.shape[0]):
        d_in = d_in + dffn_ref[i].astype(f32)
    gain_ref[...] = jnp.sum(d_in * normed, axis=0, keepdims=True)
    scaled = d_in * gains_ref[1:2, :]
    d_middle = xg_ref[0:tok, D:].astype(f32) + inverse * (
        scaled - normed * jnp.mean(scaled * normed, axis=1, keepdims=True)
    )
    dmid_ref[...] = d_middle
    d_branch = d_middle.astype(bf16)
    dbranch_ref[...] = d_branch
    d_attn = dot_cols(d_branch, wo_ref[...]).astype(bf16)
    attn_f = attn_f_ref[...]
    row = lax.broadcasted_iota(jnp.int32, (tok, wide), 0)
    col = lax.broadcasted_iota(jnp.int32, (tok, wide), 1) % tok
    ahead = (row - col).astype(f32)
    q = q_ref[...]
    queries = [group_rows(q, g) for g in range(KV_HEADS)]
    outs = [group_rows(d_attn, g) for g in range(KV_HEADS)]
    product = d_attn.astype(f32) * attn_f
    deltas = [
        jnp.sum(group_rows(product, g).T, axis=0, keepdims=True) for g in range(KV_HEADS)
    ]
    dq_acc[...] = jnp.zeros(dq_acc.shape, f32)

    def visit(j):
        allowed = ahead <= query_base - kv_ref[j, tok : tok + 1, 0:1].astype(f32) * tok
        d_keys, d_values = [], []
        for g in range(KV_HEADS):
            at = KV_WIDTH + g * HEAD_DIM
            key = kv_ref[j, 0:tok, g * HEAD_DIM : (g + 1) * HEAD_DIM]
            value = kv_ref[j, 0:tok, at : at + HEAD_DIM]
            s = dot_cols(key, queries[g])
            p = jnp.where(allowed, jnp.exp(s - lse_ref[g : g + 1, :]), 0.0)
            d_weight = dot_cols(value, outs[g])
            ds = (p * (d_weight - deltas[g])).astype(bf16)
            d_values.append(dot(p.astype(bf16), outs[g]))
            d_keys.append(dot(ds, queries[g]))
            dq_acc[g] += dot_rows(key, ds)
        dkv_ref[j] = jnp.concatenate(d_keys + d_values, axis=1).astype(bf16)

    each_block(blocks, visit)
    d_query = ungroup([dq_acc[g].T * 0.125 for g in range(KV_HEADS)], tok)
    dq_ref[...] = turn_wide(d_query, cos_ref[...], -sin_ref[...]).astype(bf16)


def input_body(
    tok, rows, dkv_ref, xg_ref, dmid_ref, gains_ref, w_ref, dq_ref, dbranch_ref, gain_two_ref,
    cos_ref, sin_ref, dx_ref, send_ref,
):
    total = dkv_ref[0].astype(f32)
    for i in range(1, dkv_ref.shape[0]):
        total = total + dkv_ref[i].astype(f32)
    d_key = turn_wide(total[:, :KV_WIDTH], cos_ref[...], -sin_ref[...]).astype(bf16)
    d_value = total[:, KV_WIDTH:].astype(bf16)
    cat = jnp.concatenate([d_key, d_value, dq_ref[...]], axis=1)
    d_in = dot_cols(cat, w_ref[...])
    x = xg_ref[0:tok, 0:D].astype(f32)
    inverse = inverse_rms(x)
    normed = x * inverse
    gain_one = jnp.sum(d_in * normed, axis=0, keepdims=True)
    scaled = d_in * gains_ref[0:1, :]
    dx_ref[...] = dmid_ref[...] + inverse * (
        scaled - normed * jnp.mean(scaled * normed, axis=1, keepdims=True)
    )
    wide = jnp.concatenate([cat, dbranch_ref[...]], axis=1)
    gain_two = gain_two_ref[...]
    count = send_ref.shape[0]
    slot = wide.shape[1] // count
    for s in range(count):
        send_ref[s, 0:tok, :] = wide[:, s * slot : (s + 1) * slot]
        pair = jnp.concatenate(
            [
                gain_one[:, s * rows : (s + 1) * rows],
                gain_two[:, s * rows : (s + 1) * rows],
                jnp.zeros((6, rows), f32),
            ],
            axis=0,
        )
        send_ref[s, tok:, :] = jnp.concatenate(
            [pair, jnp.zeros((8, slot - rows), f32)], axis=1
        ).astype(bf16)


def attn_grad_body(tok, n_lo, where_ref, recv_ref, both_ref, grad_ref, gain_ref):
    me = where_ref[0]
    count = recv_ref.shape[0]
    columns = jnp.concatenate([recv_ref[s, 0:tok, :] for s in range(count)], axis=0)
    attn_in = jnp.concatenate([both_ref[s, 0] for s in range(count)], axis=0)
    attn_rows = jnp.concatenate([both_ref[s, 1] for s in range(count)], axis=0)
    unit = KV_WIDTH
    left = jnp.where(me >= 3, attn_rows, attn_in)
    right = jnp.where(me >= 2, attn_rows, attn_in)
    grad_ref[0:unit, :] = dot_rows(columns[:, 0:unit], left).astype(bf16)
    grad_ref[unit:, :] = dot_rows(columns[:, unit:], right).astype(bf16)
    total = recv_ref[0, tok:, :].astype(f32)
    for s in range(1, count):
        total = total + recv_ref[s, tok:, :].astype(f32)
    gain_ref[...] = total


def sweep(z_ref, zb_ref, count, steps):
    n = z_ref.shape[0]
    row = lax.broadcasted_iota(jnp.int32, (n, n), 0)
    col = lax.broadcasted_iota(jnp.int32, (n, n), 1)
    eye = jnp.where(row == col, jnp.where(row < count, 1.0, 0.0), 0.0)
    for _ in range(steps):
        zb = z_ref[...].astype(bf16)
        zb_ref[...] = zb
        gram = dot_cols(zb, zb)
        center = jnp.sum(gram * eye) / count.astype(f32)
        rest = gram - center * eye
        rest_b = rest.astype(bf16)
        square = dot(rest_b, rest_b)
        poly = (NS_C * square + (NS_B + 2.0 * NS_C * center) * rest).astype(bf16)
        lead = NS_A + NS_B * center + NS_C * center * center
        z_ref[...] = lead * z_ref[...] + dot(poly, zb_ref[...])


def rms_rows(total, entries):
    value = jnp.sqrt(jnp.full((8, 128), total, f32) / entries)
    high = value.astype(bf16)
    low = (value - high.astype(f32)).astype(bf16)
    return high, low


def feed_ns_body(swap_ref, grad_ref, old_ref, out_ref, norm_ref, z_ref, zb_ref):
    rowwise = swap_ref[0] == 1
    parts, height, width = grad_ref.shape
    rows = height // parts
    total = jnp.zeros((), f32)
    for b in range(parts):
        for s in range(parts):
            across = old_ref[s, b * rows : (b + 1) * rows, :].astype(f32)
            along = old_ref[b, s * rows : (s + 1) * rows, :].astype(f32)
            old = jnp.where(rowwise, across, along)
            m = MOMENTUM * old + grad_ref[b, s * rows : (s + 1) * rows, :].astype(f32)
            total = total + jnp.sum(m * m)
            z_ref[s * rows : (s + 1) * rows, b * width : (b + 1) * width] = m
    scale = 1.0 / (jnp.sqrt(jnp.full((1, 1), total, f32)) + 1e-07)
    z_ref[...] = z_ref[...] * scale
    sweep(z_ref, zb_ref, jnp.int32(height), NS_STEPS)
    for b in range(parts):
        for s in range(parts):
            block = z_ref[s * rows : (s + 1) * rows, b * width : (b + 1) * width].astype(bf16)

            @pl.when(rowwise)
            def _():
                out_ref[s, b * rows : (b + 1) * rows, :] = block

            @pl.when(jnp.logical_not(rowwise))
            def _():
                out_ref[b, s * rows : (s + 1) * rows, :] = block

    high, low = rms_rows(total, height * width * parts)
    norm_ref[0] = high
    norm_ref[1] = low


def attn_ns_body(info_ref, grad_ref, old_ref, out_ref, gout_ref, norm_ref, z_ref, zb_ref, y_ref):
    shift, count = info_ref[0], info_ref[1]
    pieces, slots, height, width = grad_ref.shape
    for i in range(slots):
        for c in range(pieces):
            at = (i * pieces + c) * height
            y_ref[at : at + height, :] = grad_ref[c, i].astype(f32)
    g = jnp.where(shift == 0, y_ref[0:D, :], y_ref[KV_WIDTH : KV_WIDTH + D, :])
    row = lax.broadcasted_iota(jnp.int32, (D, D), 0)
    keep = row < count
    g = jnp.where(keep, g, 0.0)
    gout_ref[...] = g.T.astype(bf16)
    m = jnp.where(keep, MOMENTUM * old_ref[...].astype(f32).T + g, 0.0)
    total = jnp.sum(m * m)
    scale = 1.0 / (jnp.sqrt(jnp.full((1, 1), total, f32)) + 1e-07)
    z_ref[...] = m * scale
    sweep(z_ref, zb_ref, count, NS_STEPS)
    out_ref[...] = z_ref[...].T.astype(bf16)
    high, low = rms_rows(total, (count * D).astype(f32))
    norm_ref[0] = high
    norm_ref[1] = low


def trade(x, axis):
    return lax.ppermute(x, axis, TRADE)


def spread(x, axis, size):
    return lax.all_to_all(jnp.broadcast_to(x[None], (size,) + x.shape), axis, 0, 0, tiled=True)


def deal(x, axis):
    return lax.all_to_all(x, axis, 0, 0, tiled=True)


def in_order(index, mine, other):
    return jnp.stack([jnp.where(index == 0, mine, other), jnp.where(index == 0, other, mine)])


def on_device(
    n_hi, n_lo, block_input, out_grad, positions, norm_gains, w_query, w_kv, w_out, w_gate_up,
    w_down, mom_gains, mom_query, mom_kv, mom_out, mom_gate_up, mom_down,
):
    tok = block_input.shape[1]
    rows = w_query.shape[0]
    part = w_down.shape[0]
    n_shard = 4
    n_ctx = n_hi * n_lo
    blocks = 2 * n_lo
    at_hi, at_y, at_core = lax.axis_index("hi"), lax.axis_index("y"), lax.axis_index("core")
    me = at_y * 2 + at_core

    base = (positions[0] // tok).astype(bf16)
    xg = jnp.concatenate([block_input[0], out_grad[0]], axis=1)
    xg = jnp.concatenate([xg, jnp.broadcast_to(base, (8, 2 * D))], axis=0)
    moves = []
    for hi in range(2):
        for lo in range(n_lo):
            for y in range(2):
                for core in range(2):
                    moves.append(
                        (
                            ((hi * n_lo + lo) * 2 + y) * 2 + core,
                            ((core * n_lo + lo) * 2 + y) * 2 + hi,
                        )
                    )
    xg = lax.ppermute(xg, ALL, moves)

    cat = jnp.concatenate([w_kv[0], w_kv[1], w_query, w_out], axis=1)
    gains_row = jnp.concatenate(
        [
            jnp.pad(norm_gains, ((0, 6), (0, cat.shape[1] - norm_gains.shape[1]))),
        ],
        axis=0,
    )
    packed = jnp.concatenate([cat, gains_row], axis=0)
    pair = jnp.stack([packed, trade(packed, "y")])
    far = trade(pair, "core")
    by_core = in_order(at_core, pair, far)
    ordered = jnp.where(at_y == 0, by_core, by_core[:, ::-1])
    ordered = jnp.transpose(ordered, (1, 0, 2, 3)).reshape(n_shard, rows + 8, cat.shape[1])
    whole = ordered[:, :rows].reshape(n_shard * rows, cat.shape[1])
    w_kvq = whole[:, : 2 * KV_WIDTH + D]
    w_o = whole[:, 2 * KV_WIDTH + D :]
    gains = jnp.transpose(ordered[:, rows : rows + 2, :rows], (1, 0, 2)).reshape(2, D).astype(f32)

    gu = w_gate_up.reshape(2, rows, n_shard, part).transpose(2, 1, 0, 3)
    gu = deal(gu.reshape(n_shard, rows, 2 * part), SHARD).reshape(n_shard * rows, 2 * part)
    cot = lax.all_gather(xg[:tok, D:], SHARD, axis=0, tiled=True)

    pos = xg[tok, 0].astype(f32) * tok + jnp.arange(tok, dtype=f32)
    half = HEAD_DIM // 2
    lane = jnp.arange(128)
    inverse = 1.0 / 10000.0 ** ((lane % half).astype(f32) * 2.0 / HEAD_DIM)
    angles = pos[:, None] * inverse[None, :]
    cosine = jnp.cos(angles)
    sine = jnp.sin(angles) * jnp.where(lane % HEAD_DIM < half, -1.0, 1.0)[None, :]

    attn_in, query, kv = call(
        functools.partial(project_body, tok),
        [((tok, D), bf16), ((tok, D), bf16), ((tok + 8, 2 * KV_WIDTH), bf16)],
        (xg, w_kvq, gains, cosine, sine),
        flops=2 * tok * D * 960,
    )
    kv_all = lax.all_gather(kv, ("lo", "core"), axis=0, tiled=False)
    kv_all = kv_all.reshape(blocks, tok + 8, 2 * KV_WIDTH)
    wide = GROUPS * tok
    attn_f, both, middle, lse = call(
        functools.partial(attend_body, tok, blocks),
        [((tok, D), f32), ((2, tok, D), bf16), ((tok, D), f32), ((KV_HEADS, wide), f32)],
        (xg, query, kv_all, w_o, gains),
        scratch=(
            pltpu.VMEM((KV_HEADS, blocks * tok, wide), f32),
            pltpu.VMEM((KV_HEADS, wide), f32),
            pltpu.VMEM((KV_HEADS, wide), f32),
            pltpu.VMEM((KV_HEADS, HEAD_DIM, wide), f32),
        ),
        flops=4 * HEADS * tok * blocks * tok * HEAD_DIM,
    )
    ffn_all = lax.all_gather(both[0], SHARD, axis=0, tiled=True)
    out_part, dffn_part, feed_grad = call(
        feed_body,
        [((n_shard * tok, D), bf16), ((n_shard * tok, D), bf16), ((D, 3 * part), bf16)],
        (ffn_all, cot, gu, w_down),
        flops=2 * n_shard * tok * D * part * 9,
    )
    dffn = deal(dffn_part.reshape(n_shard, tok, D), SHARD)
    out_sum = deal(out_part.reshape(n_shard, tok, D), SHARD)
    output = middle + jnp.sum(out_sum.astype(f32), axis=0)

    def reduce_ctx(grad):
        height = grad.shape[0] // n_ctx
        got = deal(grad.reshape(n_lo, n_hi * height, grad.shape[1]), "lo")
        total = jnp.sum(got.astype(f32), axis=0).reshape(n_hi, height, grad.shape[1])
        mine = lax.dynamic_index_in_dim(total, at_hi, 0, False)
        other = lax.dynamic_index_in_dim(total, 1 - at_hi, 0, False)
        return mine + trade(other.astype(bf16), "hi").astype(f32)

    def spread_ctx(piece):
        other = trade(piece, "hi")
        return spread(in_order(at_hi, piece, other), "lo", n_lo)

    feed_piece = reduce_ctx(feed_grad).astype(bf16)
    height = feed_piece.shape[0]
    feed_piece = feed_piece.reshape(height, 3, part).transpose(1, 0, 2)
    feed_piece = jnp.concatenate([feed_piece, feed_piece[:1]], axis=0)
    feed_piece = deal(feed_piece, SHARD)
    feed_full = spread_ctx(feed_piece)
    feed_full = feed_full.reshape(n_ctx, n_shard, height, part).transpose(1, 0, 2, 3)
    feed_full = feed_full.reshape(n_shard, D, part)

    def by_rows(x):
        return x.reshape(n_shard, n_shard, rows, part).transpose(1, 0, 2, 3).reshape(x.shape)

    rowwise = me != 2
    feed_grad_back = deal(jnp.where(rowwise, by_rows(feed_full), feed_full), SHARD)

    old_gu = mom_gate_up.astype(bf16).reshape(2, rows, n_shard, part).transpose(0, 2, 1, 3)
    old_gu = old_gu.reshape(2, n_shard * rows, part)
    old_down = mom_down.astype(bf16).T[None]
    feed_old = deal(jnp.concatenate([old_gu, old_down, old_down], axis=0), SHARD)
    feed_ortho, feed_norm = call(
        feed_ns_body,
        [((n_shard, D, part), bf16), ((2, 8, 128), bf16)],
        (rowwise.astype(jnp.int32)[None], feed_full, feed_old),
        scratch=(pltpu.VMEM((D, FF), f32), pltpu.VMEM((D, FF), bf16)),
        flops=NS_STEPS * (4 * D * D * FF + 2 * D * D * D),
        smem=(0,),
    )

    d_middle, d_query, d_branch, dkv, gain_two = call(
        functools.partial(back_body, tok, blocks),
        [
            ((tok, D), f32), ((tok, D), bf16), ((tok, D), bf16),
            ((blocks, tok, 2 * KV_WIDTH), bf16), ((1, D), f32),
        ],
        (dffn, xg, middle, gains, w_o, attn_f, query, kv_all, lse, cosine, sine),
        scratch=(pltpu.VMEM((KV_HEADS, HEAD_DIM, wide), f32),),
        flops=10 * HEADS * tok * blocks * tok * HEAD_DIM,
    )
    dkv = deal(dkv, ("lo", "core"))
    d_input, sends = call(
        functools.partial(input_body, tok, rows),
        [((tok, D), f32), ((n_shard, tok + 8, 2 * KV_WIDTH), bf16)],
        (dkv, xg, d_middle, gains, w_kvq, d_query, d_branch, gain_two, cosine, sine),
        flops=2 * tok * D * 960,
    )
    results = lax.ppermute(jnp.stack([output, d_input]).astype(bf16), ALL, moves).astype(f32)

    both_all = lax.all_gather(jnp.stack([attn_in, both[1]]), SHARD, axis=0)
    both_all = both_all.reshape(n_shard, 2, tok, D)
    received = deal(sends, SHARD)
    attn_grad, gain_part = call(
        functools.partial(attn_grad_body, tok, n_lo),
        [((2 * KV_WIDTH, D), bf16), ((8, 2 * KV_WIDTH), f32)],
        (me.astype(jnp.int32)[None], received, both_all),
        flops=2 * n_shard * tok * D * 384,
        smem=(0,),
    )
    step = 2 * KV_WIDTH // n_ctx
    gain_rows = jnp.pad(gain_part, ((0, 0), (0, D - 2 * KV_WIDTH))).astype(bf16)
    body = jnp.concatenate(
        [
            attn_grad.reshape(n_lo, n_hi * step, D),
            jnp.broadcast_to(gain_rows[None], (n_lo, 8, D)),
        ],
        axis=1,
    )
    got = jnp.sum(deal(body, "lo").astype(f32), axis=0)
    pieces = got[: n_hi * step].reshape(n_hi, step, D)
    mine = jnp.concatenate(
        [lax.dynamic_index_in_dim(pieces, at_hi, 0, False), got[n_hi * step :]], axis=0
    )
    other = jnp.concatenate(
        [lax.dynamic_index_in_dim(pieces, 1 - at_hi, 0, False), got[n_hi * step :]], axis=0
    )
    total = mine + trade(other.astype(bf16), "hi").astype(f32)
    grad_gains = total[step : step + 2, :rows].astype(bf16).astype(f32)
    attn_pieces = lax.all_gather(total[:step].astype(bf16), SHARD, axis=0)
    attn_pieces = attn_pieces.reshape(n_shard, step, D)
    start = jnp.where(me == 0, 1, jnp.where(me == 2, 2, 0))
    attn_full = spread_ctx(lax.dynamic_slice_in_dim(attn_pieces, start, 2, 0))
    attn_full = attn_full.reshape(n_ctx, 2, step, D)

    widen = ((0, 0), (0, D - KV_WIDTH))
    attn_old = jnp.stack(
        [mom_query, jnp.pad(mom_kv[0], widen), mom_out, jnp.pad(mom_kv[1], widen)]
    ).astype(bf16)
    attn_old = deal(attn_old, SHARD).reshape(D, D)
    shift = jnp.where(me >= 2, 1, 0)
    count = jnp.where(me % 2 == 0, D, KV_WIDTH)
    attn_ortho, attn_grad_full, attn_norm = call(
        attn_ns_body,
        [((D, D), bf16), ((D, D), bf16), ((2, 8, 128), bf16)],
        (jnp.stack([shift, count]).astype(jnp.int32), attn_full, attn_old),
        scratch=(
            pltpu.VMEM((D, D), f32), pltpu.VMEM((D, D), bf16),
            pltpu.VMEM((4 * KV_WIDTH, D), f32),
        ),
        flops=NS_STEPS * 6 * D * D * D,
        smem=(0,),
    )
    norm_rows = jnp.concatenate(
        [feed_norm[:, 0, :], attn_norm[:, 0, :], jnp.zeros((4, 128), bf16)], axis=0
    )
    norm_rows = jnp.pad(norm_rows, ((0, 0), (0, D - 128)))
    attn_slots = jnp.concatenate(
        [
            attn_ortho.reshape(n_shard, rows, D), attn_grad_full.reshape(n_shard, rows, D),
            jnp.broadcast_to(norm_rows[None], (n_shard, 8, D)),
        ],
        axis=1,
    )
    attn_back = deal(attn_slots, SHARD)
    feed_back = deal(feed_ortho, SHARD)

    norms = attn_back[:, 2 * rows :, 0].astype(f32)
    feed_n = norms[:, 0] + norms[:, 1]
    attn_n = norms[:, 2] + norms[:, 3]
    momentum_norms = jnp.stack(
        [attn_n[0], attn_n[1], attn_n[3], attn_n[2], feed_n[0], feed_n[1], feed_n[2]]
    )

    def feed_rows(x):
        gate_up = x[:2].reshape(2, n_shard, rows, part).transpose(0, 2, 1, 3)
        return gate_up.reshape(2, rows, n_shard * part).astype(f32), x[2].T.astype(f32)

    def attn_rows_of(x):
        kv_rows = jnp.stack([x[1, :, :KV_WIDTH], x[3, :, :KV_WIDTH]])
        return x[0].astype(f32), kv_rows.astype(f32), x[2].astype(f32)

    grad_gate_up, grad_down = feed_rows(feed_grad_back)
    ortho_gate_up, ortho_down = feed_rows(feed_back)
    grad_query, grad_kv, grad_out = attn_rows_of(attn_back[:, rows : 2 * rows])
    ortho_query, ortho_kv, ortho_out = attn_rows_of(attn_back[:, :rows])

    grads = (grad_gains, grad_query, grad_kv, grad_out, grad_gate_up, grad_down)
    olds = (mom_gains, mom_query, mom_kv, mom_out, mom_gate_up, mom_down)
    moments = tuple(MOMENTUM * old + grad for old, grad in zip(olds, grads))
    all_tokens = tok * n_ctx * n_shard
    new_gains = norm_gains.astype(f32) + -GAIN_RATE / math.sqrt(all_tokens) * moments[0]
    wide_rate = -RATE * SHAPE_SCALE
    news = tuple(
        weight.astype(f32) + wide_rate * math.sqrt(long) * ortho
        for weight, ortho, long in (
            (w_query, ortho_query, D), (w_kv, ortho_kv, D), (w_out, ortho_out, D),
            (w_gate_up, ortho_gate_up, FF), (w_down, ortho_down, FF),
        )
    )
    return (
        (results[0][None], results[1][None]) + grads + moments + (momentum_norms, new_gains) + news
    )


def solution(mesh):
    n_ctx = mesh.shape["ctx"]
    split = Mesh(mesh.devices.reshape(2, n_ctx // 2, 2, 2), ALL)
    tokens = P(SHARD, CTX, None)
    first, second, gains = P(SHARD, None), P(None, SHARD, None), P(None, SHARD)
    weights = (gains, first, second, first, second, first)
    return jax.shard_map(
        functools.partial(on_device, 2, n_ctx // 2),
        mesh=split,
        in_specs=(tokens, tokens, P(CTX)) + weights + weights,
        out_specs=(tokens, tokens) + weights + weights + (P(),) + weights,
        check_vma=False,
    )
```

```python
import functools
import math

import jax
import jax.numpy as jnp
from jax import lax
from jax.experimental import pallas as pl
from jax.experimental.pallas import tpu as pltpu
from jax.sharding import Mesh
from jax.sharding import PartitionSpec as P

D = 576
FF = 1536
HEAD_DIM = 64
HEADS = 9
KV_HEADS = 3
GROUPS = 3
KV_WIDTH = 192
NS_STEPS = 5
NS_A = 3.4445
NS_B = -4.775
NS_C = 2.0315
NORM_EPS = 1e-05
MOMENTUM = 0.95
RATE = 0.2
SHAPE_SCALE = 0.2
GAIN_RATE = 0.02
NEG_LARGE = -1e30

bf16 = jnp.bfloat16
f32 = jnp.float32
SHARD = ("y", "core")
LO = ("lh", "lx")
OWNER = ("lx", "core")
CTX = ("hi", "lh", "lx")
ALL = ("hi", "lh", "lx", "y", "core")
TRADE = ((0, 1), (1, 0))


def dot(left, right):
    return jnp.dot(left, right, preferred_element_type=f32)


def dot_cols(left, right):
    return lax.dot_general(left, right, (((1,), (1,)), ((), ())), preferred_element_type=f32)


def dot_rows(left, right):
    return lax.dot_general(left, right, (((0,), (0,)), ((), ())), preferred_element_type=f32)


def call(body, outs, args, scratch=(), smem=(), hold=(), limit=56):
    count = len(args)
    spaces = [pltpu.SMEM if i in smem else pltpu.VMEM for i in range(count)]
    spaces += [pl.ANY] * len(hold)

    def run(*refs):
        body(*refs[:count], *refs[count + len(hold) :])

    return pl.pallas_call(
        run,
        name=getattr(body, "func", body).__name__,
        out_shape=[jax.ShapeDtypeStruct(s, d) for s, d in outs],
        in_specs=[pl.BlockSpec(memory_space=space) for space in spaces],
        out_specs=[pl.BlockSpec(memory_space=pltpu.VMEM) for _ in outs],
        scratch_shapes=list(scratch),
        compiler_params=pltpu.CompilerParams(vmem_limit_bytes=limit * 2**20),
        cost_estimate=pl.CostEstimate(flops=0, bytes_accessed=1024, transcendentals=0),
    )(*args, *hold)


def after(x, *hold):
    return pl.pallas_call(
        lambda *refs: None,
        name="after",
        out_shape=jax.ShapeDtypeStruct(x.shape, x.dtype),
        in_specs=[pl.BlockSpec(memory_space=pl.ANY)] * (1 + len(hold)),
        out_specs=pl.BlockSpec(memory_space=pl.ANY),
        input_output_aliases={0: 0},
        cost_estimate=pl.CostEstimate(flops=0, bytes_accessed=1024, transcendentals=0),
    )(x, *hold)


def turn(chunk, cosine, sine):
    lane = lax.broadcasted_iota(jnp.int32, chunk.shape, 1)
    other = jnp.where(lane % 64 < 32, pltpu.roll(chunk, 96, 1), pltpu.roll(chunk, 32, 1))
    return chunk * cosine + other * sine


def turn_wide(rows, cosine, sine):
    width = rows.shape[1]
    parts = []
    for at in range(0, width, 128):
        if at + 128 <= width:
            parts.append(turn(rows[:, at : at + 128], cosine, sine))
        else:
            tail = rows[:, at:]
            parts.append(turn(jnp.concatenate([tail, tail], axis=1), cosine, sine)[:, :64])
    return jnp.concatenate(parts, axis=1)


def inverse_rms(rows):
    return lax.rsqrt(jnp.mean(rows * rows, axis=1, keepdims=True) + NORM_EPS)


def pack_body(tok, pos_ref, x_ref, gains_ref, wq_ref, wkv_ref, xs_ref, packed_ref):
    rows = wq_ref.shape[0]
    xs_ref[0:tok, :] = x_ref[...].T
    base = (pos_ref[0] // tok).astype(f32)
    xs_ref[tok:, :] = jnp.full((8, D), base, f32).astype(bf16)
    packed_ref[0:rows, 0:KV_WIDTH] = wkv_ref[0]
    packed_ref[0:rows, KV_WIDTH : 2 * KV_WIDTH] = wkv_ref[1]
    packed_ref[0:rows, 2 * KV_WIDTH :] = wq_ref[...]
    packed_ref[rows:, :] = jnp.zeros((8, packed_ref.shape[1]), bf16)
    packed_ref[rows : rows + 2, 0:rows] = gains_ref[...]


def pack_wide_body(me_ref, wgu_ref, *out_refs):
    me = me_ref[0]
    part = wgu_ref.shape[2] // len(out_refs)
    for j, out_ref in enumerate(out_refs):
        at = pl.multiple_of((me ^ j) * part, 128)
        out_ref[:, 0:part] = wgu_ref[0, :, pl.ds(at, part)]
        out_ref[:, part : 2 * part] = wgu_ref[1, :, pl.ds(at, part)]


def project_body(
    tok, me_ref, xs_ref, p0, p1, p2, p3, cos_ref, sin_ref,
    attn_in_ref, q_ref, kv_ref, w_ref, gains_ref, pieces,
):
    me = me_ref[0]
    rows = p0.shape[0] - 8
    for j, piece in enumerate((p0, p1, p2, p3)):
        at = me ^ j
        w_ref[pl.ds(pl.multiple_of(at * rows, 16), rows), :] = piece[0:rows, :]
        pieces[at] = piece[rows:, 0:256].astype(f32)
    gains = jnp.concatenate([pieces[t, :, 0:rows] for t in range(4)], axis=1)
    gains_ref[...] = gains
    x = xs_ref[0:tok, :].astype(f32)
    attn_in = (x * inverse_rms(x) * gains[0:1, :]).astype(bf16)
    attn_in_ref[...] = attn_in
    cosine, sine = cos_ref[...], sin_ref[...]
    keys_values = dot(attn_in, w_ref[:, 0 : 2 * KV_WIDTH])
    key = turn_wide(keys_values[:, 0:KV_WIDTH], cosine, sine).astype(bf16)
    value = keys_values[:, KV_WIDTH:].astype(bf16)
    for t in range(kv_ref.shape[0]):
        kv_ref[t, 0:tok, 0:KV_WIDTH] = key
        kv_ref[t, 0:tok, KV_WIDTH:] = value
        kv_ref[t, tok:, :] = xs_ref[tok:, 0 : 2 * KV_WIDTH]
    query = dot(attn_in, w_ref[:, 2 * KV_WIDTH :])
    q_ref[...] = turn_wide(query, cosine, sine).astype(bf16) * jnp.asarray(0.125, bf16)


def group_rows(rows, group):
    return jnp.concatenate(
        [
            rows[:, (GROUPS * group + i) * HEAD_DIM : (GROUPS * group + i + 1) * HEAD_DIM]
            for i in range(GROUPS)
        ],
        axis=0,
    )


def ungroup(groups, tok):
    return jnp.concatenate(
        [g[i * tok : (i + 1) * tok, :] for g in groups for i in range(GROUPS)], axis=1
    )


def each_block(count, visit):
    if count <= 8:
        for j in range(count):
            visit(j)
    else:
        lax.fori_loop(0, count, lambda j, c: (visit(j), c)[1], 0)


def attend_body(
    tok, blocks, me_ref, xg_ref, q_ref, kv_ref, p0, p1, p2, p3, gains_ref,
    wo_ref, attn_f_ref, ffn_ref, rows_ref, middle_ref, lse_ref, scores_ref, peak_ref, total_ref, mixed_ref,
):
    wide = GROUPS * tok
    for j, piece in enumerate((p0, p1, p2, p3)):
        rows = piece.shape[0]
        wo_ref[pl.ds(pl.multiple_of((me_ref[0] ^ j) * rows, 16), rows), :] = piece[...]
    x = xg_ref[0:tok, :].astype(f32)
    query_base = xg_ref[tok : tok + 1, 0:1].astype(f32) * tok
    row = lax.broadcasted_iota(jnp.int32, (tok, wide), 0)
    col = lax.broadcasted_iota(jnp.int32, (tok, wide), 1) % tok
    ahead = (row - col).astype(f32)
    q = q_ref[...]
    queries = [group_rows(q, g) for g in range(KV_HEADS)]
    peak_ref[...] = jnp.full(peak_ref.shape, NEG_LARGE, f32)
    total_ref[...] = jnp.zeros(total_ref.shape, f32)
    mixed_ref[...] = jnp.zeros(mixed_ref.shape, f32)

    def first(j):
        allowed = ahead <= query_base - kv_ref[j, tok : tok + 1, 0:1].astype(f32) * tok
        for g in range(KV_HEADS):
            s = dot_cols(kv_ref[j, 0:tok, g * HEAD_DIM : (g + 1) * HEAD_DIM], queries[g])
            s = jnp.where(allowed, s, NEG_LARGE)
            scores_ref[g, j] = s
            peak_ref[g : g + 1, :] = jnp.maximum(
                peak_ref[g : g + 1, :], jnp.max(s, axis=0, keepdims=True)
            )

    each_block(blocks, first)

    def second(j):
        for g in range(KV_HEADS):
            p = jnp.exp(scores_ref[g, j] - peak_ref[g : g + 1, :])
            total_ref[g : g + 1, :] += jnp.sum(p, axis=0, keepdims=True)
            at = KV_WIDTH + g * HEAD_DIM
            mixed_ref[g] += dot_rows(kv_ref[j, 0:tok, at : at + HEAD_DIM], p.astype(bf16))

    each_block(blocks, second)
    lse_ref[...] = peak_ref[...] + jnp.log(total_ref[...])
    attn_f = ungroup(
        [(mixed_ref[g] / total_ref[g : g + 1, :]).T for g in range(KV_HEADS)], tok
    )
    attn_f_ref[...] = attn_f
    attn_rows = attn_f.astype(bf16)
    middle = x + dot(attn_rows, wo_ref[...])
    middle_ref[...] = middle
    ffn_ref[...] = (middle * inverse_rms(middle) * gains_ref[1:2, :]).astype(bf16)
    rows_ref[...] = attn_rows


def feed_body(
    me_ref, lo_ref, ffn_ref, g0, g1, g2, g3, p0, p1, p2, p3, wd_ref, out_ref, dffn_ref, *rest
):
    grad_refs, (cot_ref, wgu_ref, whole_ref) = rest[:-3], rest[-3:]
    part = wd_ref.shape[1]
    tok = g0.shape[1]
    me, lo = me_ref[0], lo_ref[0]
    for j, piece in enumerate((g0, g1, g2, g3)):
        cot_ref[:, pl.ds(pl.multiple_of((me ^ j) * tok, 128), tok)] = piece[...]
    for j, piece in enumerate((p0, p1, p2, p3)):
        rows = piece.shape[0]
        wgu_ref[pl.ds(pl.multiple_of((me ^ j) * rows, 16), rows), :] = piece[...]
    ffn_in = ffn_ref[...]
    cotangent = cot_ref[...]
    wgu = wgu_ref[...]
    wd = wd_ref[...]
    gate_up = dot(ffn_in, wgu)
    gate, up = gate_up[:, :part], gate_up[:, part:]
    sigma = jax.nn.sigmoid(gate)
    swish = gate * sigma
    hidden = (swish * up).astype(bf16)
    d_hidden = dot_rows(cotangent, wd)
    d_gate = (d_hidden * up * sigma * (1.0 + gate * (1.0 - sigma))).astype(bf16)
    d_up = (d_hidden * swish).astype(bf16)
    both = jnp.concatenate([d_gate, d_up], axis=1)
    dffn = dot_cols(both, wgu).astype(bf16)
    out = dot_cols(hidden, wd).astype(bf16)
    for s in range(4):
        dffn_ref[s, 0:tok, :] = dffn[s * tok : (s + 1) * tok, :]
        out_ref[s] = out[s * tok : (s + 1) * tok, :]
    gu_grad = dot_rows(ffn_in, both).astype(bf16)
    down_grad = dot(cotangent, hidden).astype(bf16)
    height = whole_ref.shape[1]
    for t in range(whole_ref.shape[0]):
        whole_ref[t, :, 0 : 2 * part] = gu_grad[t * height : (t + 1) * height, :]
        whole_ref[t, :, 2 * part :] = down_grad[t * height : (t + 1) * height, :]
    for k, grad_ref in enumerate(grad_refs):
        grad_ref[...] = whole_ref[lo ^ k]


def misc_body(tok, me_ref, out_ref, in_ref, rows_ref, *send_refs):
    for j, send in enumerate(send_refs):
        to = me_ref[0] ^ j
        send[0:tok, :] = out_ref[to]
        send[tok:, :] = jnp.where(to == 2, rows_ref[...], in_ref[...])


def attn_old_body(me_ref, mq_ref, mkv_ref, mo_ref, *send_refs):
    rows = mq_ref.shape[0]
    blank = jnp.zeros((rows, D - KV_WIDTH), f32)
    key = jnp.concatenate([mkv_ref[0], blank], axis=1).astype(bf16)
    value = jnp.concatenate([mkv_ref[1], blank], axis=1).astype(bf16)
    query, out = mq_ref[...].astype(bf16), mo_ref[...].astype(bf16)
    for j, send in enumerate(send_refs):
        to = me_ref[0] ^ j
        send[...] = jnp.where(
            to == 0, query, jnp.where(to == 1, key, jnp.where(to == 2, out, value))
        )


def old_body(flags_ref, mgu_ref, md_ref, same_ref, other_ref):
    lx, core = flags_ref[0], flags_ref[1]
    rows = mgu_ref.shape[1]
    part = md_ref.shape[1]

    @pl.when(lx == 0)
    def _():
        for b in range(4):
            at = slice(b * part, (b + 1) * part)
            gate, up = mgu_ref[0, :, at].astype(bf16), mgu_ref[1, :, at].astype(bf16)
            same_ref[b * rows : (b + 1) * rows, :] = jnp.where(core == 0, gate, up)
            other_ref[b * rows : (b + 1) * rows, :] = jnp.where(core == 0, up, gate)

    @pl.when(lx != 0)
    def _():
        down = md_ref[...].astype(bf16)
        same_ref[...] = down
        other_ref[...] = down


def add_pieces_body(*refs):
    total = refs[0][...].astype(f32)
    for piece in refs[1:-1]:
        total = total + piece[...].astype(f32)
    refs[-1][...] = total.astype(bf16)


def add_slots_body(part, total_ref, got_ref, slots_ref):
    total = (total_ref[...].astype(f32) + got_ref[...].astype(f32)).astype(bf16)
    n_lh = slots_ref.shape[0]
    blank = jnp.zeros(slots_ref.shape[4:], bf16)
    for number in range(4):
        piece = total[:, number * part : (number + 1) * part] if number < 3 else blank
        for lh in range(n_lh):
            for y in range(2):
                slots_ref[lh, number // 2, y, number % 2] = piece


def grad_rows_body(flags_ref, grad_ref, same_ref, other_ref):
    core, y, rowwise = flags_ref[1], flags_ref[2], flags_ref[3] == 1
    n_lo, parts, height, part = grad_ref.shape
    chunks = n_lo // parts
    for out_ref, to in ((same_ref, core), (other_ref, 1 - core)):
        s = 2 * y + to

        @pl.when(rowwise)
        def _():
            for b in range(parts):
                for i in range(chunks):
                    at = (b * chunks + i) * height
                    out_ref[at : at + height, :] = grad_ref[s * chunks + i, b]

        @pl.when(jnp.logical_not(rowwise))
        def _():
            for i in range(n_lo):
                out_ref[i * height : (i + 1) * height, :] = grad_ref[i, s]


def back_body(
    tok, blocks, dffn_ref, xg_ref, g_ref, middle_ref, gains_ref, wo_ref, attn_f_ref, q_ref, kv_ref,
    lse_ref, cos_ref, sin_ref,
    dmid_ref, dq_ref, dbranch_ref, dkv_ref, gain_ref, dq_acc,
):
    wide = GROUPS * tok
    query_base = xg_ref[tok : tok + 1, 0:1].astype(f32) * tok
    middle = middle_ref[...]
    inverse = inverse_rms(middle)
    normed = middle * inverse
    d_in = dffn_ref[0, 0:tok, :].astype(f32)
    for i in range(1, dffn_ref.shape[0]):
        d_in = d_in + dffn_ref[i, 0:tok, :].astype(f32)
    gain_ref[...] = jnp.sum(d_in * normed, axis=0, keepdims=True)
    scaled = d_in * gains_ref[1:2, :]
    d_middle = g_ref[...].astype(f32).T + inverse * (
        scaled - normed * jnp.mean(scaled * normed, axis=1, keepdims=True)
    )
    dmid_ref[...] = d_middle
    d_branch = d_middle.astype(bf16)
    dbranch_ref[...] = d_branch
    d_attn = dot_cols(d_branch, wo_ref[...]).astype(bf16)
    attn_f = attn_f_ref[...]
    row = lax.broadcasted_iota(jnp.int32, (tok, wide), 0)
    col = lax.broadcasted_iota(jnp.int32, (tok, wide), 1) % tok
    ahead = (row - col).astype(f32)
    q = q_ref[...]
    queries = [group_rows(q, g) for g in range(KV_HEADS)]
    outs = [group_rows(d_attn, g) for g in range(KV_HEADS)]
    product = d_attn.astype(f32) * attn_f
    deltas = [
        jnp.sum(group_rows(product, g).T, axis=0, keepdims=True) for g in range(KV_HEADS)
    ]
    dq_acc[...] = jnp.zeros(dq_acc.shape, f32)

    def visit(j):
        allowed = ahead <= query_base - kv_ref[j, tok : tok + 1, 0:1].astype(f32) * tok
        d_keys, d_values = [], []
        for g in range(KV_HEADS):
            at = KV_WIDTH + g * HEAD_DIM
            key = kv_ref[j, 0:tok, g * HEAD_DIM : (g + 1) * HEAD_DIM]
            value = kv_ref[j, 0:tok, at : at + HEAD_DIM]
            s = dot_cols(key, queries[g])
            p = jnp.where(allowed, jnp.exp(s - lse_ref[g : g + 1, :]), 0.0)
            d_weight = dot_cols(value, outs[g])
            ds = (p * (d_weight - deltas[g])).astype(bf16)
            d_values.append(dot(p.astype(bf16), outs[g]))
            d_keys.append(dot(ds, queries[g]))
            dq_acc[g] += dot_rows(key, ds)
        dkv_ref[j] = jnp.concatenate(d_keys + d_values, axis=1).astype(bf16)

    each_block(blocks, visit)
    d_query = ungroup([dq_acc[g].T * 0.125 for g in range(KV_HEADS)], tok)
    dq_ref[...] = turn_wide(d_query, cos_ref[...], -sin_ref[...]).astype(bf16)


def input_body(
    tok, rows, me_ref, dkv_ref, xg_ref, dmid_ref, gains_ref, w_ref, dq_ref, dbranch_ref, gain_two_ref,
    cos_ref, sin_ref, dx_ref, s0, s1, s2, s3, send_ref,
):
    total = dkv_ref[0].astype(f32)
    for i in range(1, dkv_ref.shape[0]):
        total = total + dkv_ref[i].astype(f32)
    d_key = turn_wide(total[:, :KV_WIDTH], cos_ref[...], -sin_ref[...]).astype(bf16)
    d_value = total[:, KV_WIDTH:].astype(bf16)
    cat = jnp.concatenate([d_key, d_value, dq_ref[...]], axis=1)
    d_in = dot_cols(cat, w_ref[...])
    x = xg_ref[0:tok, :].astype(f32)
    inverse = inverse_rms(x)
    normed = x * inverse
    gain_one = jnp.sum(d_in * normed, axis=0, keepdims=True)
    scaled = d_in * gains_ref[0:1, :]
    dx_ref[...] = dmid_ref[...] + inverse * (
        scaled - normed * jnp.mean(scaled * normed, axis=1, keepdims=True)
    )
    gain_two = gain_two_ref[...]
    blank = jnp.zeros((tok, D - KV_WIDTH), bf16)
    columns = (
        dq_ref[...], jnp.concatenate([d_key, blank], axis=1), dbranch_ref[...],
        jnp.concatenate([d_value, blank], axis=1),
    )
    for s, column in enumerate(columns):
        send_ref[s, 0:tok, :] = column
        pair = jnp.concatenate(
            [
                gain_one[:, s * rows : (s + 1) * rows],
                gain_two[:, s * rows : (s + 1) * rows],
                jnp.zeros((6, rows), f32),
            ],
            axis=0,
        )
        send_ref[s, tok:, :] = jnp.concatenate(
            [pair, jnp.zeros((8, D - rows), f32)], axis=1
        ).astype(bf16)
    for j, out_ref in enumerate((s0, s1, s2, s3)):
        out_ref[...] = send_ref[me_ref[0] ^ j]


def finish_body(tok, middle_ref, dx_ref, m0, m1, m2, m3, out_ref):
    output = middle_ref[...]
    for piece in (m0, m1, m2, m3):
        output = output + piece[0:tok, :].astype(f32)
    out_ref[0] = output.T.astype(bf16)
    out_ref[1] = dx_ref[...].T.astype(bf16)


def attn_grad_body(tok, me_ref, lo_ref, r0, r1, r2, r3, m0, m1, m2, m3, *rest):
    out_refs, (rows_ref, cols_ref, whole_ref) = rest[:-3], rest[-3:]
    me, lo = me_ref[0], lo_ref[0]
    gain = jnp.zeros((8, D), f32)
    for j, (cols, piece) in enumerate(((r0, m0), (r1, m1), (r2, m2), (r3, m3))):
        rows_ref[j * tok : (j + 1) * tok, :] = piece[tok : 2 * tok, :]
        cols_ref[j * tok : (j + 1) * tok, :] = cols[0:tok, :]
        gain = gain + cols[tok:, :].astype(f32)
    grad = dot_rows(cols_ref[...], rows_ref[...]).astype(bf16)
    gain = gain.astype(bf16)
    height = whole_ref.shape[1] - 8
    for t in range(whole_ref.shape[0]):
        whole_ref[t, 0:height, :] = grad[t * height : (t + 1) * height, :]
        whole_ref[t, height:, :] = gain
    for k, out_ref in enumerate(out_refs):
        out_ref[...] = whole_ref[lo ^ k]


def add_second_body(total_ref, got_ref, slots_ref, gain_ref):
    total = total_ref[...].astype(f32) + got_ref[...].astype(f32)
    height = slots_ref.shape[1]
    piece = total[0:height, :].astype(bf16)
    for t in range(slots_ref.shape[0]):
        slots_ref[t] = piece
    gain_ref[...] = total[height:, :]


def sweeps(z_ref, zb_ref, rest_ref, rest_b_ref, poly_ref, squares, count, block, steps):
    n = z_ref.shape[0]
    row = lax.broadcasted_iota(jnp.int32, (block, n), 0)
    col = lax.broadcasted_iota(jnp.int32, (block, n), 1)
    for _ in range(steps):
        center = squares / count
        slope = NS_B + 2.0 * NS_C * center
        lead = NS_A + NS_B * center + NS_C * center * center
        for at in range(0, n, block):
            here = slice(at, at + block)
            gram = dot_cols(zb_ref[here, :], zb_ref[...])
            mine = jnp.logical_and(row + at == col, (row + at).astype(f32) < count)
            rest = jnp.where(mine, gram - center, gram)
            rest_ref[here, :] = rest
            rest_b_ref[here, :] = rest.astype(bf16)
        for at in range(0, n, block):
            here = slice(at, at + block)
            square = dot(rest_b_ref[here, :], rest_b_ref[...])
            poly_ref[here, :] = (NS_C * square + slope * rest_ref[here, :]).astype(bf16)
        squares = jnp.zeros((1, 1), f32)
        for at in range(0, n, block):
            here = slice(at, at + block)
            z = lead * z_ref[here, :] + dot(poly_ref[here, :], zb_ref[...])
            z_ref[here, :] = z
            squares = squares + jnp.sum(
                jnp.sum(z * z, axis=0, keepdims=True), axis=1, keepdims=True
            )
        zb_ref[...] = z_ref[...].astype(bf16)
    return squares


def normalize(z_ref, zb_ref):
    m = z_ref[...]
    total = jnp.sum(jnp.sum(m * m, axis=0, keepdims=True), axis=1, keepdims=True)
    scale = 1.0 / (jnp.sqrt(total) + 1e-07)
    z = m * scale
    z_ref[...] = z
    zb_ref[...] = z.astype(bf16)
    return total, total * scale * scale


def norm_rows(total, entries, shape):
    value = jnp.broadcast_to(jnp.sqrt(total / entries), shape)
    high = value.astype(bf16).astype(f32)
    row = lax.broadcasted_iota(jnp.int32, shape, 0)
    return jnp.where(row == 0, high, value - high).astype(bf16)


def feed_ns_body(
    steps, flags_ref, grad_ref, o0, o1, o2, o3, z_ref, zb_ref, norm_ref, square_ref,
    rest_ref, rest_b_ref, poly_ref,
):
    rowwise, me = flags_ref[3] == 1, flags_ref[4]
    n_lo, parts, height, part = grad_ref.shape
    rows = D // parts
    for j, old_ref in enumerate((o0, o1, o2, o3)):
        s = me ^ j

        @pl.when(rowwise)
        def _():
            for b in range(parts):
                z_ref[pl.ds(pl.multiple_of(s * rows, 16), rows), b * part : (b + 1) * part] = (
                    MOMENTUM * old_ref[b * rows : (b + 1) * rows, :].astype(f32)
                )

        @pl.when(jnp.logical_not(rowwise))
        def _():
            z_ref[:, pl.ds(pl.multiple_of(s * part, 128), part)] = MOMENTUM * old_ref[...].astype(f32)

    for t in range(n_lo):
        for b in range(parts):
            z_ref[t * height : (t + 1) * height, b * part : (b + 1) * part] += grad_ref[
                t, b
            ].astype(f32)
    total, squares = normalize(z_ref, zb_ref)
    squares = sweeps(
        z_ref, zb_ref, rest_ref, rest_b_ref, poly_ref, squares, jnp.float32(D), D // 2, steps
    )
    square_ref[...] = jnp.broadcast_to(squares, square_ref.shape)
    norm_ref[...] = norm_rows(total, jnp.float32(D * parts * part), (8, part))


def feed_ns_rest_body(
    steps, flags_ref, z_in, zb_in, norm_ref, square_ref, same_ref, other_ref,
    z_ref, zb_ref, rest_ref, rest_b_ref, poly_ref,
):
    core, y, rowwise = flags_ref[1], flags_ref[2], flags_ref[3] == 1
    parts = 4
    rows, part = D // parts, z_ref.shape[1] // parts
    z_ref[...] = z_in[...]
    zb_ref[...] = zb_in[...]
    sweeps(
        z_ref, zb_ref, rest_ref, rest_b_ref, poly_ref, square_ref[0:1, 0:1], jnp.float32(D),
        D // 2, steps,
    )
    norm = norm_ref[...]
    for out_ref, to in ((same_ref, core), (other_ref, 1 - core)):
        s = 2 * y + to
        out_ref[D:, :] = norm

        @pl.when(rowwise)
        def _():
            for b in range(parts):
                out_ref[b * rows : (b + 1) * rows, :] = z_ref[
                    pl.ds(pl.multiple_of(s * rows, 16), rows), b * part : (b + 1) * part
                ].astype(bf16)

        @pl.when(jnp.logical_not(rowwise))
        def _():
            out_ref[0:D, :] = z_ref[:, pl.ds(pl.multiple_of(s * part, 128), part)].astype(bf16)


def attn_ns_body(
    me_ref, grad_ref, m0, m1, m2, m3, out_ref,
    z_ref, zb_ref, rest_ref, rest_b_ref, poly_ref, old_ref,
):
    me = me_ref[0]
    rows = m0.shape[0]
    for j, piece in enumerate((m0, m1, m2, m3)):
        old_ref[pl.ds(pl.multiple_of((me ^ j) * rows, 16), rows), :] = piece[...].astype(f32)
    n_lo, height, _ = grad_ref.shape
    for t in range(n_lo):
        z_ref[t * height : (t + 1) * height, :] = grad_ref[t].astype(f32)
    count = jnp.where(me % 2 == 0, float(D), float(KV_WIDTH))
    grad_rows = z_ref[...].T.astype(bf16)
    z_ref[...] = MOMENTUM * old_ref[...].T + z_ref[...]
    total, squares = normalize(z_ref, zb_ref)
    sweeps(z_ref, zb_ref, rest_ref, rest_b_ref, poly_ref, squares, count, D, NS_STEPS)
    ortho = z_ref[...].T.astype(bf16)
    norm = norm_rows(total, count * D, (8, D))
    for s in range(4):
        out_ref[s, 0:rows, :] = ortho[s * rows : (s + 1) * rows, :]
        out_ref[s, rows : 2 * rows, :] = grad_rows[s * rows : (s + 1) * rows, :]
        out_ref[s, 2 * rows :, :] = norm


def pick(mine, number, refs, piece):
    value = refs[3][piece, :]
    for j in range(3):
        value = jnp.where(mine == (number ^ j), refs[j][piece, :], value)
    return value.astype(f32)


def feed_moment_body(flags_ref, g0, g1, g2, g3, mgu_ref, md_ref, ggu_ref, gd_ref, ngu_ref, nd_ref):
    mine = flags_ref[0] * 2 + flags_ref[1]
    refs = (g0, g1, g2, g3)
    rows = mgu_ref.shape[1]
    part = md_ref.shape[1]
    for number in range(2):
        for b in range(4):
            at = slice(b * part, (b + 1) * part)
            grad = pick(mine, number, refs, slice(b * rows, (b + 1) * rows))
            ggu_ref[number, :, at] = grad
            ngu_ref[number, :, at] = MOMENTUM * mgu_ref[number, :, at] + grad
    grad = pick(mine, 2, refs, slice(0, D))
    gd_ref[...] = grad
    nd_ref[...] = MOMENTUM * md_ref[...] + grad


def feed_new_body(flags_ref, g0, g1, g2, g3, wgu_ref, wd_ref, ngu_ref, nd_ref, norm_ref):
    mine = flags_ref[0] * 2 + flags_ref[1]
    refs = (g0, g1, g2, g3)
    rate = -RATE * SHAPE_SCALE * math.sqrt(FF)
    rows = wgu_ref.shape[1]
    part = wd_ref.shape[1]
    for number in range(2):
        for b in range(4):
            at = slice(b * part, (b + 1) * part)
            ortho = pick(mine, number, refs, slice(b * rows, (b + 1) * rows))
            ngu_ref[number, :, at] = wgu_ref[number, :, at].astype(f32) + rate * ortho
    nd_ref[...] = wd_ref[...].astype(f32) + rate * pick(mine, 2, refs, slice(0, D))
    for number in range(3):
        norm_ref[number] = pick(mine, number, refs, slice(D, D + 8))


def attn_new_body(
    back_ref, wq_ref, wkv_ref, wo_ref, mq_ref, mkv_ref, mo_ref,
    gq, gkv, go, nq, nkv, no, uq, ukv, uo,
):
    rate = -RATE * SHAPE_SCALE * math.sqrt(D)
    rows = wq_ref.shape[0]

    def update(number, width, weight, old):
        ortho = back_ref[number, 0:rows, 0:width].astype(f32)
        grad = back_ref[number, rows : 2 * rows, 0:width].astype(f32)
        return grad, MOMENTUM * old + grad, weight.astype(f32) + rate * ortho

    gq[...], nq[...], uq[...] = update(0, D, wq_ref[...], mq_ref[...])
    go[...], no[...], uo[...] = update(2, D, wo_ref[...], mo_ref[...])
    for i, number in enumerate((1, 3)):
        gkv[i], nkv[i], ukv[i] = update(number, KV_WIDTH, wkv_ref[i], mkv_ref[i])


def trade(x, axis):
    return lax.ppermute(x, axis, TRADE)


def pass_on(x, axis, size, j):
    return lax.ppermute(x, axis, [(i, i ^ j) for i in range(size)])


def spread(x, axis, size):
    return deal(jnp.broadcast_to(x[None], (size,) + x.shape), axis)


def deal(x, axis):
    return lax.all_to_all(x, axis, 0, 0, tiled=True)


def on_device(
    n_hi, n_lo, block_input, out_grad, positions, norm_gains, w_query, w_kv, w_out, w_gate_up,
    w_down, mom_gains, mom_query, mom_kv, mom_out, mom_gate_up, mom_down,
):
    tok = block_input.shape[1]
    rows = w_query.shape[0]
    part = w_down.shape[0]
    n_shard = 4
    n_ctx = n_hi * n_lo
    blocks = 2 * n_lo
    wide = GROUPS * tok
    height = D // n_lo
    at_lx, at_y, at_core = lax.axis_index("lx"), lax.axis_index("y"), lax.axis_index("core")
    me = (at_y * 2 + at_core).astype(jnp.int32)
    lo = lax.axis_index(LO).astype(jnp.int32)[None]
    rowwise = jnp.where(jnp.logical_and(at_lx == 1, at_core == 0), 0, 1)
    flags = jnp.stack([at_lx, at_core, at_y, rowwise, me]).astype(jnp.int32)
    me = me[None]

    moves = []
    for hi in range(2):
        for at in range(n_lo):
            for y in range(2):
                for core in range(2):
                    moves.append(
                        (
                            ((hi * n_lo + at) * 2 + y) * 2 + core,
                            ((core * n_lo + at) * 2 + y) * 2 + hi,
                        )
                    )

    xs, packed = call(
        functools.partial(pack_body, tok),
        [((tok + 8, D), bf16), ((rows + 8, 2 * KV_WIDTH + D), bf16)],
        (positions, block_input[0].T, norm_gains, w_query, w_kv),
        smem=(0,),
    )
    xs = lax.ppermute(xs, ALL, moves)

    def gathered(x):
        far = trade(x, "y")
        return (x, trade(x, "core"), far, trade(far, "core"))

    def pass_shard(pieces):
        return (pieces[0],) + tuple(pass_on(pieces[j], SHARD, n_shard, j) for j in (1, 2, 3))

    attn_weights = gathered(packed)
    wide_parts = call(
        pack_wide_body, [((rows, 2 * part), bf16)] * n_shard, (me, w_gate_up), smem=(0,)
    )
    out_weights = gathered(w_out)
    wide_pieces = pass_shard(wide_parts)
    cot = lax.ppermute(out_grad[0].T, ALL, moves)
    cots = pass_shard((cot,) * n_shard)

    pos = xs[tok, 0].astype(f32) * tok + jnp.arange(tok, dtype=f32)
    half = HEAD_DIM // 2
    lane = jnp.arange(128)
    inverse = 1.0 / 10000.0 ** ((lane % half).astype(f32) * 2.0 / HEAD_DIM)
    angles = pos[:, None] * inverse[None, :]
    cosine = jnp.cos(angles)
    sine = jnp.sin(angles) * jnp.where(lane % HEAD_DIM < half, -1.0, 1.0)[None, :]

    attn_in, query, kv, w_kvq, gains = call(
        functools.partial(project_body, tok),
        [
            ((tok, D), bf16), ((tok, D), bf16), ((blocks, tok + 8, 2 * KV_WIDTH), bf16),
            ((D, 2 * KV_WIDTH + D), bf16), ((8, D), f32),
        ],
        (me, xs) + attn_weights + (cosine, sine),
        scratch=(pltpu.VMEM((n_shard, 8, 256), f32),),
        smem=(0,),
        hold=(wide_parts[0], cot),
    )
    kv = deal(kv, LO + ("core",))
    w_o, attn_f, ffn_in, attn_rows, middle, lse = call(
        functools.partial(attend_body, tok, blocks),
        [
            ((D, D), bf16), ((tok, D), f32), ((tok, D), bf16), ((tok, D), bf16),
            ((tok, D), f32), ((KV_HEADS, wide), f32),
        ],
        (me, xs, query, kv) + out_weights + (gains,),
        scratch=(
            pltpu.VMEM((KV_HEADS, blocks, tok, wide), f32),
            pltpu.VMEM((KV_HEADS, wide), f32),
            pltpu.VMEM((KV_HEADS, wide), f32),
            pltpu.VMEM((KV_HEADS, HEAD_DIM, wide), f32),
        ),
        smem=(0,),
        hold=wide_pieces[1:],
    )
    ffn_all = lax.all_gather(ffn_in, SHARD, axis=0, tiled=True)
    out_part, dffn_part, *feed_grads = call(
        feed_body,
        [((n_shard, tok, D), bf16), ((n_shard, tok + 8, D), bf16)]
        + [((height, 3 * part), bf16)] * n_lo,
        (me, lo, ffn_all) + cots + wide_pieces + (w_down.T,),
        scratch=(
            pltpu.VMEM((D, n_shard * tok), bf16), pltpu.VMEM((D, 2 * part), bf16),
            pltpu.VMEM((n_lo, height, 3 * part), bf16),
        ),
        smem=(0, 1),
    )
    dffn = deal(dffn_part, SHARD)
    feed_got = [feed_grads[0]] + [pass_on(feed_grads[k], LO, n_lo, k) for k in range(1, n_lo)]

    d_middle, d_query, d_branch, dkv, gain_two = call(
        functools.partial(back_body, tok, blocks),
        [
            ((tok, D), f32), ((tok, D), bf16), ((tok, D), bf16),
            ((blocks, tok, 2 * KV_WIDTH), bf16), ((1, D), f32),
        ],
        (dffn, xs, cot, middle, gains, w_o, attn_f, query, kv, lse, cosine, sine),
        scratch=(pltpu.VMEM((KV_HEADS, HEAD_DIM, wide), f32),),
    )
    misc = pass_shard(
        call(
            functools.partial(misc_body, tok),
            [((2 * tok, D), bf16)] * n_shard,
            (me, out_part, attn_in, attn_rows),
            smem=(0,),
            hold=(dffn,),
        )
    )
    (feed_sum,) = call(
        add_pieces_body, [((height, 3 * part), bf16)], tuple(feed_got), hold=(gain_two,)
    )
    dkv = deal(after(dkv, *feed_got[1:]), LO + ("core",))
    feed_other = trade(feed_sum, "hi")
    d_input, *sends = call(
        functools.partial(input_body, tok, rows),
        [((tok, D), f32)] + [((tok + 8, D), bf16)] * n_shard,
        (me, dkv, xs, d_middle, gains, w_kvq, d_query, d_branch, gain_two, cosine, sine),
        scratch=(pltpu.VMEM((n_shard, tok + 8, D), bf16),),
        smem=(0,),
        hold=misc[1:],
    )
    sends = pass_shard(sends)
    old_same, old_other = call(
        old_body,
        [((D, part), bf16)] * 2,
        (flags, mom_gate_up, mom_down.T),
        smem=(0,),
        hold=sends[3:],
    )
    olds = pass_shard((old_same, old_other, old_same, old_other))
    (feed_slots,) = call(
        functools.partial(add_slots_body, part),
        [((n_lo // 2, 2, 2, 2, height, part), bf16)],
        (feed_sum, feed_other),
        hold=(d_input,),
    )
    feed_full = after(feed_slots.reshape(n_lo * n_shard, height, part), *sends[1:])
    feed_full = deal(feed_full, LO + SHARD)
    feed_full = feed_full.reshape(n_lo, n_shard, height, part)
    (finished,) = call(
        functools.partial(finish_body, tok),
        [((2, D, tok), bf16)],
        (middle, d_input) + misc,
    )
    results = lax.ppermute(finished, ALL, moves)

    attn_chunks = call(
        functools.partial(attn_grad_body, tok),
        [((height + 8, D), bf16)] * n_lo,
        (me, lo) + sends + misc,
        scratch=(
            pltpu.VMEM((n_shard * tok, D), bf16), pltpu.VMEM((n_shard * tok, D), bf16),
            pltpu.VMEM((n_lo, height + 8, D), bf16),
        ),
        smem=(0, 1),
    )
    attn_got = [attn_chunks[0]] + [pass_on(attn_chunks[k], LO, n_lo, k) for k in range(1, n_lo)]
    (attn_sum,) = call(
        add_pieces_body, [((height + 8, D), bf16)], tuple(attn_got), hold=(finished,) + olds[1:3]
    )
    attn_other = trade(attn_sum, "hi")
    grad_same, grad_other = call(
        grad_rows_body, [((D, part), bf16)] * 2, (flags, feed_full), smem=(0,), hold=(attn_sum,)
    )

    def pass_owner(same, other):
        return (
            same, pass_on(other, OWNER, 4, 1), pass_on(same, OWNER, 4, 2),
            pass_on(other, OWNER, 4, 3),
        )

    feed_rows = pass_owner(grad_same, grad_other)
    attn_slots, gain_rows = call(
        add_second_body,
        [((n_lo, height, D), bf16), ((8, D), f32)],
        (attn_sum, attn_other),
        hold=(grad_same,) + olds[3:],
    )
    attn_olds = pass_shard(
        call(
            attn_old_body,
            [((rows, D), bf16)] * n_shard,
            (me, mom_query, mom_kv, mom_out),
            smem=(0,),
            hold=(attn_sum,),
        )
    )
    small = (pltpu.VMEM((D, D), f32), pltpu.VMEM((D, D), bf16), pltpu.VMEM((D, D), bf16))
    begun = call(
        functools.partial(feed_ns_body, 3),
        [((D, FF), f32), ((D, FF), bf16), ((8, part), bf16), ((8, 128), f32)],
        (flags, feed_full) + olds,
        scratch=small,
        smem=(0,),
        hold=(attn_slots,),
    )
    ortho_same, ortho_other = call(
        functools.partial(feed_ns_rest_body, NS_STEPS - 3),
        [((D + 8, part), bf16)] * 2,
        (flags,) + tuple(begun),
        scratch=(pltpu.VMEM((D, FF), f32), pltpu.VMEM((D, FF), bf16)) + small,
        smem=(0,),
        hold=(results,) + feed_rows[1:3] + attn_olds[1:],
    )
    feed_back = pass_owner(ortho_same, ortho_other)
    attn_full = deal(attn_slots, LO)
    (attn_ortho,) = call(
        attn_ns_body,
        [((n_shard, 2 * rows + 8, D), bf16)],
        (me, attn_full) + attn_olds,
        scratch=(
            pltpu.VMEM((D, D), f32), pltpu.VMEM((D, D), bf16), pltpu.VMEM((D, D), f32),
            pltpu.VMEM((D, D), bf16), pltpu.VMEM((D, D), bf16), pltpu.VMEM((D, D), f32),
        ),
        smem=(0,),
        hold=(ortho_same,),
    )
    attn_ortho = after(attn_ortho, *feed_back[1:3])
    two = [((2, rows, FF), f32), ((D, part), f32)]
    grad_gate_up, grad_down, moment_gate_up, moment_down = call(
        feed_moment_body, two + two, (flags,) + feed_rows + (mom_gate_up, mom_down.T), smem=(0,),
        hold=(attn_ortho,),
    )
    attn_back = deal(attn_ortho, SHARD)
    new_gate_up, new_down, feed_norm = call(
        feed_new_body,
        two + [((3, 8, part), f32)],
        (flags,) + feed_back + (w_gate_up, w_down.T),
        smem=(0,),
        hold=(attn_ortho,),
    )
    three = [((rows, D), f32), ((2, rows, KV_WIDTH), f32), ((rows, D), f32)]
    (
        grad_query, grad_kv, grad_out, moment_query, moment_kv, moment_out,
        new_query, new_kv, new_out,
    ) = call(
        attn_new_body, three * 3, (attn_back, w_query, w_kv, w_out, mom_query, mom_kv, mom_out)
    )
    attn_n = jnp.sum(attn_back[:, 2 * rows : 2 * rows + 2, 0].astype(f32), axis=1)
    feed_n = jnp.sum(feed_norm[:, :2, 0], axis=1)
    momentum_norms = jnp.concatenate([attn_n[:2], attn_n[3:], attn_n[2:3], feed_n])
    grad_gains = gain_rows[:2, :rows]
    moment_gains = MOMENTUM * mom_gains + grad_gains
    all_tokens = tok * n_ctx * n_shard
    new_gains = norm_gains.astype(f32) + -GAIN_RATE / math.sqrt(all_tokens) * moment_gains
    results = jnp.transpose(results, (0, 2, 1)).astype(f32)
    return (
        results[0][None], results[1][None],
        grad_gains, grad_query, grad_kv, grad_out, grad_gate_up, grad_down.T,
        moment_gains, moment_query, moment_kv, moment_out, moment_gate_up, moment_down.T,
        momentum_norms,
        new_gains, new_query, new_kv, new_out, new_gate_up, new_down.T,
    )


def solution(mesh):
    n_ctx = mesh.shape["ctx"]
    split = Mesh(mesh.devices.reshape(2, n_ctx // 4, 2, 2, 2), ALL)
    tokens = P(SHARD, CTX, None)
    first, second, gains = P(SHARD, None), P(None, SHARD, None), P(None, SHARD)
    weights = (gains, first, second, first, second, first)
    return jax.shard_map(
        functools.partial(on_device, 2, n_ctx // 2),
        mesh=split,
        in_specs=(tokens, tokens, P(CTX)) + weights + weights,
        out_specs=(tokens, tokens) + weights + weights + (P(),) + weights,
        check_vma=False,
    )
```

```python
import functools
import math

import jax
import jax.numpy as jnp
from jax import lax
from jax.experimental import pallas as pl
from jax.experimental.pallas import tpu as pltpu
from jax.sharding import Mesh
from jax.sharding import PartitionSpec as P

D = 576
FF = 1536
HEAD_DIM = 64
HEADS = 9
KV_HEADS = 3
GROUPS = 3
KV_WIDTH = 192
NS_STEPS = 5
NS_A = 3.4445
NS_B = -4.775
NS_C = 2.0315
NORM_EPS = 1e-05
MOMENTUM = 0.95
RATE = 0.2
SHAPE_SCALE = 0.2
GAIN_RATE = 0.02
NEG_LARGE = -1e30

bf16 = jnp.bfloat16
f32 = jnp.float32
SHARD = ("y", "core")
LO = ("lh", "lx")
OWNER = ("lx", "core")
CTX = ("hi", "lh", "lx")
ALL = ("hi", "lh", "lx", "y", "core")
TRADE = ((0, 1), (1, 0))


def dot(left, right):
    return jnp.dot(left, right, preferred_element_type=f32)


def dot_cols(left, right):
    return lax.dot_general(left, right, (((1,), (1,)), ((), ())), preferred_element_type=f32)


def dot_rows(left, right):
    return lax.dot_general(left, right, (((0,), (0,)), ((), ())), preferred_element_type=f32)


def call(body, outs, args, scratch=(), smem=(), hold=(), limit=64):
    count = len(args)
    spaces = [pltpu.SMEM if i in smem else pltpu.VMEM for i in range(count)]
    spaces += [pl.ANY] * len(hold)

    def run(*refs):
        body(*refs[:count], *refs[count + len(hold) :])

    return pl.pallas_call(
        run,
        name=getattr(body, "func", body).__name__,
        out_shape=[jax.ShapeDtypeStruct(s, d) for s, d in outs],
        in_specs=[pl.BlockSpec(memory_space=space) for space in spaces],
        out_specs=[pl.BlockSpec(memory_space=pltpu.VMEM) for _ in outs],
        scratch_shapes=list(scratch),
        compiler_params=pltpu.CompilerParams(vmem_limit_bytes=limit * 2**20),
        cost_estimate=pl.CostEstimate(flops=0, bytes_accessed=1024, transcendentals=0),
    )(*args, *hold)


def after(x, *hold):
    return pl.pallas_call(
        lambda *refs: None,
        name="after",
        out_shape=jax.ShapeDtypeStruct(x.shape, x.dtype),
        in_specs=[pl.BlockSpec(memory_space=pl.ANY)] * (1 + len(hold)),
        out_specs=pl.BlockSpec(memory_space=pl.ANY),
        input_output_aliases={0: 0},
        cost_estimate=pl.CostEstimate(flops=0, bytes_accessed=1024, transcendentals=0),
    )(x, *hold)


def turn(chunk, cosine, sine):
    lane = lax.broadcasted_iota(jnp.int32, chunk.shape, 1)
    other = jnp.where(lane % 64 < 32, pltpu.roll(chunk, 96, 1), pltpu.roll(chunk, 32, 1))
    return chunk * cosine + other * sine


def turn_wide(rows, cosine, sine):
    width = rows.shape[1]
    parts = []
    for at in range(0, width, 128):
        if at + 128 <= width:
            parts.append(turn(rows[:, at : at + 128], cosine, sine))
        else:
            tail = rows[:, at:]
            parts.append(turn(jnp.concatenate([tail, tail], axis=1), cosine, sine)[:, :64])
    return jnp.concatenate(parts, axis=1)


def inverse_rms(rows):
    return lax.rsqrt(jnp.mean(rows * rows, axis=1, keepdims=True) + NORM_EPS)


def pack_body(tok, pos_ref, x_ref, gains_ref, wq_ref, wkv_ref, xs_ref, packed_ref):
    rows = wq_ref.shape[0]
    xs_ref[0:tok, :] = x_ref[...].T
    base = (pos_ref[0] // tok).astype(f32)
    xs_ref[tok:, :] = jnp.full((8, D), base, f32).astype(bf16)
    packed_ref[0:rows, 0:KV_WIDTH] = wkv_ref[0]
    packed_ref[0:rows, KV_WIDTH : 2 * KV_WIDTH] = wkv_ref[1]
    packed_ref[0:rows, 2 * KV_WIDTH :] = wq_ref[...]
    packed_ref[rows:, :] = jnp.zeros((8, packed_ref.shape[1]), bf16)
    packed_ref[rows : rows + 2, 0:rows] = gains_ref[...]


def pack_wide_body(me_ref, wgu_ref, *out_refs):
    me = me_ref[0]
    part = wgu_ref.shape[2] // len(out_refs)
    for j, out_ref in enumerate(out_refs):
        at = pl.multiple_of((me ^ j) * part, 128)
        out_ref[:, 0:part] = wgu_ref[0, :, pl.ds(at, part)]
        out_ref[:, part : 2 * part] = wgu_ref[1, :, pl.ds(at, part)]


def project_body(
    tok, me_ref, xs_ref, p0, p1, p2, p3, cos_ref, sin_ref,
    attn_in_ref, q_ref, kv_ref, w_ref, gains_ref, pieces,
):
    me = me_ref[0]
    rows = p0.shape[0] - 8
    for j, piece in enumerate((p0, p1, p2, p3)):
        at = me ^ j
        w_ref[pl.ds(pl.multiple_of(at * rows, 16), rows), :] = piece[0:rows, :]
        pieces[at] = piece[rows:, 0:256].astype(f32)
    gains = jnp.concatenate([pieces[t, :, 0:rows] for t in range(4)], axis=1)
    gains_ref[...] = gains
    x = xs_ref[0:tok, :].astype(f32)
    attn_in = (x * inverse_rms(x) * gains[0:1, :]).astype(bf16)
    attn_in_ref[...] = attn_in
    cosine, sine = cos_ref[...], sin_ref[...]
    keys_values = dot(attn_in, w_ref[:, 0 : 2 * KV_WIDTH])
    key = turn_wide(keys_values[:, 0:KV_WIDTH], cosine, sine).astype(bf16)
    value = keys_values[:, KV_WIDTH:].astype(bf16)
    for t in range(kv_ref.shape[0]):
        kv_ref[t, 0:tok, 0:KV_WIDTH] = key
        kv_ref[t, 0:tok, KV_WIDTH:] = value
        kv_ref[t, tok:, :] = xs_ref[tok:, 0 : 2 * KV_WIDTH]
    query = dot(attn_in, w_ref[:, 2 * KV_WIDTH :])
    q_ref[...] = turn_wide(query, cosine, sine).astype(bf16) * jnp.asarray(0.125, bf16)


def group_rows(rows, group):
    return jnp.concatenate(
        [
            rows[:, (GROUPS * group + i) * HEAD_DIM : (GROUPS * group + i + 1) * HEAD_DIM]
            for i in range(GROUPS)
        ],
        axis=0,
    )


def ungroup(groups, tok):
    return jnp.concatenate(
        [g[i * tok : (i + 1) * tok, :] for g in groups for i in range(GROUPS)], axis=1
    )


def each_block(count, visit):
    if count <= 8:
        for j in range(count):
            visit(j)
    else:
        lax.fori_loop(0, count, lambda j, c: (visit(j), c)[1], 0)


def attend_body(
    tok, blocks, me_ref, xg_ref, q_ref, kv_ref, p0, p1, p2, p3, gains_ref,
    wo_ref, attn_f_ref, ffn_ref, rows_ref, middle_ref, lse_ref, scores_ref, peak_ref, total_ref, mixed_ref,
):
    wide = GROUPS * tok
    for j, piece in enumerate((p0, p1, p2, p3)):
        rows = piece.shape[0]
        wo_ref[pl.ds(pl.multiple_of((me_ref[0] ^ j) * rows, 16), rows), :] = piece[...]
    x = xg_ref[0:tok, :].astype(f32)
    query_base = xg_ref[tok : tok + 1, 0:1].astype(f32) * tok
    row = lax.broadcasted_iota(jnp.int32, (tok, wide), 0)
    col = lax.broadcasted_iota(jnp.int32, (tok, wide), 1) % tok
    ahead = (row - col).astype(f32)
    q = q_ref[...]
    queries = [group_rows(q, g) for g in range(KV_HEADS)]
    peak_ref[...] = jnp.full(peak_ref.shape, NEG_LARGE, f32)
    total_ref[...] = jnp.zeros(total_ref.shape, f32)
    mixed_ref[...] = jnp.zeros(mixed_ref.shape, f32)

    def first(j):
        allowed = ahead <= query_base - kv_ref[j, tok : tok + 1, 0:1].astype(f32) * tok
        for g in range(KV_HEADS):
            s = dot_cols(kv_ref[j, 0:tok, g * HEAD_DIM : (g + 1) * HEAD_DIM], queries[g])
            s = jnp.where(allowed, s, NEG_LARGE)
            scores_ref[g, j] = s
            peak_ref[g : g + 1, :] = jnp.maximum(
                peak_ref[g : g + 1, :], jnp.max(s, axis=0, keepdims=True)
            )

    each_block(blocks, first)

    def second(j):
        for g in range(KV_HEADS):
            p = jnp.exp(scores_ref[g, j] - peak_ref[g : g + 1, :])
            total_ref[g : g + 1, :] += jnp.sum(p, axis=0, keepdims=True)
            at = KV_WIDTH + g * HEAD_DIM
            mixed_ref[g] += dot_rows(kv_ref[j, 0:tok, at : at + HEAD_DIM], p.astype(bf16))

    each_block(blocks, second)
    lse_ref[...] = peak_ref[...] + jnp.log(total_ref[...])
    attn_f = ungroup(
        [(mixed_ref[g] / total_ref[g : g + 1, :]).T for g in range(KV_HEADS)], tok
    )
    attn_f_ref[...] = attn_f
    attn_rows = attn_f.astype(bf16)
    middle = x + dot(attn_rows, wo_ref[...])
    middle_ref[...] = middle
    ffn_ref[...] = (middle * inverse_rms(middle) * gains_ref[1:2, :]).astype(bf16)
    rows_ref[...] = attn_rows


def feed_body(
    me_ref, lo_ref, ffn_ref, g0, g1, g2, g3, p0, p1, p2, p3, wd_ref, in_ref, rows_ref,
    m0, m1, m2, m3, dffn_ref, *rest,
):
    grad_refs, (cot_ref, wgu_ref, whole_ref, out_ref) = rest[:-4], rest[-4:]
    part = wd_ref.shape[1]
    tok = g0.shape[1]
    me, lo = me_ref[0], lo_ref[0]
    for j, piece in enumerate((g0, g1, g2, g3)):
        cot_ref[:, pl.ds(pl.multiple_of((me ^ j) * tok, 128), tok)] = piece[...]
    for j, piece in enumerate((p0, p1, p2, p3)):
        rows = piece.shape[0]
        wgu_ref[pl.ds(pl.multiple_of((me ^ j) * rows, 16), rows), :] = piece[...]
    ffn_in = ffn_ref[...]
    cotangent = cot_ref[...]
    wgu = wgu_ref[...]
    wd = wd_ref[...]
    gate_up = dot(ffn_in, wgu)
    gate, up = gate_up[:, :part], gate_up[:, part:]
    sigma = jax.nn.sigmoid(gate)
    swish = gate * sigma
    hidden = (swish * up).astype(bf16)
    d_hidden = dot_rows(cotangent, wd)
    d_gate = (d_hidden * up * sigma * (1.0 + gate * (1.0 - sigma))).astype(bf16)
    d_up = (d_hidden * swish).astype(bf16)
    both = jnp.concatenate([d_gate, d_up], axis=1)
    dffn = dot_cols(both, wgu).astype(bf16)
    out = dot_cols(hidden, wd).astype(bf16)
    for s in range(4):
        dffn_ref[s, 0:tok, :] = dffn[s * tok : (s + 1) * tok, :]
        out_ref[s] = out[s * tok : (s + 1) * tok, :]
    for j, send in enumerate((m0, m1, m2, m3)):
        send[0:tok, :] = out_ref[me ^ j]
        send[tok:, :] = jnp.where((me ^ j) == 2, rows_ref[...], in_ref[...])
    gu_grad = dot_rows(ffn_in, both).astype(bf16)
    down_grad = dot(cotangent, hidden).astype(bf16)
    height = whole_ref.shape[1]
    for t in range(whole_ref.shape[0]):
        whole_ref[t, :, 0 : 2 * part] = gu_grad[t * height : (t + 1) * height, :]
        whole_ref[t, :, 2 * part :] = down_grad[t * height : (t + 1) * height, :]
    for k, grad_ref in enumerate(grad_refs):
        grad_ref[...] = whole_ref[lo ^ k]


def old_body(
    me_ref, flags_ref, mq_ref, mkv_ref, mo_ref, mgu_ref, md_ref, q0, q1, q2, q3, same_ref, other_ref
):
    me, lx, core = me_ref[0], flags_ref[0], flags_ref[1]
    rows = mq_ref.shape[0]
    blank = jnp.zeros((rows, D - KV_WIDTH), f32)
    key = jnp.concatenate([mkv_ref[0], blank], axis=1).astype(bf16)
    value = jnp.concatenate([mkv_ref[1], blank], axis=1).astype(bf16)
    query, out = mq_ref[...].astype(bf16), mo_ref[...].astype(bf16)
    for j, old in enumerate((q0, q1, q2, q3)):
        to = me ^ j
        old[...] = jnp.where(
            to == 0, query, jnp.where(to == 1, key, jnp.where(to == 2, out, value))
        )
    part = md_ref.shape[1]

    @pl.when(lx == 0)
    def _():
        for b in range(4):
            at = slice(b * part, (b + 1) * part)
            gate, up = mgu_ref[0, :, at].astype(bf16), mgu_ref[1, :, at].astype(bf16)
            same_ref[b * rows : (b + 1) * rows, :] = jnp.where(core == 0, gate, up)
            other_ref[b * rows : (b + 1) * rows, :] = jnp.where(core == 0, up, gate)

    @pl.when(lx != 0)
    def _():
        down = md_ref[...].astype(bf16)
        up = jnp.concatenate(
            [mgu_ref[1, :, b * part : (b + 1) * part].astype(bf16) for b in range(4)], axis=0
        )
        same_ref[...] = jnp.where(core == 0, down, up)
        other_ref[...] = jnp.where(core == 0, up, down)


def add_pieces_body(*refs):
    total = refs[0][...].astype(f32)
    for piece in refs[1:-1]:
        total = total + piece[...].astype(f32)
    refs[-1][...] = total.astype(bf16)


def add_slots_body(part, total_ref, got_ref, slots_ref):
    total = (total_ref[...].astype(f32) + got_ref[...].astype(f32)).astype(bf16)
    for lx in range(2):
        for core in range(2):
            number = 1 if core == 1 else 2 * lx
            piece = total[:, number * part : (number + 1) * part]
            for lh in range(slots_ref.shape[0]):
                slots_ref[lh, lx, core] = piece


def back_body(
    tok, blocks, dffn_ref, xg_ref, g_ref, middle_ref, gains_ref, wo_ref, attn_f_ref, q_ref, kv_ref,
    lse_ref, cos_ref, sin_ref,
    dmid_ref, dq_ref, dbranch_ref, dkv_ref, gain_ref, dq_acc,
):
    wide = GROUPS * tok
    query_base = xg_ref[tok : tok + 1, 0:1].astype(f32) * tok
    middle = middle_ref[...]
    inverse = inverse_rms(middle)
    normed = middle * inverse
    d_in = dffn_ref[0, 0:tok, :].astype(f32)
    for i in range(1, dffn_ref.shape[0]):
        d_in = d_in + dffn_ref[i, 0:tok, :].astype(f32)
    gain_ref[...] = jnp.sum(d_in * normed, axis=0, keepdims=True)
    scaled = d_in * gains_ref[1:2, :]
    d_middle = g_ref[...].astype(f32).T + inverse * (
        scaled - normed * jnp.mean(scaled * normed, axis=1, keepdims=True)
    )
    dmid_ref[...] = d_middle
    d_branch = d_middle.astype(bf16)
    dbranch_ref[...] = d_branch
    d_attn = dot_cols(d_branch, wo_ref[...]).astype(bf16)
    attn_f = attn_f_ref[...]
    row = lax.broadcasted_iota(jnp.int32, (tok, wide), 0)
    col = lax.broadcasted_iota(jnp.int32, (tok, wide), 1) % tok
    ahead = (row - col).astype(f32)
    q = q_ref[...]
    queries = [group_rows(q, g) for g in range(KV_HEADS)]
    outs = [group_rows(d_attn, g) for g in range(KV_HEADS)]
    product = d_attn.astype(f32) * attn_f
    deltas = [
        jnp.sum(group_rows(product, g).T, axis=0, keepdims=True) for g in range(KV_HEADS)
    ]
    dq_acc[...] = jnp.zeros(dq_acc.shape, f32)

    def visit(j):
        allowed = ahead <= query_base - kv_ref[j, tok : tok + 1, 0:1].astype(f32) * tok
        d_keys, d_values = [], []
        for g in range(KV_HEADS):
            at = KV_WIDTH + g * HEAD_DIM
            key = kv_ref[j, 0:tok, g * HEAD_DIM : (g + 1) * HEAD_DIM]
            value = kv_ref[j, 0:tok, at : at + HEAD_DIM]
            s = dot_cols(key, queries[g])
            p = jnp.where(allowed, jnp.exp(s - lse_ref[g : g + 1, :]), 0.0)
            d_weight = dot_cols(value, outs[g])
            ds = (p * (d_weight - deltas[g])).astype(bf16)
            d_values.append(dot(p.astype(bf16), outs[g]))
            d_keys.append(dot(ds, queries[g]))
            dq_acc[g] += dot_rows(key, ds)
        dkv_ref[j] = jnp.concatenate(d_keys + d_values, axis=1).astype(bf16)

    each_block(blocks, visit)
    d_query = ungroup([dq_acc[g].T * 0.125 for g in range(KV_HEADS)], tok)
    dq_ref[...] = turn_wide(d_query, cos_ref[...], -sin_ref[...]).astype(bf16)


def input_body(
    tok, rows, me_ref, dkv_ref, xg_ref, dmid_ref, gains_ref, w_ref, dq_ref, dbranch_ref, gain_two_ref,
    cos_ref, sin_ref, dx_ref, s0, s1, s2, s3, send_ref,
):
    total = dkv_ref[0].astype(f32)
    for i in range(1, dkv_ref.shape[0]):
        total = total + dkv_ref[i].astype(f32)
    d_key = turn_wide(total[:, :KV_WIDTH], cos_ref[...], -sin_ref[...]).astype(bf16)
    d_value = total[:, KV_WIDTH:].astype(bf16)
    cat = jnp.concatenate([d_key, d_value, dq_ref[...]], axis=1)
    d_in = dot_cols(cat, w_ref[...])
    x = xg_ref[0:tok, :].astype(f32)
    inverse = inverse_rms(x)
    normed = x * inverse
    gain_one = jnp.sum(d_in * normed, axis=0, keepdims=True)
    scaled = d_in * gains_ref[0:1, :]
    dx_ref[...] = dmid_ref[...] + inverse * (
        scaled - normed * jnp.mean(scaled * normed, axis=1, keepdims=True)
    )
    gain_two = gain_two_ref[...]
    blank = jnp.zeros((tok, D - KV_WIDTH), bf16)
    columns = (
        dq_ref[...], jnp.concatenate([d_key, blank], axis=1), dbranch_ref[...],
        jnp.concatenate([d_value, blank], axis=1),
    )
    for s, column in enumerate(columns):
        send_ref[s, 0:tok, :] = column
        pair = jnp.concatenate(
            [
                gain_one[:, s * rows : (s + 1) * rows],
                gain_two[:, s * rows : (s + 1) * rows],
                jnp.zeros((6, rows), f32),
            ],
            axis=0,
        )
        send_ref[s, tok:, :] = jnp.concatenate(
            [pair, jnp.zeros((8, D - rows), f32)], axis=1
        ).astype(bf16)
    for j, out_ref in enumerate((s0, s1, s2, s3)):
        out_ref[...] = send_ref[me_ref[0] ^ j]


def finish_body(tok, middle_ref, dx_ref, m0, m1, m2, m3, out_ref):
    output = middle_ref[...]
    for piece in (m0, m1, m2, m3):
        output = output + piece[0:tok, :].astype(f32)
    out_ref[0] = output.T.astype(bf16)
    out_ref[1] = dx_ref[...].T.astype(bf16)


def attn_grad_body(tok, me_ref, lo_ref, r0, r1, r2, r3, m0, m1, m2, m3, *rest):
    out_refs, (rows_ref, cols_ref, whole_ref) = rest[:-3], rest[-3:]
    me, lo = me_ref[0], lo_ref[0]
    gain = jnp.zeros((8, D), f32)
    for j, (cols, piece) in enumerate(((r0, m0), (r1, m1), (r2, m2), (r3, m3))):
        rows_ref[j * tok : (j + 1) * tok, :] = piece[tok:, :]
        cols_ref[j * tok : (j + 1) * tok, :] = cols[0:tok, :]
        gain = gain + cols[tok:, :].astype(f32)
    grad = dot_rows(cols_ref[...], rows_ref[...]).astype(bf16)
    gain = gain.astype(bf16)
    height = whole_ref.shape[1] - 8
    for t in range(whole_ref.shape[0]):
        whole_ref[t, 0:height, :] = grad[t * height : (t + 1) * height, :]
        whole_ref[t, height:, :] = gain
    for k, out_ref in enumerate(out_refs):
        out_ref[...] = whole_ref[lo ^ k]


def add_second_body(total_ref, got_ref, slots_ref, gain_ref):
    total = total_ref[...].astype(f32) + got_ref[...].astype(f32)
    height = slots_ref.shape[1]
    piece = total[0:height, :].astype(bf16)
    for t in range(slots_ref.shape[0]):
        slots_ref[t] = piece
    gain_ref[...] = total[height:, :]


def each_rows(n, block, visit, carry):
    def step(i, value):
        at = pl.multiple_of(i * block, 16)
        return visit(at, pl.ds(at, block), value)

    return lax.fori_loop(0, n // block, step, carry)


def sum_all(rows):
    return jnp.sum(jnp.sum(rows, axis=0, keepdims=True), axis=1, keepdims=True)


def sweeps(z_ref, zb_ref, rest_ref, rest_b_ref, poly_ref, squares, count, block, steps):
    n = z_ref.shape[0]
    row = lax.broadcasted_iota(jnp.int32, (block, n), 0)
    col = lax.broadcasted_iota(jnp.int32, (block, n), 1)

    def sweep(_, squares):
        center = squares / count
        slope = NS_B + 2.0 * NS_C * center
        lead = NS_A + NS_B * center + NS_C * center * center

        def first(at, here):
            gram = dot_cols(zb_ref[here, :], zb_ref[...])
            mine = jnp.logical_and(row + at == col, (row + at).astype(f32) < count)
            rest = jnp.where(mine, gram - center, gram)
            rest_ref[here, :] = rest
            rest_b_ref[here, :] = rest.astype(bf16)

        def second(at, here):
            square = dot(rest_b_ref[here, :], rest_b_ref[...])
            poly_ref[here, :] = (NS_C * square + slope * rest_ref[here, :]).astype(bf16)

        def third(at, here, total):
            z = lead * z_ref[here, :] + dot(poly_ref[here, :], zb_ref[...])
            z_ref[here, :] = z
            return total + sum_all(z * z)

        for at in range(0, n, block):
            first(at, slice(at, at + block))
        for at in range(0, n, block):
            second(at, slice(at, at + block))
        total = jnp.zeros((1, 1), f32)
        for at in range(0, n, block):
            total = third(at, slice(at, at + block), total)
        zb_ref[...] = z_ref[...].astype(bf16)
        return total

    return lax.fori_loop(0, steps, sweep, squares)


def normalize(z_ref, zb_ref):
    n = z_ref.shape[0]
    total = each_rows(
        n, 48, lambda at, here, total: total + sum_all(z_ref[here, :] * z_ref[here, :]),
        jnp.zeros((1, 1), f32),
    )
    scale = 1.0 / (jnp.sqrt(total) + 1e-07)

    def visit(at, here, carry):
        z = z_ref[here, :] * scale
        z_ref[here, :] = z
        zb_ref[here, :] = z.astype(bf16)
        return carry

    each_rows(n, 48, visit, 0)
    return total, total * scale * scale


def norm_rows(total, entries, shape):
    value = jnp.broadcast_to(jnp.sqrt(total / entries), shape)
    high = value.astype(bf16).astype(f32)
    row = lax.broadcasted_iota(jnp.int32, shape, 0)
    return jnp.where(row == 0, high, value - high).astype(bf16)


def feed_ns_body(
    flags_ref, near_ref, far_ref, o0, o1, o2, o3, same_ref, other_ref,
    z_ref, g_ref, zb_ref, rest_ref, rest_b_ref, poly_ref,
):
    core, y, rowwise, me = flags_ref[1], flags_ref[2], flags_ref[3] == 1, flags_ref[4]
    n_lo, _, height, part = near_ref.shape
    parts = 4
    rows = D // parts
    for t in range(n_lo):
        for c in range(2):
            here = slice(t * height, (t + 1) * height)
            near = pl.ds(pl.multiple_of((2 * y + c) * part, 128), part)
            far = pl.ds(pl.multiple_of((2 * (1 - y) + c) * part, 128), part)
            g_ref[here, near] = near_ref[t, c]
            g_ref[here, far] = far_ref[t, c]
    for j, old_ref in enumerate((o0, o1, o2, o3)):
        s = me ^ j

        @pl.when(rowwise)
        def _():
            for b in range(parts):
                z_ref[pl.ds(pl.multiple_of(s * rows, 16), rows), b * part : (b + 1) * part] = (
                    MOMENTUM * old_ref[b * rows : (b + 1) * rows, :].astype(f32)
                )

        @pl.when(jnp.logical_not(rowwise))
        def _():
            z_ref[:, pl.ds(pl.multiple_of(s * part, 128), part)] = MOMENTUM * old_ref[...].astype(f32)


    def add(at, here, carry):
        z_ref[here, :] += g_ref[here, :].astype(f32)
        return carry

    each_rows(D, 48, add, 0)
    total, squares = normalize(z_ref, zb_ref)
    sweeps(
        z_ref, zb_ref, rest_ref, rest_b_ref, poly_ref, squares, jnp.float32(D), D // 2, NS_STEPS
    )
    norm = norm_rows(total, jnp.float32(D * parts * part), (8, part))
    for out_ref, to in ((same_ref, core), (other_ref, 1 - core)):
        s = 2 * y + to
        out_ref[D : D + 8, :] = norm
        for first, source in ((0, zb_ref), (D + 8, g_ref)):

            @pl.when(rowwise)
            def _():
                for b in range(parts):
                    out_ref[first + b * rows : first + (b + 1) * rows, :] = source[
                        pl.ds(pl.multiple_of(s * rows, 16), rows), b * part : (b + 1) * part
                    ]

            @pl.when(jnp.logical_not(rowwise))
            def _():
                out_ref[first : first + D, :] = source[
                    :, pl.ds(pl.multiple_of(s * part, 128), part)
                ]


def attn_old_body(me_ref, m0, m1, m2, m3, out_ref, old_ref):
    rows = m0.shape[0]
    for j, piece in enumerate((m0, m1, m2, m3)):
        old_ref[pl.ds(pl.multiple_of((me_ref[0] ^ j) * rows, 16), rows), :] = piece[...]
    out_ref[...] = MOMENTUM * old_ref[...].T.astype(f32)


def attn_ns_body(
    me_ref, grad_ref, old_ref, out_ref, z_ref, zb_ref, rest_ref, rest_b_ref, poly_ref
):
    n_lo, height, _ = grad_ref.shape
    rows = D // 4
    for t in range(n_lo):
        zb_ref[t * height : (t + 1) * height, :] = grad_ref[t]
    count = jnp.where(me_ref[0] % 2 == 0, float(D), float(KV_WIDTH))
    grad_rows = zb_ref[...].T
    for s in range(4):
        out_ref[s, rows : 2 * rows, :] = grad_rows[s * rows : (s + 1) * rows, :]
    z_ref[...] = old_ref[...] + zb_ref[...].astype(f32)
    total, squares = normalize(z_ref, zb_ref)
    sweeps(z_ref, zb_ref, rest_ref, rest_b_ref, poly_ref, squares, count, D, NS_STEPS)
    ortho = zb_ref[...].T
    norm = norm_rows(total, count * D, (8, D))
    for s in range(4):
        out_ref[s, 0:rows, :] = ortho[s * rows : (s + 1) * rows, :]
        out_ref[s, 2 * rows :, :] = norm


def feed_new_body(
    flags_ref, own, core_ref, even, odd, mgu_ref, md_ref, wgu_ref, wd_ref,
    ggu_ref, gd_ref, ngu_ref, nd_ref, ugu_ref, ud_ref, norm_ref,
):
    lx, core = flags_ref[0], flags_ref[1]
    rate = -RATE * SHAPE_SCALE * math.sqrt(FF)
    rows = mgu_ref.shape[1]
    part = md_ref.shape[1]

    def pick(number, piece):
        if number == 1:
            return jnp.where(core == 1, own[piece, :], core_ref[piece, :]).astype(f32)
        near = jnp.where(core == 0, own[piece, :], core_ref[piece, :])
        far = jnp.where(core == 0, even[piece, :], odd[piece, :])
        return jnp.where(lx == number // 2, near, far).astype(f32)

    for number in range(2):
        for b in range(4):
            at = slice(b * part, (b + 1) * part)
            ortho = pick(number, slice(b * rows, (b + 1) * rows))
            grad = pick(number, slice(D + 8 + b * rows, D + 8 + (b + 1) * rows))
            ggu_ref[number, :, at] = grad
            ngu_ref[number, :, at] = MOMENTUM * mgu_ref[number, :, at] + grad
            ugu_ref[number, :, at] = wgu_ref[number, :, at].astype(f32) + rate * ortho
    grad = pick(2, slice(D + 8, 2 * D + 8))
    gd_ref[...] = grad
    nd_ref[...] = MOMENTUM * md_ref[...] + grad
    ud_ref[...] = wd_ref[...].astype(f32) + rate * pick(2, slice(0, D))
    for number in range(3):
        norm_ref[number] = pick(number, slice(D, D + 8))


def attn_new_body(
    back_ref, feed_norm_ref, wq_ref, wkv_ref, wo_ref, mq_ref, mkv_ref, mo_ref,
    gq, gkv, go, nq, nkv, no, uq, ukv, uo, norm_ref,
):
    rate = -RATE * SHAPE_SCALE * math.sqrt(D)
    rows = wq_ref.shape[0]

    def update(number, width, weight, old):
        ortho = back_ref[number, 0:rows, 0:width].astype(f32)
        grad = back_ref[number, rows : 2 * rows, 0:width].astype(f32)
        return grad, MOMENTUM * old + grad, weight.astype(f32) + rate * ortho

    gq[...], nq[...], uq[...] = update(0, D, wq_ref[...], mq_ref[...])
    go[...], no[...], uo[...] = update(2, D, wo_ref[...], mo_ref[...])
    for i, number in enumerate((1, 3)):
        gkv[i], nkv[i], ukv[i] = update(number, KV_WIDTH, wkv_ref[i], mkv_ref[i])
    lane = lax.broadcasted_iota(jnp.int32, (1, 128), 1)
    norms = jnp.zeros((1, 128), f32)
    for i, number in enumerate((0, 1, 3, 2)):
        pair = back_ref[number, 2 * rows :, 0:1].astype(f32)
        norms = jnp.where(lane == i, pair[0:1] + pair[1:2], norms)
    for i in range(3):
        pair = feed_norm_ref[i, :, 0:1]
        norms = jnp.where(lane == 4 + i, pair[0:1] + pair[1:2], norms)
    norm_ref[...] = norms


def trade(x, axis):
    return lax.ppermute(x, axis, TRADE)


def pass_on(x, axis, size, j):
    return lax.ppermute(x, axis, [(i, i ^ j) for i in range(size)])


def spread(x, axis, size):
    return deal(jnp.broadcast_to(x[None], (size,) + x.shape), axis)


def deal(x, axis):
    return lax.all_to_all(x, axis, 0, 0, tiled=True)


def on_device(
    n_hi, n_lo, block_input, out_grad, positions, norm_gains, w_query, w_kv, w_out, w_gate_up,
    w_down, mom_gains, mom_query, mom_kv, mom_out, mom_gate_up, mom_down,
):
    tok = block_input.shape[1]
    rows = w_query.shape[0]
    part = w_down.shape[0]
    n_shard = 4
    n_ctx = n_hi * n_lo
    blocks = 2 * n_lo
    wide = GROUPS * tok
    height = D // n_lo
    at_lx, at_y, at_core = lax.axis_index("lx"), lax.axis_index("y"), lax.axis_index("core")
    me = (at_y * 2 + at_core).astype(jnp.int32)
    lo = lax.axis_index(LO).astype(jnp.int32)[None]
    rowwise = jnp.where(jnp.logical_and(at_lx == 1, at_core == 0), 0, 1)
    flags = jnp.stack([at_lx, at_core, at_y, rowwise, me]).astype(jnp.int32)
    me = me[None]

    moves = []
    for hi in range(2):
        for at in range(n_lo):
            for y in range(2):
                for core in range(2):
                    moves.append(
                        (
                            ((hi * n_lo + at) * 2 + y) * 2 + core,
                            ((core * n_lo + at) * 2 + y) * 2 + hi,
                        )
                    )

    xs, packed = call(
        functools.partial(pack_body, tok),
        [((tok + 8, D), bf16), ((rows + 8, 2 * KV_WIDTH + D), bf16)],
        (positions, block_input[0].T, norm_gains, w_query, w_kv),
        smem=(0,),
    )
    xs = lax.ppermute(xs, ALL, moves)

    def gathered(x):
        far = trade(x, "y")
        return (x, trade(x, "core"), far, trade(far, "core"))

    def pass_shard(pieces):
        return (pieces[0],) + tuple(pass_on(pieces[j], SHARD, n_shard, j) for j in (1, 2, 3))

    attn_weights = gathered(packed)
    wide_parts = call(
        pack_wide_body, [((rows, 2 * part), bf16)] * n_shard, (me, w_gate_up), smem=(0,)
    )
    out_weights = gathered(w_out)
    wide_pieces = pass_shard(wide_parts)
    cot = lax.ppermute(out_grad[0].T, ALL, moves)
    cots = pass_shard((cot,) * n_shard)

    pos = xs[tok, 0].astype(f32) * tok + jnp.arange(tok, dtype=f32)
    half = HEAD_DIM // 2
    lane = jnp.arange(128)
    inverse = 1.0 / 10000.0 ** ((lane % half).astype(f32) * 2.0 / HEAD_DIM)
    angles = pos[:, None] * inverse[None, :]
    cosine = jnp.cos(angles)
    sine = jnp.sin(angles) * jnp.where(lane % HEAD_DIM < half, -1.0, 1.0)[None, :]

    attn_in, query, kv, w_kvq, gains = call(
        functools.partial(project_body, tok),
        [
            ((tok, D), bf16), ((tok, D), bf16), ((blocks, tok + 8, 2 * KV_WIDTH), bf16),
            ((D, 2 * KV_WIDTH + D), bf16), ((8, D), f32),
        ],
        (me, xs) + attn_weights + (cosine, sine),
        scratch=(pltpu.VMEM((n_shard, 8, 256), f32),),
        smem=(0,),
        hold=(wide_parts[0],) + out_weights[1:],
    )
    kv = deal(kv, LO + ("core",))
    *attn_old, old_same, old_other = call(
        old_body,
        [((rows, D), bf16)] * n_shard + [((D, part), bf16)] * 2,
        (me, flags, mom_query, mom_kv, mom_out, mom_gate_up, mom_down.T),
        smem=(0, 1),
    )
    w_o, attn_f, ffn_in, attn_rows, middle, lse = call(
        functools.partial(attend_body, tok, blocks),
        [
            ((D, D), bf16), ((tok, D), f32), ((tok, D), bf16), ((tok, D), bf16),
            ((tok, D), f32), ((KV_HEADS, wide), f32),
        ],
        (me, xs, query, kv) + out_weights + (gains,),
        scratch=(
            pltpu.VMEM((KV_HEADS, blocks, tok, wide), f32),
            pltpu.VMEM((KV_HEADS, wide), f32),
            pltpu.VMEM((KV_HEADS, wide), f32),
            pltpu.VMEM((KV_HEADS, HEAD_DIM, wide), f32),
        ),
        smem=(0,),
        hold=wide_pieces[1:] + (old_same,),
        limit=64,
    )
    ffn_all = lax.all_gather(ffn_in, SHARD, axis=0, tiled=True)
    old_same, old_other = after(old_same, ffn_all), after(old_other, ffn_all)
    attn_olds = pass_shard([attn_old[0]] + [after(old, ffn_all) for old in attn_old[1:]])
    olds = pass_shard((old_same, old_other, old_same, old_other))
    misc_0, misc_1, misc_2, misc_3, dffn_part, *feed_grads = call(
        feed_body,
        [((2 * tok, D), bf16)] * n_shard + [((n_shard, tok + 8, D), bf16)]
        + [((height, 3 * part), bf16)] * n_lo,
        (me, lo, ffn_all) + cots + wide_pieces + (w_down.T, attn_in, attn_rows),
        scratch=(
            pltpu.VMEM((D, n_shard * tok), bf16), pltpu.VMEM((D, 2 * part), bf16),
            pltpu.VMEM((n_lo, height, 3 * part), bf16), pltpu.VMEM((n_shard, tok, D), bf16),
        ),
        smem=(0, 1),
    )
    dffn = deal(dffn_part, SHARD)
    feed_got = [feed_grads[0]] + [pass_on(feed_grads[k], LO, n_lo, k) for k in range(1, n_lo)]

    misc = pass_shard((misc_0, misc_1, misc_2, misc_3))

    d_middle, d_query, d_branch, dkv, gain_two = call(
        functools.partial(back_body, tok, blocks),
        [
            ((tok, D), f32), ((tok, D), bf16), ((tok, D), bf16),
            ((blocks, tok, 2 * KV_WIDTH), bf16), ((1, D), f32),
        ],
        (dffn, xs, cot, middle, gains, w_o, attn_f, query, kv, lse, cosine, sine),
        scratch=(pltpu.VMEM((KV_HEADS, HEAD_DIM, wide), f32),),
    )
    (feed_sum,) = call(
        add_pieces_body, [((height, 3 * part), bf16)], tuple(feed_got), hold=(gain_two,)
    )
    dkv = deal(after(dkv, *feed_got[1:], *olds[1:3], *attn_olds[1:]), LO + ("core",))
    feed_other = trade(feed_sum, "hi")
    d_input, *sends = call(
        functools.partial(input_body, tok, rows),
        [((tok, D), f32)] + [((tok + 8, D), bf16)] * n_shard,
        (me, dkv, xs, d_middle, gains, w_kvq, d_query, d_branch, gain_two, cosine, sine),
        scratch=(pltpu.VMEM((n_shard, tok + 8, D), bf16),),
        smem=(0,),
        hold=misc[1:],
    )
    sends = pass_shard(sends)
    (feed_slots,) = call(
        functools.partial(add_slots_body, part),
        [((n_lo // 2, 2, 2, height, part), bf16)],
        (feed_sum, feed_other),
        hold=(d_input,),
    )
    feed_near = deal(feed_slots.reshape(n_lo * 2, height, part), LO + ("core",))
    feed_near = feed_near.reshape(n_lo, 2, height, part)
    (finished,) = call(
        functools.partial(finish_body, tok),
        [((2, D, tok), bf16)],
        (middle, d_input) + misc,
    )

    attn_chunks = call(
        functools.partial(attn_grad_body, tok),
        [((height + 8, D), bf16)] * n_lo,
        (me, lo) + sends + misc,
        scratch=(
            pltpu.VMEM((n_shard * tok, D), bf16), pltpu.VMEM((n_shard * tok, D), bf16),
            pltpu.VMEM((n_lo, height + 8, D), bf16),
        ),
        smem=(0, 1),
    )
    feed_near = after(feed_near, attn_chunks[0])
    feed_far = trade(feed_near, "y")
    attn_got = [attn_chunks[0]] + [pass_on(attn_chunks[k], LO, n_lo, k) for k in range(1, n_lo)]
    (attn_sum,) = call(
        add_pieces_body, [((height + 8, D), bf16)], tuple(attn_got), hold=(finished,)
    )
    attn_other = trade(attn_sum, "hi")
    results = lax.ppermute(finished, ALL, moves)
    (attn_old_rows,) = call(
        attn_old_body,
        [((D, D), f32)],
        (me,) + attn_olds,
        scratch=(pltpu.VMEM((D, D), bf16),),
        smem=(0,),
        hold=(attn_sum,),
    )
    attn_slots, gain_rows = call(
        add_second_body,
        [((n_lo, height, D), bf16), ((8, D), f32)],
        (attn_sum, attn_other),
        hold=(attn_old_rows,),
    )
    feed_same, feed_other = call(
        feed_ns_body,
        [((2 * D + 8, part), bf16)] * 2,
        (flags, feed_near, feed_far) + olds,
        scratch=(
            pltpu.VMEM((D, FF), f32), pltpu.VMEM((D, FF), bf16), pltpu.VMEM((D, FF), bf16),
            pltpu.VMEM((D, D), f32), pltpu.VMEM((D, D), bf16), pltpu.VMEM((D, D), bf16),
        ),
        smem=(0,),
        hold=(attn_slots, results),
    )
    feed_back = (
        feed_same, trade(feed_other, "core"),
        lax.ppermute(feed_same, OWNER, [(0, 2), (2, 0)]),
        lax.ppermute(feed_other, OWNER, [(0, 3), (2, 1)]),
    )
    attn_full = deal(attn_slots, LO)
    (attn_ortho,) = call(
        attn_ns_body,
        [((n_shard, 2 * rows + 8, D), bf16)],
        (me, attn_full, attn_old_rows),
        scratch=(
            pltpu.VMEM((D, D), f32), pltpu.VMEM((D, D), bf16), pltpu.VMEM((D, D), f32),
            pltpu.VMEM((D, D), bf16), pltpu.VMEM((D, D), bf16),
        ),
        smem=(0,),
        hold=(feed_same,),
    )
    attn_ortho = after(attn_ortho, *feed_back[2:])
    attn_back = deal(attn_ortho, SHARD)
    two = [((2, rows, FF), f32), ((D, part), f32)]
    grad_gate_up, grad_down, moment_gate_up, moment_down, new_gate_up, new_down, feed_norm = call(
        feed_new_body,
        two * 3 + [((3, 8, part), f32)],
        (flags,) + feed_back + (mom_gate_up, mom_down.T, w_gate_up, w_down.T),
        smem=(0,),
        hold=(attn_ortho,),
    )
    three = [((rows, D), f32), ((2, rows, KV_WIDTH), f32), ((rows, D), f32)]
    (
        grad_query, grad_kv, grad_out, moment_query, moment_kv, moment_out,
        new_query, new_kv, new_out, norms,
    ) = call(
        attn_new_body,
        three * 3 + [((1, 128), f32)],
        (attn_back, feed_norm, w_query, w_kv, w_out, mom_query, mom_kv, mom_out),
    )
    momentum_norms = norms[0, :7]
    grad_gains = gain_rows[:2, :rows]
    moment_gains = MOMENTUM * mom_gains + grad_gains
    all_tokens = tok * n_ctx * n_shard
    new_gains = norm_gains.astype(f32) + -GAIN_RATE / math.sqrt(all_tokens) * moment_gains
    results = jnp.transpose(results, (0, 2, 1)).astype(f32)
    return (
        results[0][None], results[1][None],
        grad_gains, grad_query, grad_kv, grad_out, grad_gate_up, grad_down.T,
        moment_gains, moment_query, moment_kv, moment_out, moment_gate_up, moment_down.T,
        momentum_norms,
        new_gains, new_query, new_kv, new_out, new_gate_up, new_down.T,
    )


def solution(mesh):
    n_ctx = mesh.shape["ctx"]
    split = Mesh(mesh.devices.reshape(2, n_ctx // 4, 2, 2, 2), ALL)
    tokens = P(SHARD, CTX, None)
    first, second, gains = P(SHARD, None), P(None, SHARD, None), P(None, SHARD)
    weights = (gains, first, second, first, second, first)
    return jax.shard_map(
        functools.partial(on_device, 2, n_ctx // 2),
        mesh=split,
        in_specs=(tokens, tokens, P(CTX)) + weights + weights,
        out_specs=(tokens, tokens) + weights + weights + (P(),) + weights,
        check_vma=False,
    )
```

```python
import functools
import math

import jax
import jax.numpy as jnp
from jax import lax
from jax.experimental import pallas as pl
from jax.experimental.pallas import tpu as pltpu
from jax.sharding import Mesh
from jax.sharding import PartitionSpec as P

D = 576
FF = 1536
HEAD_DIM = 64
HEADS = 9
KV_HEADS = 3
GROUPS = 3
KV_WIDTH = 192
NS_STEPS = 5
NS_A = 3.4445
NS_B = -4.775
NS_C = 2.0315
NORM_EPS = 1e-05
MOMENTUM = 0.95
RATE = 0.2
SHAPE_SCALE = 0.2
GAIN_RATE = 0.02
NEG_LARGE = -1e30

bf16 = jnp.bfloat16
f32 = jnp.float32
SHARD = ("y", "core")
LO = ("lh", "lx")
OWNER = ("lx", "core")
CTX = ("hi", "lh", "lx")
ALL = ("hi", "lh", "lx", "y", "core")
TRADE = ((0, 1), (1, 0))


def dot(left, right):
    return jnp.dot(left, right, preferred_element_type=f32)


def dot_cols(left, right):
    return lax.dot_general(left, right, (((1,), (1,)), ((), ())), preferred_element_type=f32)


def dot_rows(left, right):
    return lax.dot_general(left, right, (((0,), (0,)), ((), ())), preferred_element_type=f32)


def call(body, outs, args, scratch=(), smem=(), hold=(), limit=64):
    count = len(args)
    spaces = [pltpu.SMEM if i in smem else pltpu.VMEM for i in range(count)]
    spaces += [pl.ANY] * len(hold)

    def run(*refs):
        body(*refs[:count], *refs[count + len(hold) :])

    return pl.pallas_call(
        run,
        name=getattr(body, "func", body).__name__,
        out_shape=[jax.ShapeDtypeStruct(s, d) for s, d in outs],
        in_specs=[pl.BlockSpec(memory_space=space) for space in spaces],
        out_specs=[
            pl.BlockSpec(memory_space=pltpu.SMEM if len(s) == 1 else pltpu.VMEM) for s, _ in outs
        ],
        scratch_shapes=list(scratch),
        compiler_params=pltpu.CompilerParams(vmem_limit_bytes=limit * 2**20),
        cost_estimate=pl.CostEstimate(flops=0, bytes_accessed=1024, transcendentals=0),
    )(*args, *hold)


def after(x, *hold):
    return pl.pallas_call(
        lambda *refs: None,
        name="after",
        out_shape=jax.ShapeDtypeStruct(x.shape, x.dtype),
        in_specs=[pl.BlockSpec(memory_space=pl.ANY)] * (1 + len(hold)),
        out_specs=pl.BlockSpec(memory_space=pl.ANY),
        input_output_aliases={0: 0},
        cost_estimate=pl.CostEstimate(flops=0, bytes_accessed=1024, transcendentals=0),
    )(x, *hold)


def turn(chunk, cosine, sine):
    lane = lax.broadcasted_iota(jnp.int32, chunk.shape, 1)
    other = jnp.where(lane % 64 < 32, pltpu.roll(chunk, 96, 1), pltpu.roll(chunk, 32, 1))
    return chunk * cosine + other * sine


def turn_wide(rows, cosine, sine):
    width = rows.shape[1]
    parts = []
    for at in range(0, width, 128):
        if at + 128 <= width:
            parts.append(turn(rows[:, at : at + 128], cosine, sine))
        else:
            tail = rows[:, at:]
            parts.append(turn(jnp.concatenate([tail, tail], axis=1), cosine, sine)[:, :64])
    return jnp.concatenate(parts, axis=1)


def inverse_rms(rows):
    return lax.rsqrt(jnp.mean(rows * rows, axis=1, keepdims=True) + NORM_EPS)


def pack_body(tok, pos_ref, x_ref, gains_ref, wq_ref, wkv_ref, xs_ref, packed_ref):
    rows = wq_ref.shape[0]
    xs_ref[0:tok, :] = x_ref[...].T
    base = (pos_ref[0] // tok).astype(f32)
    xs_ref[tok:, :] = jnp.full((8, D), base, f32).astype(bf16)
    packed_ref[0:rows, 0:KV_WIDTH] = wkv_ref[0]
    packed_ref[0:rows, KV_WIDTH : 2 * KV_WIDTH] = wkv_ref[1]
    packed_ref[0:rows, 2 * KV_WIDTH :] = wq_ref[...]
    packed_ref[rows:, :] = jnp.zeros((8, packed_ref.shape[1]), bf16)
    packed_ref[rows : rows + 2, 0:rows] = gains_ref[...]


def pack_wide_body(me_ref, wgu_ref, *out_refs):
    me = me_ref[0]
    part = wgu_ref.shape[2] // len(out_refs)
    for j, out_ref in enumerate(out_refs):
        at = pl.multiple_of((me ^ j) * part, 128)
        out_ref[:, 0:part] = wgu_ref[0, :, pl.ds(at, part)]
        out_ref[:, part : 2 * part] = wgu_ref[1, :, pl.ds(at, part)]


def project_body(
    tok, me_ref, xs_ref, p0, p1, p2, p3, cos_ref, sin_ref,
    attn_in_ref, q_ref, kv_ref, w_ref, gains_ref, pieces,
):
    me = me_ref[0]
    rows = p0.shape[0] - 8
    for j, piece in enumerate((p0, p1, p2, p3)):
        at = me ^ j
        w_ref[pl.ds(pl.multiple_of(at * rows, 16), rows), :] = piece[0:rows, :]
        pieces[at] = piece[rows:, 0:256].astype(f32)
    gains = jnp.concatenate([pieces[t, :, 0:rows] for t in range(4)], axis=1)
    gains_ref[...] = gains
    x = xs_ref[0:tok, :].astype(f32)
    attn_in = (x * inverse_rms(x) * gains[0:1, :]).astype(bf16)
    attn_in_ref[...] = attn_in
    cosine, sine = cos_ref[...], sin_ref[...]
    keys_values = dot(attn_in, w_ref[:, 0 : 2 * KV_WIDTH])
    key = turn_wide(keys_values[:, 0:KV_WIDTH], cosine, sine).astype(bf16)
    value = keys_values[:, KV_WIDTH:].astype(bf16)
    for t in range(kv_ref.shape[0]):
        kv_ref[t, 0:tok, 0:KV_WIDTH] = key
        kv_ref[t, 0:tok, KV_WIDTH:] = value
        kv_ref[t, tok:, :] = xs_ref[tok:, 0 : 2 * KV_WIDTH]
    query = dot(attn_in, w_ref[:, 2 * KV_WIDTH :])
    q_ref[...] = turn_wide(query, cosine, sine).astype(bf16) * jnp.asarray(0.125, bf16)


def group_rows(rows, group):
    return jnp.concatenate(
        [
            rows[:, (GROUPS * group + i) * HEAD_DIM : (GROUPS * group + i + 1) * HEAD_DIM]
            for i in range(GROUPS)
        ],
        axis=0,
    )


def ungroup(groups, tok):
    return jnp.concatenate(
        [g[i * tok : (i + 1) * tok, :] for g in groups for i in range(GROUPS)], axis=1
    )


def kv_block(kv_refs, j):
    half = kv_refs[0].shape[0]
    return kv_refs[j // half].at[j % half]


def head_rows(kv_refs, tok, first, count, group):
    return tuple(
        jnp.concatenate(
            [
                kv_block(kv_refs, j)[0:tok, at : at + HEAD_DIM]
                for j in range(first, first + count)
            ],
            axis=0,
        )
        for at in (group * HEAD_DIM, KV_WIDTH + group * HEAD_DIM)
    )


def attend_body(
    tok, blocks, me_ref, xg_ref, q_ref, near_ref, far_ref, p0, p1, p2, p3, gains_ref,
    wo_ref, attn_f_ref, ffn_ref, rows_ref, middle_ref, lse_ref, scores_ref, peak_ref, total_ref, mixed_ref,
):
    wide = GROUPS * tok
    kv_refs = (near_ref, far_ref)
    for j, piece in enumerate((p0, p1, p2, p3)):
        rows = piece.shape[0]
        wo_ref[pl.ds(pl.multiple_of((me_ref[0] ^ j) * rows, 16), rows), :] = piece[...]
    x = xg_ref[0:tok, :].astype(f32)
    query_base = xg_ref[tok : tok + 1, 0:1].astype(f32) * tok
    row = lax.broadcasted_iota(jnp.int32, (tok, wide), 0)
    col = lax.broadcasted_iota(jnp.int32, (tok, wide), 1) % tok
    ahead = (row - col).astype(f32)
    q = q_ref[...]
    queries = [group_rows(q, g) for g in range(KV_HEADS)]
    peak_ref[...] = jnp.full(peak_ref.shape, NEG_LARGE, f32)
    total_ref[...] = jnp.zeros(total_ref.shape, f32)
    mixed_ref[...] = jnp.zeros(mixed_ref.shape, f32)

    for j in range(blocks):
        block_ref = kv_block(kv_refs, j)
        allowed = ahead <= query_base - block_ref[tok : tok + 1, 0:1].astype(f32) * tok
        for g in range(KV_HEADS):
            s = dot_cols(block_ref[0:tok, g * HEAD_DIM : (g + 1) * HEAD_DIM], queries[g])
            s = jnp.where(allowed, s, NEG_LARGE)
            scores_ref[g, j] = s
            peak_ref[g : g + 1, :] = jnp.maximum(
                peak_ref[g : g + 1, :], jnp.max(s, axis=0, keepdims=True)
            )

    for j in range(blocks):
        block_ref = kv_block(kv_refs, j)
        for g in range(KV_HEADS):
            p = jnp.exp(scores_ref[g, j] - peak_ref[g : g + 1, :])
            total_ref[g : g + 1, :] += jnp.sum(p, axis=0, keepdims=True)
            at = KV_WIDTH + g * HEAD_DIM
            mixed_ref[g] += dot_rows(block_ref[0:tok, at : at + HEAD_DIM], p.astype(bf16))

    lse_ref[...] = peak_ref[...] + jnp.log(total_ref[...])
    attn_f = ungroup(
        [(mixed_ref[g] / total_ref[g : g + 1, :]).T for g in range(KV_HEADS)], tok
    )
    attn_f_ref[...] = attn_f
    attn_rows = attn_f.astype(bf16)
    middle = x + dot(attn_rows, wo_ref[...])
    middle_ref[...] = middle
    ffn_ref[...] = (middle * inverse_rms(middle) * gains_ref[1:2, :]).astype(bf16)
    rows_ref[...] = attn_rows


def feed_body(
    me_ref, lo_ref, ffn_ref, g0, g1, g2, g3, p0, p1, p2, p3, wd_ref, in_ref, rows_ref,
    m0, m1, m2, m3, dffn_ref, *rest,
):
    grad_refs, (cot_ref, wgu_ref, whole_ref, out_ref) = rest[:-4], rest[-4:]
    part = wd_ref.shape[1]
    tok = g0.shape[1]
    me, lo = me_ref[0], lo_ref[0]
    for j, piece in enumerate((g0, g1, g2, g3)):
        cot_ref[:, pl.ds(pl.multiple_of((me ^ j) * tok, 128), tok)] = piece[...]
    for j, piece in enumerate((p0, p1, p2, p3)):
        rows = piece.shape[0]
        wgu_ref[pl.ds(pl.multiple_of((me ^ j) * rows, 16), rows), :] = piece[...]
    ffn_in = ffn_ref[...]
    cotangent = cot_ref[...]
    wgu = wgu_ref[...]
    wd = wd_ref[...]
    gate_up = dot(ffn_in, wgu)
    gate, up = gate_up[:, :part], gate_up[:, part:]
    sigma = jax.nn.sigmoid(gate)
    swish = gate * sigma
    hidden = (swish * up).astype(bf16)
    d_hidden = dot_rows(cotangent, wd)
    d_gate = (d_hidden * up * sigma * (1.0 + gate * (1.0 - sigma))).astype(bf16)
    d_up = (d_hidden * swish).astype(bf16)
    both = jnp.concatenate([d_gate, d_up], axis=1)
    dffn = dot_cols(both, wgu).astype(bf16)
    out = dot_cols(hidden, wd).astype(bf16)
    for s in range(4):
        dffn_ref[s, 0:tok, :] = dffn[s * tok : (s + 1) * tok, :]
        out_ref[s] = out[s * tok : (s + 1) * tok, :]
    for j, send in enumerate((m0, m1, m2, m3)):
        send[0:tok, :] = out_ref[me ^ j]
        send[tok:, :] = jnp.where((me ^ j) == 2, rows_ref[...], in_ref[...])
    gu_grad = dot_rows(ffn_in, both).astype(bf16)
    down_grad = dot(cotangent, hidden).astype(bf16)
    height = whole_ref.shape[1]
    for t in range(whole_ref.shape[0]):
        whole_ref[t, :, 0 : 2 * part] = gu_grad[t * height : (t + 1) * height, :]
        whole_ref[t, :, 2 * part :] = down_grad[t * height : (t + 1) * height, :]
    for k, grad_ref in enumerate(grad_refs):
        grad_ref[...] = whole_ref[lo ^ k]


def old_body(
    me_ref, flags_ref, mq_ref, mkv_ref, mo_ref, mgu_ref, md_ref, q0, q1, q2, q3, same_ref, other_ref
):
    me, lx, core = me_ref[0], flags_ref[0], flags_ref[1]
    rows = mq_ref.shape[0]
    blank = jnp.zeros((rows, D - KV_WIDTH), f32)
    key = jnp.concatenate([mkv_ref[0], blank], axis=1).astype(bf16)
    value = jnp.concatenate([mkv_ref[1], blank], axis=1).astype(bf16)
    query, out = mq_ref[...].astype(bf16), mo_ref[...].astype(bf16)
    for j, old in enumerate((q0, q1, q2, q3)):
        to = me ^ j
        old[...] = jnp.where(
            to == 0, query, jnp.where(to == 1, key, jnp.where(to == 2, out, value))
        )
    part = md_ref.shape[1]

    @pl.when(lx == 0)
    def _():
        for b in range(4):
            at = slice(b * part, (b + 1) * part)
            gate, up = mgu_ref[0, :, at].astype(bf16), mgu_ref[1, :, at].astype(bf16)
            same_ref[b * rows : (b + 1) * rows, :] = jnp.where(core == 0, gate, up)
            other_ref[b * rows : (b + 1) * rows, :] = jnp.where(core == 0, up, gate)

    @pl.when(lx != 0)
    def _():
        down = md_ref[...].astype(bf16)
        up = jnp.concatenate(
            [mgu_ref[1, :, b * part : (b + 1) * part].astype(bf16) for b in range(4)], axis=0
        )
        same_ref[...] = jnp.where(core == 0, down, up)
        other_ref[...] = jnp.where(core == 0, up, down)


def add_pieces_body(*refs):
    total = refs[0][...].astype(f32)
    for piece in refs[1:-1]:
        total = total + piece[...].astype(f32)
    refs[-1][...] = total.astype(bf16)


def add_slots_body(part, total_ref, got_ref, slots_ref):
    total = (total_ref[...].astype(f32) + got_ref[...].astype(f32)).astype(bf16)
    for lx in range(2):
        for core in range(2):
            number = 1 if core == 1 else 2 * lx
            piece = total[:, number * part : (number + 1) * part]
            for lh in range(slots_ref.shape[0]):
                slots_ref[lh, lx, core] = piece


def back_body(
    tok, blocks, flags_ref, dffn_ref, xg_ref, g_ref, middle_ref, gains_ref, wo_ref, attn_f_ref, q_ref, near_ref,
    far_ref, lse_ref, cos_ref, sin_ref,
    dmid_ref, dq_ref, dbranch_ref, dkv_ref, gain_ref, dq_acc,
):
    wide = GROUPS * tok
    core, kv_refs = flags_ref[1], (near_ref, far_ref)
    query_base = xg_ref[tok : tok + 1, 0:1].astype(f32) * tok
    middle = middle_ref[...]
    inverse = inverse_rms(middle)
    normed = middle * inverse
    d_in = dffn_ref[0, 0:tok, :].astype(f32)
    for i in range(1, dffn_ref.shape[0]):
        d_in = d_in + dffn_ref[i, 0:tok, :].astype(f32)
    gain_ref[...] = jnp.sum(d_in * normed, axis=0, keepdims=True)
    scaled = d_in * gains_ref[1:2, :]
    d_middle = g_ref[...].astype(f32).T + inverse * (
        scaled - normed * jnp.mean(scaled * normed, axis=1, keepdims=True)
    )
    dmid_ref[...] = d_middle
    d_branch = d_middle.astype(bf16)
    dbranch_ref[...] = d_branch
    d_attn = dot_cols(d_branch, wo_ref[...]).astype(bf16)
    attn_f = attn_f_ref[...]
    row = lax.broadcasted_iota(jnp.int32, (tok, wide), 0)
    col = lax.broadcasted_iota(jnp.int32, (tok, wide), 1) % tok
    ahead = (row - col).astype(f32)
    q = q_ref[...]
    queries = [group_rows(q, g) for g in range(KV_HEADS)]
    outs = [group_rows(d_attn, g) for g in range(KV_HEADS)]
    product = d_attn.astype(f32) * attn_f
    deltas = [
        jnp.sum(group_rows(product, g).T, axis=0, keepdims=True) for g in range(KV_HEADS)
    ]
    dq_acc[...] = jnp.zeros(dq_acc.shape, f32)
    count = min(blocks, 8)
    for first in range(0, blocks, count):
        masked = jnp.concatenate(
            [
                jnp.where(
                    ahead
                    <= query_base - kv_block(kv_refs, j)[tok : tok + 1, 0:1].astype(f32) * tok,
                    0.0,
                    NEG_LARGE,
                )
                for j in range(first, first + count)
            ],
            axis=0,
        )
        d_keys, d_values = [], []
        for g in range(KV_HEADS):
            key, value = head_rows(kv_refs, tok, first, count, g)
            p = jnp.exp(dot_cols(key, queries[g]) + (masked - lse_ref[g : g + 1, :]))
            d_weight = dot_cols(value, outs[g])
            ds = (p * (d_weight - deltas[g])).astype(bf16)
            d_values.append(dot(p.astype(bf16), outs[g]).astype(bf16))
            d_keys.append(dot(ds, queries[g]).astype(bf16))
            dq_acc[g] += dot_rows(key, ds)
        both = jnp.concatenate(d_keys + d_values, axis=1)
        for j in range(count):
            dkv_ref[(core * (blocks // 2) + first + j) % blocks] = both[j * tok : (j + 1) * tok, :]
    d_query = ungroup([dq_acc[g].T * 0.125 for g in range(KV_HEADS)], tok)
    dq_ref[...] = turn_wide(d_query, cos_ref[...], -sin_ref[...]).astype(bf16)


def input_body(
    tok, rows, me_ref, dkv_ref, xg_ref, dmid_ref, gains_ref, w_ref, dq_ref, dbranch_ref, gain_two_ref,
    cos_ref, sin_ref, dx_ref, s0, s1, s2, s3, send_ref,
):
    total = dkv_ref[0].astype(f32)
    for i in range(1, dkv_ref.shape[0]):
        total = total + dkv_ref[i].astype(f32)
    d_key = turn_wide(total[:, :KV_WIDTH], cos_ref[...], -sin_ref[...]).astype(bf16)
    d_value = total[:, KV_WIDTH:].astype(bf16)
    cat = jnp.concatenate([d_key, d_value, dq_ref[...]], axis=1)
    d_in = dot_cols(cat, w_ref[...])
    x = xg_ref[0:tok, :].astype(f32)
    inverse = inverse_rms(x)
    normed = x * inverse
    gain_one = jnp.sum(d_in * normed, axis=0, keepdims=True)
    scaled = d_in * gains_ref[0:1, :]
    dx_ref[...] = dmid_ref[...] + inverse * (
        scaled - normed * jnp.mean(scaled * normed, axis=1, keepdims=True)
    )
    gain_two = gain_two_ref[...]
    blank = jnp.zeros((tok, D - KV_WIDTH), bf16)
    columns = (
        dq_ref[...], jnp.concatenate([d_key, blank], axis=1), dbranch_ref[...],
        jnp.concatenate([d_value, blank], axis=1),
    )
    for s, column in enumerate(columns):
        send_ref[s, 0:tok, :] = column
        pair = jnp.concatenate(
            [
                gain_one[:, s * rows : (s + 1) * rows],
                gain_two[:, s * rows : (s + 1) * rows],
                jnp.zeros((6, rows), f32),
            ],
            axis=0,
        )
        send_ref[s, tok:, :] = jnp.concatenate(
            [pair, jnp.zeros((8, D - rows), f32)], axis=1
        ).astype(bf16)
    for j, out_ref in enumerate((s0, s1, s2, s3)):
        out_ref[...] = send_ref[me_ref[0] ^ j]


def finish_body(tok, middle_ref, dx_ref, m0, m1, m2, m3, out_ref):
    output = middle_ref[...]
    for piece in (m0, m1, m2, m3):
        output = output + piece[0:tok, :].astype(f32)
    out_ref[0] = output.T.astype(bf16)
    out_ref[1] = dx_ref[...].T.astype(bf16)


def attn_grad_body(tok, me_ref, lo_ref, r0, r1, r2, r3, m0, m1, m2, m3, *rest):
    out_refs, (rows_ref, cols_ref, whole_ref) = rest[:-3], rest[-3:]
    me, lo = me_ref[0], lo_ref[0]
    gain = jnp.zeros((8, D), f32)
    for j, (cols, piece) in enumerate(((r0, m0), (r1, m1), (r2, m2), (r3, m3))):
        rows_ref[j * tok : (j + 1) * tok, :] = piece[tok:, :]
        cols_ref[j * tok : (j + 1) * tok, :] = cols[0:tok, :]
        gain = gain + cols[tok:, :].astype(f32)
    grad = dot_rows(rows_ref[...], cols_ref[...]).astype(bf16)
    gain = gain.astype(bf16)
    height = whole_ref.shape[1] - 8
    for t in range(whole_ref.shape[0]):
        whole_ref[t, 0:height, :] = grad[t * height : (t + 1) * height, :]
        whole_ref[t, height:, :] = gain
    for k, out_ref in enumerate(out_refs):
        out_ref[...] = whole_ref[lo ^ k]


def add_second_body(total_ref, got_ref, slots_ref, gain_ref):
    total = total_ref[...].astype(f32) + got_ref[...].astype(f32)
    height = slots_ref.shape[1]
    piece = total[0:height, :].astype(bf16)
    for t in range(slots_ref.shape[0]):
        slots_ref[t] = piece
    gain_ref[...] = total[height:, :]


def each_rows(n, block, visit, carry):
    def step(i, value):
        at = pl.multiple_of(i * block, 16)
        return visit(at, pl.ds(at, block), value)

    return lax.fori_loop(0, n // block, step, carry)


def sum_all(rows):
    return jnp.sum(jnp.sum(rows, axis=0, keepdims=True), axis=1, keepdims=True)


def sweeps(z_ref, zb_ref, rest_ref, rest_b_ref, poly_ref, squares, block, steps):
    n = z_ref.shape[0]
    row = lax.broadcasted_iota(jnp.int32, (block, n), 0)
    col = lax.broadcasted_iota(jnp.int32, (block, n), 1)

    def sweep(_, squares):
        center = squares / float(n)
        slope = NS_B + 2.0 * NS_C * center
        lead = NS_A + NS_B * center + NS_C * center * center

        def first(at, here):
            gram = dot_cols(zb_ref[here, :], zb_ref[...])
            rest = jnp.where(row + at == col, gram - center, gram)
            rest_ref[here, :] = rest
            rest_b_ref[here, :] = rest.astype(bf16)

        def second(at, here):
            square = dot(rest_b_ref[here, :], rest_b_ref[...])
            poly_ref[here, :] = (NS_C * square + slope * rest_ref[here, :]).astype(bf16)

        def third(at, here, total):
            z = lead * z_ref[here, :] + dot(poly_ref[here, :], zb_ref[...])
            z_ref[here, :] = z
            return total + sum_all(z * z)

        for at in range(0, n, block):
            first(at, slice(at, at + block))
        for at in range(0, n, block):
            second(at, slice(at, at + block))
        total = jnp.zeros((1, 1), f32)
        for at in range(0, n, block):
            total = third(at, slice(at, at + block), total)
        zb_ref[...] = z_ref[...].astype(bf16)
        return total

    return lax.fori_loop(0, steps, sweep, squares)


def normalize(z_ref, zb_ref):
    n = z_ref.shape[0]
    total = each_rows(
        n, 48, lambda at, here, total: total + sum_all(z_ref[here, :] * z_ref[here, :]),
        jnp.zeros((1, 1), f32),
    )
    scale = 1.0 / (jnp.sqrt(total) + 1e-07)

    def visit(at, here, carry):
        z = z_ref[here, :] * scale
        z_ref[here, :] = z
        zb_ref[here, :] = z.astype(bf16)
        return carry

    each_rows(n, 48, visit, 0)
    return total, total * scale * scale


def norm_rows(total, entries, shape):
    value = jnp.broadcast_to(jnp.sqrt(total / entries), shape)
    high = value.astype(bf16).astype(f32)
    row = lax.broadcasted_iota(jnp.int32, shape, 0)
    return jnp.where(row == 0, high, value - high).astype(bf16)


def feed_ns_body(
    flags_ref, near_ref, far_ref, o0, o1, o2, o3, same_ref, other_ref,
    z_ref, g_ref, zb_ref, rest_ref, rest_b_ref, poly_ref,
):
    core, y, rowwise, me = flags_ref[1], flags_ref[2], flags_ref[3] == 1, flags_ref[4]
    n_lo, _, height, part = near_ref.shape
    parts = 4
    rows = D // parts
    for t in range(n_lo):
        for c in range(2):
            here = slice(t * height, (t + 1) * height)
            near = pl.ds(pl.multiple_of((2 * y + c) * part, 128), part)
            far = pl.ds(pl.multiple_of((2 * (1 - y) + c) * part, 128), part)
            g_ref[here, near] = near_ref[t, c]
            g_ref[here, far] = far_ref[t, c]
    for j, old_ref in enumerate((o0, o1, o2, o3)):
        s = me ^ j

        @pl.when(rowwise)
        def _():
            for b in range(parts):
                z_ref[pl.ds(pl.multiple_of(s * rows, 16), rows), b * part : (b + 1) * part] = (
                    MOMENTUM * old_ref[b * rows : (b + 1) * rows, :].astype(f32)
                )

        @pl.when(jnp.logical_not(rowwise))
        def _():
            z_ref[:, pl.ds(pl.multiple_of(s * part, 128), part)] = MOMENTUM * old_ref[...].astype(f32)


    def add(at, here, carry):
        z_ref[here, :] += g_ref[here, :].astype(f32)
        return carry

    each_rows(D, 48, add, 0)
    total, squares = normalize(z_ref, zb_ref)
    sweeps(
        z_ref, zb_ref, rest_ref, rest_b_ref, poly_ref, squares, D // 2, NS_STEPS
    )
    norm = norm_rows(total, jnp.float32(D * parts * part), (8, part))
    for out_ref, to in ((same_ref, core), (other_ref, 1 - core)):
        s = 2 * y + to
        out_ref[D : D + 8, :] = norm
        for first, source in ((0, zb_ref), (D + 8, g_ref)):

            @pl.when(rowwise)
            def _():
                for b in range(parts):
                    out_ref[first + b * rows : first + (b + 1) * rows, :] = source[
                        pl.ds(pl.multiple_of(s * rows, 16), rows), b * part : (b + 1) * part
                    ]

            @pl.when(jnp.logical_not(rowwise))
            def _():
                out_ref[first : first + D, :] = source[
                    :, pl.ds(pl.multiple_of(s * part, 128), part)
                ]


def attn_ns_body(
    me_ref, grad_ref, m0, m1, m2, m3, out_ref, z_ref, zb_ref, rest_ref, rest_b_ref, poly_ref,
    *narrow_refs,
):
    me = me_ref[0]
    narrow = me % 2 == 1
    n_lo, height, _ = grad_ref.shape
    rows = D // 4
    for t in range(n_lo):
        z_ref[t * height : (t + 1) * height, :] = grad_ref[t].astype(f32)
    for j, piece in enumerate((m0, m1, m2, m3)):
        here = pl.ds(pl.multiple_of((me ^ j) * rows, 16), rows)
        z_ref[here, :] += MOMENTUM * piece[...].astype(f32)
    total, squares = normalize(z_ref, zb_ref)

    @pl.when(narrow)
    def _():
        z_ref[...] = z_ref[...].T
        zb_ref[...] = zb_ref[...].T
        part = slice(0, KV_WIDTH)
        sweeps(z_ref.at[part], zb_ref.at[part], *narrow_refs, squares, KV_WIDTH, NS_STEPS)
        zb_ref[...] = zb_ref[...].T

    @pl.when(jnp.logical_not(narrow))
    def _():
        sweeps(z_ref, zb_ref, rest_ref, rest_b_ref, poly_ref, squares, D, NS_STEPS)

    count = jnp.where(narrow, float(KV_WIDTH), float(D))
    norm = norm_rows(total, count * D, (8, D))
    for s in range(4):
        out_ref[s, 0:rows, :] = zb_ref[s * rows : (s + 1) * rows, :]
        out_ref[s, rows:, :] = norm


def feed_new_body(
    flags_ref, own, core_ref, even, odd, mgu_ref, md_ref, wgu_ref, wd_ref,
    ggu_ref, gd_ref, ngu_ref, nd_ref, ugu_ref, ud_ref, norm_ref,
):
    lx, core = flags_ref[0], flags_ref[1]
    rate = -RATE * SHAPE_SCALE * math.sqrt(FF)
    rows = mgu_ref.shape[1]
    part = md_ref.shape[1]

    def pick(number, piece):
        if number == 1:
            return jnp.where(core == 1, own[piece, :], core_ref[piece, :]).astype(f32)
        near = jnp.where(core == 0, own[piece, :], core_ref[piece, :])
        far = jnp.where(core == 0, even[piece, :], odd[piece, :])
        return jnp.where(lx == number // 2, near, far).astype(f32)

    for number in range(2):
        for b in range(4):
            at = slice(b * part, (b + 1) * part)
            ortho = pick(number, slice(b * rows, (b + 1) * rows))
            grad = pick(number, slice(D + 8 + b * rows, D + 8 + (b + 1) * rows))
            ggu_ref[number, :, at] = grad
            ngu_ref[number, :, at] = MOMENTUM * mgu_ref[number, :, at] + grad
            ugu_ref[number, :, at] = wgu_ref[number, :, at].astype(f32) + rate * ortho
    grad = pick(2, slice(D + 8, 2 * D + 8))
    gd_ref[...] = grad
    nd_ref[...] = MOMENTUM * md_ref[...] + grad
    ud_ref[...] = wd_ref[...].astype(f32) + rate * pick(2, slice(0, D))
    for number in range(3):
        norm_ref[number] = pick(number, slice(D, D + 8))


def attn_new_body(
    back_ref, grad_ref, feed_norm_ref, wq_ref, wkv_ref, wo_ref, mq_ref, mkv_ref, mo_ref,
    gq, gkv, go, nq, nkv, no, uq, ukv, uo, norm_ref,
):
    rate = -RATE * SHAPE_SCALE * math.sqrt(D)
    rows = wq_ref.shape[0]

    def update(number, width, weight, old):
        ortho = back_ref[number, 0:rows, 0:width].astype(f32)
        grad = grad_ref[number, :, 0:width].astype(f32)
        return grad, MOMENTUM * old + grad, weight.astype(f32) + rate * ortho

    gq[...], nq[...], uq[...] = update(0, D, wq_ref[...], mq_ref[...])
    go[...], no[...], uo[...] = update(2, D, wo_ref[...], mo_ref[...])
    for i, number in enumerate((1, 3)):
        gkv[i], nkv[i], ukv[i] = update(number, KV_WIDTH, wkv_ref[i], mkv_ref[i])
    for i, number in enumerate((0, 1, 3, 2)):
        norm_ref[i] = jnp.sum(back_ref[number, rows : rows + 2, 0:1].astype(f32))
    for i in range(3):
        norm_ref[4 + i] = jnp.sum(feed_norm_ref[i, 0:2, 0:1])


def trade(x, axis):
    return lax.ppermute(x, axis, TRADE)


def pass_on(x, axis, size, j):
    return lax.ppermute(x, axis, [(i, i ^ j) for i in range(size)])


def spread(x, axis, size):
    return deal(jnp.broadcast_to(x[None], (size,) + x.shape), axis)


def deal(x, axis):
    return lax.all_to_all(x, axis, 0, 0, tiled=True)


def on_device(
    n_hi, n_lo, block_input, out_grad, positions, norm_gains, w_query, w_kv, w_out, w_gate_up,
    w_down, mom_gains, mom_query, mom_kv, mom_out, mom_gate_up, mom_down,
):
    tok = block_input.shape[1]
    rows = w_query.shape[0]
    part = w_down.shape[0]
    n_shard = 4
    n_ctx = n_hi * n_lo
    blocks = 2 * n_lo
    wide = GROUPS * tok
    height = D // n_lo
    at_lx, at_y, at_core = lax.axis_index("lx"), lax.axis_index("y"), lax.axis_index("core")
    me = (at_y * 2 + at_core).astype(jnp.int32)
    lo = lax.axis_index(LO).astype(jnp.int32)[None]
    rowwise = jnp.where(jnp.logical_and(at_lx == 1, at_core == 0), 0, 1)
    flags = jnp.stack([at_lx, at_core, at_y, rowwise, me]).astype(jnp.int32)
    me = me[None]

    moves = []
    for hi in range(2):
        for at in range(n_lo):
            for y in range(2):
                for core in range(2):
                    moves.append(
                        (
                            ((hi * n_lo + at) * 2 + y) * 2 + core,
                            ((core * n_lo + at) * 2 + y) * 2 + hi,
                        )
                    )

    xs, packed = call(
        functools.partial(pack_body, tok),
        [((tok + 8, D), bf16), ((rows + 8, 2 * KV_WIDTH + D), bf16)],
        (positions, block_input[0].T, norm_gains, w_query, w_kv),
        smem=(0,),
    )
    xs = lax.ppermute(xs, ALL, moves)

    def gathered(x):
        far = trade(x, "y")
        return (x, trade(x, "core"), far, trade(far, "core"))

    def pass_shard(pieces):
        return (pieces[0],) + tuple(pass_on(pieces[j], SHARD, n_shard, j) for j in (1, 2, 3))

    attn_weights = gathered(packed)
    wide_parts = call(
        pack_wide_body, [((rows, 2 * part), bf16)] * n_shard, (me, w_gate_up), smem=(0,)
    )
    out_weights = gathered(w_out)
    wide_pieces = pass_shard(wide_parts)
    cot = lax.ppermute(out_grad[0].T, ALL, moves)
    cots = pass_shard((cot,) * n_shard)

    pos = xs[tok, 0].astype(f32) * tok + jnp.arange(tok, dtype=f32)
    half = HEAD_DIM // 2
    lane = jnp.arange(128)
    inverse = 1.0 / 10000.0 ** ((lane % half).astype(f32) * 2.0 / HEAD_DIM)
    angles = pos[:, None] * inverse[None, :]
    cosine = jnp.cos(angles)
    sine = jnp.sin(angles) * jnp.where(lane % HEAD_DIM < half, -1.0, 1.0)[None, :]

    attn_in, query, kv, w_kvq, gains = call(
        functools.partial(project_body, tok),
        [
            ((tok, D), bf16), ((tok, D), bf16), ((n_lo, tok + 8, 2 * KV_WIDTH), bf16),
            ((D, 2 * KV_WIDTH + D), bf16), ((8, D), f32),
        ],
        (me, xs) + attn_weights + (cosine, sine),
        scratch=(pltpu.VMEM((n_shard, 8, 256), f32),),
        smem=(0,),
        hold=(wide_parts[0],) + out_weights[1:],
    )
    kv = deal(kv, LO)
    *attn_old, old_same, old_other = call(
        old_body,
        [((rows, D), bf16)] * n_shard + [((D, part), bf16)] * 2,
        (me, flags, mom_query, mom_kv, mom_out, mom_gate_up, mom_down.T),
        smem=(0, 1),
    )
    kv = after(kv, old_same, cot, *wide_pieces[1:3])
    kv_pair = (kv, trade(kv, "core"))
    w_o, attn_f, ffn_in, attn_rows, middle, lse = call(
        functools.partial(attend_body, tok, blocks),
        [
            ((D, D), bf16), ((tok, D), f32), ((tok, D), bf16), ((tok, D), bf16),
            ((tok, D), f32), ((KV_HEADS, wide), f32),
        ],
        (me, xs, query) + kv_pair + out_weights + (gains,),
        scratch=(
            pltpu.VMEM((KV_HEADS, blocks, tok, wide), f32),
            pltpu.VMEM((KV_HEADS, wide), f32),
            pltpu.VMEM((KV_HEADS, wide), f32),
            pltpu.VMEM((KV_HEADS, HEAD_DIM, wide), f32),
        ),
        smem=(0,),
        limit=64,
    )
    ffn_all = lax.all_gather(after(ffn_in, wide_pieces[3]), SHARD, axis=0, tiled=True)
    old_same, old_other = after(old_same, ffn_all), after(old_other, ffn_all)
    attn_olds = pass_shard([attn_old[0]] + [after(old, ffn_all) for old in attn_old[1:]])
    olds = pass_shard((old_same, old_other, old_same, old_other))
    misc_0, misc_1, misc_2, misc_3, dffn_part, *feed_grads = call(
        feed_body,
        [((2 * tok, D), bf16)] * n_shard + [((n_shard, tok + 8, D), bf16)]
        + [((height, 3 * part), bf16)] * n_lo,
        (me, lo, ffn_all) + cots + wide_pieces + (w_down.T, attn_in, attn_rows),
        scratch=(
            pltpu.VMEM((D, n_shard * tok), bf16), pltpu.VMEM((D, 2 * part), bf16),
            pltpu.VMEM((n_lo, height, 3 * part), bf16), pltpu.VMEM((n_shard, tok, D), bf16),
        ),
        smem=(0, 1),
    )
    dffn = deal(dffn_part, SHARD)
    feed_got = [feed_grads[0]] + [pass_on(feed_grads[k], LO, n_lo, k) for k in range(1, n_lo)]

    misc = pass_shard((misc_0, misc_1, misc_2, misc_3))

    d_middle, d_query, d_branch, dkv, gain_two = call(
        functools.partial(back_body, tok, blocks),
        [
            ((tok, D), f32), ((tok, D), bf16), ((tok, D), bf16),
            ((blocks, tok, 2 * KV_WIDTH), bf16), ((1, D), f32),
        ],
        (flags, dffn, xs, cot, middle, gains, w_o, attn_f, query) + kv_pair + (lse, cosine, sine),
        scratch=(pltpu.VMEM((KV_HEADS, HEAD_DIM, wide), f32),),
        smem=(0,),
    )
    (feed_sum,) = call(
        add_pieces_body, [((height, 3 * part), bf16)], tuple(feed_got), hold=(gain_two,)
    )
    dkv = deal(after(dkv, *feed_got[1:], *olds[1:3], *attn_olds[1:]), ("core",) + LO)
    feed_other = trade(feed_sum, "hi")
    d_input, *sends = call(
        functools.partial(input_body, tok, rows),
        [((tok, D), f32)] + [((tok + 8, D), bf16)] * n_shard,
        (me, dkv, xs, d_middle, gains, w_kvq, d_query, d_branch, gain_two, cosine, sine),
        scratch=(pltpu.VMEM((n_shard, tok + 8, D), bf16),),
        smem=(0,),
        hold=misc[1:],
    )
    sends = pass_shard(sends)
    (feed_slots,) = call(
        functools.partial(add_slots_body, part),
        [((n_lo // 2, 2, 2, height, part), bf16)],
        (feed_sum, feed_other),
        hold=(d_input,),
    )
    feed_near = deal(feed_slots.reshape(n_lo * 2, height, part), LO + ("core",))
    feed_near = feed_near.reshape(n_lo, 2, height, part)
    (finished,) = call(
        functools.partial(finish_body, tok),
        [((2, D, tok), bf16)],
        (middle, d_input) + misc,
    )

    attn_chunks = call(
        functools.partial(attn_grad_body, tok),
        [((height + 8, D), bf16)] * n_lo,
        (me, lo) + sends + misc,
        scratch=(
            pltpu.VMEM((n_shard * tok, D), bf16), pltpu.VMEM((n_shard * tok, D), bf16),
            pltpu.VMEM((n_lo, height + 8, D), bf16),
        ),
        smem=(0, 1),
    )
    feed_near = after(feed_near, attn_chunks[0])
    feed_far = trade(feed_near, "y")
    attn_got = [attn_chunks[0]] + [pass_on(attn_chunks[k], LO, n_lo, k) for k in range(1, n_lo)]
    (attn_sum,) = call(
        add_pieces_body, [((height + 8, D), bf16)], tuple(attn_got), hold=(finished,)
    )
    attn_other = trade(attn_sum, "hi")
    results = lax.ppermute(finished, ALL, moves)
    attn_slots, gain_rows = call(
        add_second_body,
        [((n_lo, height, D), bf16), ((8, D), f32)],
        (attn_sum, attn_other),
        hold=(results, olds[3]),
    )
    feed_same, feed_other = call(
        feed_ns_body,
        [((2 * D + 8, part), bf16)] * 2,
        (flags, feed_near, feed_far) + olds,
        scratch=(
            pltpu.VMEM((D, FF), f32), pltpu.VMEM((D, FF), bf16), pltpu.VMEM((D, FF), bf16),
            pltpu.VMEM((D, D), f32), pltpu.VMEM((D, D), bf16), pltpu.VMEM((D, D), bf16),
        ),
        smem=(0,),
        hold=(attn_slots,),
    )
    feed_back = (
        feed_same, trade(feed_other, "core"),
        lax.ppermute(feed_same, OWNER, [(0, 2), (2, 0)]),
        lax.ppermute(feed_other, OWNER, [(0, 3), (2, 1)]),
    )
    attn_full = deal(attn_slots, LO)
    attn_rows_back = deal(attn_full.reshape(n_shard, rows, D), SHARD)
    (attn_ortho,) = call(
        attn_ns_body,
        [((n_shard, rows + 8, D), bf16)],
        (me, attn_full) + attn_olds,
        scratch=[pltpu.VMEM((D, D), kind) for kind in (f32, bf16, f32, bf16, bf16)]
        + [pltpu.VMEM((KV_WIDTH, KV_WIDTH), kind) for kind in (f32, bf16, bf16)],
        smem=(0,),
        hold=(feed_same,),
    )
    attn_ortho = after(attn_ortho, feed_back[2])
    attn_back = deal(attn_ortho, SHARD)
    two = [((2, rows, FF), f32), ((D, part), f32)]
    grad_gate_up, grad_down, moment_gate_up, moment_down, new_gate_up, new_down, feed_norm = call(
        feed_new_body,
        two * 3 + [((3, 8, part), f32)],
        (flags,) + feed_back + (mom_gate_up, mom_down.T, w_gate_up, w_down.T),
        smem=(0,),
        hold=(attn_ortho,),
    )
    three = [((rows, D), f32), ((2, rows, KV_WIDTH), f32), ((rows, D), f32)]
    (
        grad_query, grad_kv, grad_out, moment_query, moment_kv, moment_out,
        new_query, new_kv, new_out, momentum_norms,
    ) = call(
        attn_new_body,
        three * 3 + [((7,), f32)],
        (attn_back, attn_rows_back, feed_norm, w_query, w_kv, w_out, mom_query, mom_kv, mom_out),
    )
    grad_gains = gain_rows[:2, :rows]
    moment_gains = MOMENTUM * mom_gains + grad_gains
    all_tokens = tok * n_ctx * n_shard
    new_gains = norm_gains.astype(f32) + -GAIN_RATE / math.sqrt(all_tokens) * moment_gains
    results = jnp.transpose(results, (0, 2, 1)).astype(f32)
    return (
        results[0][None], results[1][None],
        grad_gains, grad_query, grad_kv, grad_out, grad_gate_up, grad_down.T,
        moment_gains, moment_query, moment_kv, moment_out, moment_gate_up, moment_down.T,
        momentum_norms,
        new_gains, new_query, new_kv, new_out, new_gate_up, new_down.T,
    )


def solution(mesh):
    n_ctx = mesh.shape["ctx"]
    split = Mesh(mesh.devices.reshape(2, n_ctx // 4, 2, 2, 2), ALL)
    tokens = P(SHARD, CTX, None)
    first, second, gains = P(SHARD, None), P(None, SHARD, None), P(None, SHARD)
    weights = (gains, first, second, first, second, first)
    return jax.shard_map(
        functools.partial(on_device, 2, n_ctx // 2),
        mesh=split,
        in_specs=(tokens, tokens, P(CTX)) + weights + weights,
        out_specs=(tokens, tokens) + weights + weights + (P(),) + weights,
        check_vma=False,
    )
```

```python
import functools
import math

import jax
import jax.numpy as jnp
from jax import lax
from jax.experimental import pallas as pl
from jax.experimental.pallas import tpu as pltpu
from jax.sharding import Mesh
from jax.sharding import PartitionSpec as P

D = 576
FF = 1536
HEAD_DIM = 64
HEADS = 9
KV_HEADS = 3
GROUPS = 3
KV_WIDTH = 192
NS_STEPS = 5
NS_A = 3.4445
NS_B = -4.775
NS_C = 2.0315
NORM_EPS = 1e-05
MOMENTUM = 0.95
RATE = 0.2
SHAPE_SCALE = 0.2
GAIN_RATE = 0.02
NEG_LARGE = -1e30

bf16 = jnp.bfloat16
f32 = jnp.float32
SHARD = ("y", "core")
LO = ("lh", "lx")
OWNER = ("lx", "core")
CTX = ("hi", "lh", "lx")
ALL = ("hi", "lh", "lx", "y", "core")
TRADE = ((0, 1), (1, 0))


def dot(left, right):
    return jnp.dot(left, right, preferred_element_type=f32)


def dot_cols(left, right):
    return lax.dot_general(left, right, (((1,), (1,)), ((), ())), preferred_element_type=f32)


def dot_rows(left, right):
    return lax.dot_general(left, right, (((0,), (0,)), ((), ())), preferred_element_type=f32)


def call(body, outs, args, scratch=(), smem=(), hold=(), limit=64):
    count = len(args)
    spaces = [pltpu.SMEM if i in smem else pltpu.VMEM for i in range(count)]
    spaces += [pl.ANY] * len(hold)

    def run(*refs):
        body(*refs[:count], *refs[count + len(hold) :])

    return pl.pallas_call(
        run,
        name=getattr(body, "func", body).__name__,
        out_shape=[jax.ShapeDtypeStruct(s, d) for s, d in outs],
        in_specs=[pl.BlockSpec(memory_space=space) for space in spaces],
        out_specs=[
            pl.BlockSpec(memory_space=pltpu.SMEM if len(s) == 1 else pltpu.VMEM) for s, _ in outs
        ],
        scratch_shapes=list(scratch),
        compiler_params=pltpu.CompilerParams(vmem_limit_bytes=limit * 2**20),
        cost_estimate=pl.CostEstimate(flops=0, bytes_accessed=1024, transcendentals=0),
    )(*args, *hold)


def after(x, *hold):
    return pl.pallas_call(
        lambda *refs: None,
        name="after",
        out_shape=jax.ShapeDtypeStruct(x.shape, x.dtype),
        in_specs=[pl.BlockSpec(memory_space=pl.ANY)] * (1 + len(hold)),
        out_specs=pl.BlockSpec(memory_space=pl.ANY),
        input_output_aliases={0: 0},
        cost_estimate=pl.CostEstimate(flops=0, bytes_accessed=1024, transcendentals=0),
    )(x, *hold)


def turn(chunk, cosine, sine):
    lane = lax.broadcasted_iota(jnp.int32, chunk.shape, 1)
    other = jnp.where(lane % 64 < 32, pltpu.roll(chunk, 96, 1), pltpu.roll(chunk, 32, 1))
    return chunk * cosine + other * sine


def turn_wide(rows, cosine, sine):
    width = rows.shape[1]
    parts = []
    for at in range(0, width, 128):
        if at + 128 <= width:
            parts.append(turn(rows[:, at : at + 128], cosine, sine))
        else:
            tail = rows[:, at:]
            parts.append(turn(jnp.concatenate([tail, tail], axis=1), cosine, sine)[:, :64])
    return jnp.concatenate(parts, axis=1)


def inverse_rms(rows):
    return lax.rsqrt(jnp.mean(rows * rows, axis=1, keepdims=True) + NORM_EPS)


def pack_body(tok, pos_ref, x_ref, gains_ref, wq_ref, wkv_ref, xs_ref, packed_ref):
    rows = wq_ref.shape[0]
    xs_ref[0:tok, :] = x_ref[...].T
    base = (pos_ref[0] // tok).astype(f32)
    xs_ref[tok:, :] = jnp.full((8, D), base, f32).astype(bf16)
    packed_ref[0:rows, 0:KV_WIDTH] = wkv_ref[0]
    packed_ref[0:rows, KV_WIDTH : 2 * KV_WIDTH] = wkv_ref[1]
    packed_ref[0:rows, 2 * KV_WIDTH :] = wq_ref[...]
    packed_ref[rows:, :] = jnp.zeros((8, packed_ref.shape[1]), bf16)
    packed_ref[rows : rows + 2, 0:rows] = gains_ref[...]


def pack_wide_body(me_ref, wgu_ref, *out_refs):
    me = me_ref[0]
    part = wgu_ref.shape[2] // len(out_refs)
    for j, out_ref in enumerate(out_refs):
        at = pl.multiple_of((me ^ j) * part, 128)
        out_ref[:, 0:part] = wgu_ref[0, :, pl.ds(at, part)]
        out_ref[:, part : 2 * part] = wgu_ref[1, :, pl.ds(at, part)]


def project_body(
    tok, me_ref, xs_ref, p0, p1, p2, p3, cos_ref, sin_ref,
    attn_in_ref, q_ref, kv_ref, w_ref, gains_ref, pieces,
):
    me = me_ref[0]
    rows = p0.shape[0] - 8
    for j, piece in enumerate((p0, p1, p2, p3)):
        at = me ^ j
        w_ref[pl.ds(pl.multiple_of(at * rows, 16), rows), :] = piece[0:rows, :]
        pieces[at] = piece[rows:, 0:256].astype(f32)
    gains = jnp.concatenate([pieces[t, :, 0:rows] for t in range(4)], axis=1)
    gains_ref[...] = gains
    x = xs_ref[0:tok, :].astype(f32)
    attn_in = (x * inverse_rms(x) * gains[0:1, :]).astype(bf16)
    attn_in_ref[...] = attn_in
    cosine, sine = cos_ref[...], sin_ref[...]
    keys_values = dot(attn_in, w_ref[:, 0 : 2 * KV_WIDTH])
    key = turn_wide(keys_values[:, 0:KV_WIDTH], cosine, sine).astype(bf16)
    value = keys_values[:, KV_WIDTH:].astype(bf16)
    for t in range(kv_ref.shape[0]):
        kv_ref[t, 0:tok, 0:KV_WIDTH] = key
        kv_ref[t, 0:tok, KV_WIDTH:] = value
        kv_ref[t, tok:, :] = xs_ref[tok:, 0 : 2 * KV_WIDTH]
    query = dot(attn_in, w_ref[:, 2 * KV_WIDTH :])
    q_ref[...] = turn_wide(query, cosine, sine).astype(bf16) * jnp.asarray(0.125, bf16)


def group_rows(rows, group):
    return jnp.concatenate(
        [
            rows[:, (GROUPS * group + i) * HEAD_DIM : (GROUPS * group + i + 1) * HEAD_DIM]
            for i in range(GROUPS)
        ],
        axis=0,
    )


def ungroup(groups, tok):
    return jnp.concatenate(
        [g[i * tok : (i + 1) * tok, :] for g in groups for i in range(GROUPS)], axis=1
    )


def kv_block(kv_refs, j):
    half = kv_refs[0].shape[0]
    return kv_refs[j // half].at[j % half]


def head_rows(kv_refs, tok, first, count, group):
    return tuple(
        jnp.concatenate(
            [
                kv_block(kv_refs, j)[0:tok, at : at + HEAD_DIM]
                for j in range(first, first + count)
            ],
            axis=0,
        )
        for at in (group * HEAD_DIM, KV_WIDTH + group * HEAD_DIM)
    )


def attend_body(
    tok, blocks, me_ref, xg_ref, q_ref, near_ref, far_ref, p0, p1, p2, p3, gains_ref,
    wo_ref, attn_f_ref, ffn_ref, rows_ref, middle_ref, lse_ref, scores_ref, peak_ref, total_ref, mixed_ref,
):
    wide = GROUPS * tok
    kv_refs = (near_ref, far_ref)
    for j, piece in enumerate((p0, p1, p2, p3)):
        rows = piece.shape[0]
        wo_ref[pl.ds(pl.multiple_of((me_ref[0] ^ j) * rows, 16), rows), :] = piece[...]
    x = xg_ref[0:tok, :].astype(f32)
    query_base = xg_ref[tok : tok + 1, 0:1].astype(f32) * tok
    row = lax.broadcasted_iota(jnp.int32, (tok, wide), 0)
    col = lax.broadcasted_iota(jnp.int32, (tok, wide), 1) % tok
    ahead = (row - col).astype(f32)
    q = q_ref[...]
    queries = [group_rows(q, g) for g in range(KV_HEADS)]
    peak_ref[...] = jnp.full(peak_ref.shape, NEG_LARGE, f32)
    total_ref[...] = jnp.zeros(total_ref.shape, f32)
    mixed_ref[...] = jnp.zeros(mixed_ref.shape, f32)

    for j in range(blocks):
        block_ref = kv_block(kv_refs, j)
        allowed = ahead <= query_base - block_ref[tok : tok + 1, 0:1].astype(f32) * tok
        for g in range(KV_HEADS):
            s = dot_cols(block_ref[0:tok, g * HEAD_DIM : (g + 1) * HEAD_DIM], queries[g])
            s = jnp.where(allowed, s, NEG_LARGE)
            scores_ref[g, j] = s
            peak_ref[g : g + 1, :] = jnp.maximum(
                peak_ref[g : g + 1, :], jnp.max(s, axis=0, keepdims=True)
            )

    for j in range(blocks):
        block_ref = kv_block(kv_refs, j)
        for g in range(KV_HEADS):
            p = jnp.exp(scores_ref[g, j] - peak_ref[g : g + 1, :])
            total_ref[g : g + 1, :] += jnp.sum(p, axis=0, keepdims=True)
            at = KV_WIDTH + g * HEAD_DIM
            mixed_ref[g] += dot_rows(block_ref[0:tok, at : at + HEAD_DIM], p.astype(bf16))

    lse_ref[...] = peak_ref[...] + jnp.log(total_ref[...])
    attn_f = ungroup(
        [(mixed_ref[g] / total_ref[g : g + 1, :]).T for g in range(KV_HEADS)], tok
    )
    attn_f_ref[...] = attn_f
    attn_rows = attn_f.astype(bf16)
    middle = x + dot(attn_rows, wo_ref[...])
    middle_ref[...] = middle
    ffn_ref[...] = (middle * inverse_rms(middle) * gains_ref[1:2, :]).astype(bf16)
    rows_ref[...] = attn_rows


def feed_body(
    me_ref, lo_ref, ffn_ref, g0, g1, g2, g3, p0, p1, p2, p3, wd_ref, in_ref, rows_ref,
    m0, m1, m2, m3, dffn_ref, *rest,
):
    grad_refs, (cot_ref, wgu_ref, whole_ref, out_ref) = rest[:-4], rest[-4:]
    part = wd_ref.shape[1]
    tok = g0.shape[1]
    me, lo = me_ref[0], lo_ref[0]
    for j, piece in enumerate((g0, g1, g2, g3)):
        cot_ref[:, pl.ds(pl.multiple_of((me ^ j) * tok, 128), tok)] = piece[...]
    for j, piece in enumerate((p0, p1, p2, p3)):
        rows = piece.shape[0]
        wgu_ref[pl.ds(pl.multiple_of((me ^ j) * rows, 16), rows), :] = piece[...]
    ffn_in = ffn_ref[...]
    cotangent = cot_ref[...]
    wgu = wgu_ref[...]
    wd = wd_ref[...]
    gate_up = dot(ffn_in, wgu)
    gate, up = gate_up[:, :part], gate_up[:, part:]
    sigma = jax.nn.sigmoid(gate)
    swish = gate * sigma
    hidden = (swish * up).astype(bf16)
    d_hidden = dot_rows(cotangent, wd)
    d_gate = (d_hidden * up * sigma * (1.0 + gate * (1.0 - sigma))).astype(bf16)
    d_up = (d_hidden * swish).astype(bf16)
    both = jnp.concatenate([d_gate, d_up], axis=1)
    dffn = dot_cols(both, wgu).astype(bf16)
    out = dot_cols(hidden, wd).astype(bf16)
    for s in range(4):
        dffn_ref[s, 0:tok, :] = dffn[s * tok : (s + 1) * tok, :]
        out_ref[s] = out[s * tok : (s + 1) * tok, :]
    for j, send in enumerate((m0, m1, m2, m3)):
        send[0:tok, :] = out_ref[me ^ j]
        send[tok : 2 * tok, :] = jnp.where((me ^ j) == 2, rows_ref[...], in_ref[...])
    gu_grad = dot_rows(ffn_in, both).astype(bf16)
    down_grad = dot(cotangent, hidden).astype(bf16)
    height = whole_ref.shape[1]
    for t in range(whole_ref.shape[0]):
        whole_ref[t, :, 0 : 2 * part] = gu_grad[t * height : (t + 1) * height, :]
        whole_ref[t, :, 2 * part :] = down_grad[t * height : (t + 1) * height, :]
    for k, grad_ref in enumerate(grad_refs):
        grad_ref[...] = whole_ref[lo ^ k]


def old_body(
    me_ref, flags_ref, mq_ref, mkv_ref, mo_ref, mgu_ref, md_ref, q0, q1, q2, q3, same_ref, other_ref
):
    me, lx, core = me_ref[0], flags_ref[0], flags_ref[1]
    rows = mq_ref.shape[0]
    blank = jnp.zeros((rows, D - KV_WIDTH), f32)
    key = jnp.concatenate([mkv_ref[0], blank], axis=1).astype(bf16)
    value = jnp.concatenate([mkv_ref[1], blank], axis=1).astype(bf16)
    query, out = mq_ref[...].astype(bf16), mo_ref[...].astype(bf16)
    for j, old in enumerate((q0, q1, q2, q3)):
        to = me ^ j
        old[...] = jnp.where(
            to == 0, query, jnp.where(to == 1, key, jnp.where(to == 2, out, value))
        )
    part = md_ref.shape[1]

    @pl.when(lx == 0)
    def _():
        for b in range(4):
            at = slice(b * part, (b + 1) * part)
            gate, up = mgu_ref[0, :, at].astype(bf16), mgu_ref[1, :, at].astype(bf16)
            same_ref[b * rows : (b + 1) * rows, :] = jnp.where(core == 0, gate, up)
            other_ref[b * rows : (b + 1) * rows, :] = jnp.where(core == 0, up, gate)

    @pl.when(lx != 0)
    def _():
        down = md_ref[...].astype(bf16)
        up = jnp.concatenate(
            [mgu_ref[1, :, b * part : (b + 1) * part].astype(bf16) for b in range(4)], axis=0
        )
        same_ref[...] = jnp.where(core == 0, down, up)
        other_ref[...] = jnp.where(core == 0, up, down)


def add_pieces_body(*refs):
    total = refs[0][...].astype(f32)
    for piece in refs[1:-1]:
        total = total + piece[...].astype(f32)
    refs[-1][...] = total.astype(bf16)


def add_slots_body(part, total_ref, got_ref, slots_ref):
    total = (total_ref[...].astype(f32) + got_ref[...].astype(f32)).astype(bf16)
    for lx in range(2):
        for core in range(2):
            number = 1 if core == 1 else 2 * lx
            piece = total[:, number * part : (number + 1) * part]
            for lh in range(slots_ref.shape[0]):
                slots_ref[lh, lx, core] = piece


def back_body(
    tok, blocks, flags_ref, dffn_ref, xg_ref, g_ref, middle_ref, gains_ref, wo_ref, attn_f_ref, q_ref, near_ref,
    far_ref, lse_ref, cos_ref, sin_ref,
    dmid_ref, dq_ref, dbranch_ref, dkv_ref, gain_ref, dq_acc,
):
    wide = GROUPS * tok
    core, kv_refs = flags_ref[1], (near_ref, far_ref)
    query_base = xg_ref[tok : tok + 1, 0:1].astype(f32) * tok
    middle = middle_ref[...]
    inverse = inverse_rms(middle)
    normed = middle * inverse
    d_in = dffn_ref[0, 0:tok, :].astype(f32)
    for i in range(1, dffn_ref.shape[0]):
        d_in = d_in + dffn_ref[i, 0:tok, :].astype(f32)
    gain_ref[...] = jnp.sum(d_in * normed, axis=0, keepdims=True)
    scaled = d_in * gains_ref[1:2, :]
    d_middle = g_ref[...].astype(f32).T + inverse * (
        scaled - normed * jnp.mean(scaled * normed, axis=1, keepdims=True)
    )
    dmid_ref[...] = d_middle
    d_branch = d_middle.astype(bf16)
    dbranch_ref[...] = d_branch
    d_attn = dot_cols(d_branch, wo_ref[...]).astype(bf16)
    attn_f = attn_f_ref[...]
    row = lax.broadcasted_iota(jnp.int32, (tok, wide), 0)
    col = lax.broadcasted_iota(jnp.int32, (tok, wide), 1) % tok
    ahead = (row - col).astype(f32)
    q = q_ref[...]
    queries = [group_rows(q, g) for g in range(KV_HEADS)]
    outs = [group_rows(d_attn, g) for g in range(KV_HEADS)]
    product = d_attn.astype(f32) * attn_f
    deltas = [
        jnp.sum(group_rows(product, g).T, axis=0, keepdims=True) for g in range(KV_HEADS)
    ]
    dq_acc[...] = jnp.zeros(dq_acc.shape, f32)
    count = min(blocks, 8)
    for first in range(0, blocks, count):
        masked = jnp.concatenate(
            [
                jnp.where(
                    ahead
                    <= query_base - kv_block(kv_refs, j)[tok : tok + 1, 0:1].astype(f32) * tok,
                    0.0,
                    NEG_LARGE,
                )
                for j in range(first, first + count)
            ],
            axis=0,
        )
        d_keys, d_values = [], []
        for g in range(KV_HEADS):
            key, value = head_rows(kv_refs, tok, first, count, g)
            p = jnp.exp(dot_cols(key, queries[g]) + (masked - lse_ref[g : g + 1, :]))
            d_weight = dot_cols(value, outs[g])
            ds = (p * (d_weight - deltas[g])).astype(bf16)
            d_values.append(dot(p.astype(bf16), outs[g]).astype(bf16))
            d_keys.append(dot(ds, queries[g]).astype(bf16))
            dq_acc[g] += dot_rows(key, ds)
        both = jnp.concatenate(d_keys + d_values, axis=1)
        for j in range(count):
            dkv_ref[(core * (blocks // 2) + first + j) % blocks] = both[j * tok : (j + 1) * tok, :]
    d_query = ungroup([dq_acc[g].T * 0.125 for g in range(KV_HEADS)], tok)
    dq_ref[...] = turn_wide(d_query, cos_ref[...], -sin_ref[...]).astype(bf16)


def input_body(
    tok, rows, me_ref, dkv_ref, xg_ref, dmid_ref, gains_ref, w_ref, dq_ref, dbranch_ref, gain_two_ref,
    cos_ref, sin_ref, dx_ref, s0, s1, s2, s3, send_ref,
):
    total = dkv_ref[0].astype(f32)
    for i in range(1, dkv_ref.shape[0]):
        total = total + dkv_ref[i].astype(f32)
    d_key = turn_wide(total[:, :KV_WIDTH], cos_ref[...], -sin_ref[...]).astype(bf16)
    d_value = total[:, KV_WIDTH:].astype(bf16)
    cat = jnp.concatenate([d_key, d_value, dq_ref[...]], axis=1)
    d_in = dot_cols(cat, w_ref[...])
    x = xg_ref[0:tok, :].astype(f32)
    inverse = inverse_rms(x)
    normed = x * inverse
    gain_one = jnp.sum(d_in * normed, axis=0, keepdims=True)
    scaled = d_in * gains_ref[0:1, :]
    dx_ref[...] = dmid_ref[...] + inverse * (
        scaled - normed * jnp.mean(scaled * normed, axis=1, keepdims=True)
    )
    gain_two = gain_two_ref[...]
    blank = jnp.zeros((tok, D - KV_WIDTH), bf16)
    columns = (
        dq_ref[...], jnp.concatenate([d_key, blank], axis=1), dbranch_ref[...],
        jnp.concatenate([d_value, blank], axis=1),
    )
    for s, column in enumerate(columns):
        send_ref[s, 0:tok, :] = column
        pair = jnp.concatenate(
            [
                gain_one[:, s * rows : (s + 1) * rows],
                gain_two[:, s * rows : (s + 1) * rows],
                jnp.zeros((6, rows), f32),
            ],
            axis=0,
        )
        send_ref[s, tok:, :] = jnp.concatenate(
            [pair, jnp.zeros((8, D - rows), f32)], axis=1
        ).astype(bf16)
    for j, out_ref in enumerate((s0, s1, s2, s3)):
        out_ref[...] = send_ref[me_ref[0] ^ j]


def finish_body(tok, middle_ref, dx_ref, m0, m1, m2, m3, out_ref):
    output = middle_ref[...]
    for piece in (m0, m1, m2, m3):
        output = output + piece[0:tok, :].astype(f32)
    out_ref[0] = output.T.astype(bf16)
    out_ref[1] = dx_ref[...].T.astype(bf16)


def attn_grad_body(tok, me_ref, lo_ref, r0, r1, r2, r3, m0, m1, m2, m3, *rest):
    out_refs, (rows_ref, cols_ref, whole_ref) = rest[:-3], rest[-3:]
    me, lo = me_ref[0], lo_ref[0]
    gain = jnp.zeros((8, D), f32)
    for j, (cols, piece) in enumerate(((r0, m0), (r1, m1), (r2, m2), (r3, m3))):
        rows_ref[j * tok : (j + 1) * tok, :] = piece[tok : 2 * tok, :]
        cols_ref[j * tok : (j + 1) * tok, :] = cols[0:tok, :]
        gain = gain + cols[tok:, :].astype(f32)
    grad = dot_rows(rows_ref[...], cols_ref[...]).astype(bf16)
    gain = gain.astype(bf16)
    height = whole_ref.shape[1] - 8
    for t in range(whole_ref.shape[0]):
        whole_ref[t, 0:height, :] = grad[t * height : (t + 1) * height, :]
        whole_ref[t, height:, :] = gain
    for k, out_ref in enumerate(out_refs):
        out_ref[...] = whole_ref[lo ^ k]


def add_second_body(total_ref, got_ref, slots_ref, gain_ref):
    total = total_ref[...].astype(f32) + got_ref[...].astype(f32)
    height = slots_ref.shape[1]
    piece = total[0:height, :].astype(bf16)
    for t in range(slots_ref.shape[0]):
        slots_ref[t] = piece
    gain_ref[...] = total[height:, :]


def each_rows(n, block, visit, carry):
    def step(i, value):
        at = pl.multiple_of(i * block, 16)
        return visit(at, pl.ds(at, block), value)

    return lax.fori_loop(0, n // block, step, carry)


def sum_all(rows):
    return jnp.sum(jnp.sum(rows, axis=0, keepdims=True), axis=1, keepdims=True)


def sweeps(z_ref, zb_ref, rest_ref, rest_b_ref, poly_ref, squares, block, steps, unroll=1):
    n = z_ref.shape[0]
    row = lax.broadcasted_iota(jnp.int32, (block, n), 0)
    col = lax.broadcasted_iota(jnp.int32, (block, n), 1)

    def sweep(_, squares):
        center = squares / float(n)
        slope = NS_B + 2.0 * NS_C * center
        lead = NS_A + NS_B * center + NS_C * center * center

        def first(at, here):
            gram = dot_cols(zb_ref[here, :], zb_ref[...])
            rest = jnp.where(row + at == col, gram - center, gram)
            rest_ref[here, :] = rest
            rest_b_ref[here, :] = rest.astype(bf16)

        def second(at, here):
            square = dot(rest_b_ref[here, :], rest_b_ref[...])
            poly_ref[here, :] = (NS_C * square + slope * rest_ref[here, :]).astype(bf16)

        def third(at, here, total):
            z = lead * z_ref[here, :] + dot(poly_ref[here, :], zb_ref[...])
            z_ref[here, :] = z
            return total + sum_all(z * z)

        for at in range(0, n, block):
            first(at, slice(at, at + block))
        for at in range(0, n, block):
            second(at, slice(at, at + block))
        total = jnp.zeros((1, 1), f32)
        for at in range(0, n, block):
            total = third(at, slice(at, at + block), total)
        zb_ref[...] = z_ref[...].astype(bf16)
        return total

    return lax.fori_loop(0, steps, sweep, squares, unroll=unroll)


def normalize(z_ref, zb_ref):
    n = z_ref.shape[0]
    total = each_rows(
        n, 48, lambda at, here, total: total + sum_all(z_ref[here, :] * z_ref[here, :]),
        jnp.zeros((1, 1), f32),
    )
    scale = 1.0 / (jnp.sqrt(total) + 1e-07)

    def visit(at, here, carry):
        z = z_ref[here, :] * scale
        z_ref[here, :] = z
        zb_ref[here, :] = z.astype(bf16)
        return carry

    each_rows(n, 48, visit, 0)
    return total, total * scale * scale


def norm_rows(total, entries, shape):
    value = jnp.broadcast_to(jnp.sqrt(total / entries), shape)
    high = value.astype(bf16).astype(f32)
    row = lax.broadcasted_iota(jnp.int32, shape, 0)
    return jnp.where(row == 0, high, value - high).astype(bf16)


def feed_ns_body(
    flags_ref, near_ref, far_ref, o0, o1, o2, o3, same_ref, other_ref,
    z_ref, g_ref, zb_ref, rest_ref, rest_b_ref, poly_ref,
):
    core, y, rowwise, me = flags_ref[1], flags_ref[2], flags_ref[3] == 1, flags_ref[4]
    n_lo, _, height, part = near_ref.shape
    parts = 4
    rows = D // parts
    for t in range(n_lo):
        for c in range(2):
            here = slice(t * height, (t + 1) * height)
            near = pl.ds(pl.multiple_of((2 * y + c) * part, 128), part)
            far = pl.ds(pl.multiple_of((2 * (1 - y) + c) * part, 128), part)
            g_ref[here, near] = near_ref[t, c]
            g_ref[here, far] = far_ref[t, c]
    for j, old_ref in enumerate((o0, o1, o2, o3)):
        s = me ^ j

        @pl.when(rowwise)
        def _():
            for b in range(parts):
                z_ref[pl.ds(pl.multiple_of(s * rows, 16), rows), b * part : (b + 1) * part] = (
                    MOMENTUM * old_ref[b * rows : (b + 1) * rows, :].astype(f32)
                )

        @pl.when(jnp.logical_not(rowwise))
        def _():
            z_ref[:, pl.ds(pl.multiple_of(s * part, 128), part)] = MOMENTUM * old_ref[...].astype(f32)


    def add(at, here, carry):
        z_ref[here, :] += g_ref[here, :].astype(f32)
        return carry

    each_rows(D, 48, add, 0)
    total, squares = normalize(z_ref, zb_ref)
    sweeps(
        z_ref, zb_ref, rest_ref, rest_b_ref, poly_ref, squares, D // 2, NS_STEPS
    )
    norm = norm_rows(total, jnp.float32(D * parts * part), (8, part))
    for out_ref, to in ((same_ref, core), (other_ref, 1 - core)):
        s = 2 * y + to
        out_ref[D : D + 8, :] = norm
        for first, source in ((0, zb_ref), (D + 8, g_ref)):

            @pl.when(rowwise)
            def _():
                for b in range(parts):
                    out_ref[first + b * rows : first + (b + 1) * rows, :] = source[
                        pl.ds(pl.multiple_of(s * rows, 16), rows), b * part : (b + 1) * part
                    ]

            @pl.when(jnp.logical_not(rowwise))
            def _():
                out_ref[first : first + D, :] = source[
                    :, pl.ds(pl.multiple_of(s * part, 128), part)
                ]


def attn_ns_body(
    me_ref, grad_ref, m0, m1, m2, m3, out_ref, z_ref, zb_ref, rest_ref, rest_b_ref, poly_ref,
    *narrow_refs,
):
    me = me_ref[0]
    narrow = me % 2 == 1
    n_lo, height, _ = grad_ref.shape
    rows = D // 4
    for t in range(n_lo):
        z_ref[t * height : (t + 1) * height, :] = grad_ref[t].astype(f32)
    for j, piece in enumerate((m0, m1, m2, m3)):
        here = pl.ds(pl.multiple_of((me ^ j) * rows, 16), rows)
        z_ref[here, :] += MOMENTUM * piece[...].astype(f32)
    total, squares = normalize(z_ref, zb_ref)

    @pl.when(narrow)
    def _():
        z_ref[...] = z_ref[...].T
        zb_ref[...] = zb_ref[...].T
        part = slice(0, KV_WIDTH)
        sweeps(z_ref.at[part], zb_ref.at[part], *narrow_refs, squares, KV_WIDTH, NS_STEPS)
        zb_ref[...] = zb_ref[...].T

    @pl.when(jnp.logical_not(narrow))
    def _():
        sweeps(z_ref, zb_ref, rest_ref, rest_b_ref, poly_ref, squares, D, NS_STEPS, NS_STEPS)

    count = jnp.where(narrow, float(KV_WIDTH), float(D))
    norm = norm_rows(total, count * D, (8, D))
    for s in range(4):
        out_ref[s, 0:rows, :] = zb_ref[s * rows : (s + 1) * rows, :]
        out_ref[s, rows:, :] = norm


def feed_new_body(
    flags_ref, own, core_ref, even, odd, mgu_ref, md_ref, wgu_ref, wd_ref,
    ggu_ref, gd_ref, ngu_ref, nd_ref, ugu_ref, ud_ref, norm_ref,
):
    lx, core = flags_ref[0], flags_ref[1]
    rate = -RATE * SHAPE_SCALE * math.sqrt(FF)
    rows = mgu_ref.shape[1]
    part = md_ref.shape[1]

    def pick(number, piece):
        if number == 1:
            return jnp.where(core == 1, own[piece, :], core_ref[piece, :]).astype(f32)
        near = jnp.where(core == 0, own[piece, :], core_ref[piece, :])
        far = jnp.where(core == 0, even[piece, :], odd[piece, :])
        return jnp.where(lx == number // 2, near, far).astype(f32)

    for number in range(2):
        for b in range(4):
            at = slice(b * part, (b + 1) * part)
            ortho = pick(number, slice(b * rows, (b + 1) * rows))
            grad = pick(number, slice(D + 8 + b * rows, D + 8 + (b + 1) * rows))
            ggu_ref[number, :, at] = grad
            ngu_ref[number, :, at] = MOMENTUM * mgu_ref[number, :, at] + grad
            ugu_ref[number, :, at] = wgu_ref[number, :, at].astype(f32) + rate * ortho
    grad = pick(2, slice(D + 8, 2 * D + 8))
    gd_ref[...] = grad
    nd_ref[...] = MOMENTUM * md_ref[...] + grad
    ud_ref[...] = wd_ref[...].astype(f32) + rate * pick(2, slice(0, D))
    for number in range(3):
        norm_ref[number] = pick(number, slice(D, D + 8))


def widen_body(results_ref, output_ref, dx_ref):
    output_ref[...] = results_ref[0].astype(f32)
    dx_ref[...] = results_ref[1].astype(f32)


def attn_moment_body(
    tokens, grad_ref, mq_ref, mkv_ref, mo_ref, rows_ref, mg_ref, gains_ref,
    gq, gkv, go, nq, nkv, no, gg, ng, ug,
):
    grad = rows_ref[0:2, 0 : mg_ref.shape[1]]
    moment = MOMENTUM * mg_ref[...] + grad
    gg[...] = grad
    ng[...] = moment
    ug[...] = gains_ref[...].astype(f32) + -GAIN_RATE / math.sqrt(tokens) * moment
    for number, old_ref, grad_out, new_out in ((0, mq_ref, gq, nq), (2, mo_ref, go, no)):
        grad = grad_ref[number].astype(f32)
        grad_out[...] = grad
        new_out[...] = MOMENTUM * old_ref[...] + grad
    for i, number in enumerate((1, 3)):
        grad = grad_ref[number, :, 0:KV_WIDTH].astype(f32)
        gkv[i] = grad
        nkv[i] = MOMENTUM * mkv_ref[i] + grad


def attn_new_body(
    back_ref, feed_norm_ref, wq_ref, wkv_ref, wo_ref, uq, ukv, uo, norm_ref
):
    rate = -RATE * SHAPE_SCALE * math.sqrt(D)
    rows = wq_ref.shape[0]
    uq[...] = wq_ref[...].astype(f32) + rate * back_ref[0, 0:rows, :].astype(f32)
    uo[...] = wo_ref[...].astype(f32) + rate * back_ref[2, 0:rows, :].astype(f32)
    for i, number in enumerate((1, 3)):
        ukv[i] = wkv_ref[i].astype(f32) + rate * back_ref[number, 0:rows, 0:KV_WIDTH].astype(f32)
    for i, number in enumerate((0, 1, 3, 2)):
        norm_ref[i] = jnp.sum(back_ref[number, rows : rows + 2, 0:1].astype(f32))
    for i in range(3):
        norm_ref[4 + i] = jnp.sum(feed_norm_ref[i, 0:2, 0:1])


def trade(x, axis):
    return lax.ppermute(x, axis, TRADE)


def pass_on(x, axis, size, j):
    return lax.ppermute(x, axis, [(i, i ^ j) for i in range(size)])


def spread(x, axis, size):
    return deal(jnp.broadcast_to(x[None], (size,) + x.shape), axis)


def deal(x, axis):
    return lax.all_to_all(x, axis, 0, 0, tiled=True)


def on_device(
    n_hi, n_lo, block_input, out_grad, positions, norm_gains, w_query, w_kv, w_out, w_gate_up,
    w_down, mom_gains, mom_query, mom_kv, mom_out, mom_gate_up, mom_down,
):
    tok = block_input.shape[1]
    rows = w_query.shape[0]
    part = w_down.shape[0]
    n_shard = 4
    n_ctx = n_hi * n_lo
    blocks = 2 * n_lo
    wide = GROUPS * tok
    height = D // n_lo
    at_lx, at_y, at_core = lax.axis_index("lx"), lax.axis_index("y"), lax.axis_index("core")
    me = (at_y * 2 + at_core).astype(jnp.int32)
    lo = lax.axis_index(LO).astype(jnp.int32)[None]
    rowwise = jnp.where(jnp.logical_and(at_lx == 1, at_core == 0), 0, 1)
    flags = jnp.stack([at_lx, at_core, at_y, rowwise, me]).astype(jnp.int32)
    me = me[None]

    moves = []
    for hi in range(2):
        for at in range(n_lo):
            for y in range(2):
                for core in range(2):
                    moves.append(
                        (
                            ((hi * n_lo + at) * 2 + y) * 2 + core,
                            ((core * n_lo + at) * 2 + y) * 2 + hi,
                        )
                    )

    xs, packed = call(
        functools.partial(pack_body, tok),
        [((tok + 8, D), bf16), ((rows + 8, 2 * KV_WIDTH + D), bf16)],
        (positions, block_input[0].T, norm_gains, w_query, w_kv),
        smem=(0,),
    )
    xs = lax.ppermute(xs, ALL, moves)

    def gathered(x):
        far = trade(x, "y")
        return (x, trade(x, "core"), far, trade(far, "core"))

    def pass_shard(pieces):
        return (pieces[0],) + tuple(pass_on(pieces[j], SHARD, n_shard, j) for j in (1, 2, 3))

    attn_weights = gathered(packed)
    wide_parts = call(
        pack_wide_body, [((rows, 2 * part), bf16)] * n_shard, (me, w_gate_up), smem=(0,)
    )
    out_weights = gathered(w_out)
    wide_pieces = pass_shard(wide_parts)
    cot = lax.ppermute(out_grad[0].T, ALL, moves)
    cots = pass_shard((cot,) * n_shard)

    pos = xs[tok, 0].astype(f32) * tok + jnp.arange(tok, dtype=f32)
    half = HEAD_DIM // 2
    lane = jnp.arange(128)
    inverse = 1.0 / 10000.0 ** ((lane % half).astype(f32) * 2.0 / HEAD_DIM)
    angles = pos[:, None] * inverse[None, :]
    cosine = jnp.cos(angles)
    sine = jnp.sin(angles) * jnp.where(lane % HEAD_DIM < half, -1.0, 1.0)[None, :]

    attn_in, query, kv, w_kvq, gains = call(
        functools.partial(project_body, tok),
        [
            ((tok, D), bf16), ((tok, D), bf16), ((n_lo, tok + 8, 2 * KV_WIDTH), bf16),
            ((D, 2 * KV_WIDTH + D), bf16), ((8, D), f32),
        ],
        (me, xs) + attn_weights + (cosine, sine),
        scratch=(pltpu.VMEM((n_shard, 8, 256), f32),),
        smem=(0,),
        hold=(wide_parts[0],) + out_weights[1:],
    )
    kv = deal(kv, LO)
    *attn_old, old_same, old_other = call(
        old_body,
        [((rows, D), bf16)] * n_shard + [((D, part), bf16)] * 2,
        (me, flags, mom_query, mom_kv, mom_out, mom_gate_up, mom_down.T),
        smem=(0, 1),
    )
    kv = after(kv, old_same, cot, *wide_pieces[1:3])
    kv_pair = (kv, trade(kv, "core"))
    w_o, attn_f, ffn_in, attn_rows, middle, lse = call(
        functools.partial(attend_body, tok, blocks),
        [
            ((D, D), bf16), ((tok, D), f32), ((tok, D), bf16), ((tok, D), bf16),
            ((tok, D), f32), ((KV_HEADS, wide), f32),
        ],
        (me, xs, query) + kv_pair + out_weights + (gains,),
        scratch=(
            pltpu.VMEM((KV_HEADS, blocks, tok, wide), f32),
            pltpu.VMEM((KV_HEADS, wide), f32),
            pltpu.VMEM((KV_HEADS, wide), f32),
            pltpu.VMEM((KV_HEADS, HEAD_DIM, wide), f32),
        ),
        smem=(0,),
        limit=64,
    )
    ffn_all = lax.all_gather(after(ffn_in, wide_pieces[3]), SHARD, axis=0, tiled=True)
    old_same, old_other = after(old_same, ffn_all), after(old_other, ffn_all)
    attn_olds = pass_shard([attn_old[0]] + [after(old, ffn_all) for old in attn_old[1:]])
    olds = pass_shard((old_same, old_other, old_same, old_other))
    misc_0, misc_1, misc_2, misc_3, dffn_part, *feed_grads = call(
        feed_body,
        [((2 * tok + 48, D), bf16)] * n_shard + [((n_shard, tok + 8, D), bf16)]
        + [((height, 3 * part), bf16)] * n_lo,
        (me, lo, ffn_all) + cots + wide_pieces + (w_down.T, attn_in, attn_rows),
        scratch=(
            pltpu.VMEM((D, n_shard * tok), bf16), pltpu.VMEM((D, 2 * part), bf16),
            pltpu.VMEM((n_lo, height, 3 * part), bf16), pltpu.VMEM((n_shard, tok, D), bf16),
        ),
        smem=(0, 1),
    )
    dffn = deal(dffn_part, SHARD)
    feed_got = [feed_grads[0]] + [pass_on(feed_grads[k], LO, n_lo, k) for k in range(1, n_lo)]

    misc = pass_shard((misc_0, misc_1, misc_2, misc_3))

    d_middle, d_query, d_branch, dkv, gain_two = call(
        functools.partial(back_body, tok, blocks),
        [
            ((tok, D), f32), ((tok, D), bf16), ((tok, D), bf16),
            ((blocks, tok, 2 * KV_WIDTH), bf16), ((1, D), f32),
        ],
        (flags, dffn, xs, cot, middle, gains, w_o, attn_f, query) + kv_pair + (lse, cosine, sine),
        scratch=(pltpu.VMEM((KV_HEADS, HEAD_DIM, wide), f32),),
        smem=(0,),
    )
    (feed_sum,) = call(
        add_pieces_body, [((height, 3 * part), bf16)], tuple(feed_got), hold=(gain_two,)
    )
    dkv = deal(after(dkv, *feed_got[1:], *olds[1:3], *attn_olds[1:]), ("core",) + LO)
    feed_other = trade(feed_sum, "hi")
    d_input, *sends = call(
        functools.partial(input_body, tok, rows),
        [((tok, D), f32)] + [((tok + 8, D), bf16)] * n_shard,
        (me, dkv, xs, d_middle, gains, w_kvq, d_query, d_branch, gain_two, cosine, sine),
        scratch=(pltpu.VMEM((n_shard, tok + 8, D), bf16),),
        smem=(0,),
        hold=misc[1:],
    )
    sends = pass_shard(sends)
    (feed_slots,) = call(
        functools.partial(add_slots_body, part),
        [((n_lo // 2, 2, 2, height, part), bf16)],
        (feed_sum, feed_other),
        hold=(d_input,),
    )
    feed_near = deal(feed_slots.reshape(n_lo * 2, height, part), LO + ("core",))
    feed_near = feed_near.reshape(n_lo, 2, height, part)
    (finished,) = call(
        functools.partial(finish_body, tok),
        [((2, D, tok), bf16)],
        (middle, d_input) + misc,
    )

    attn_chunks = call(
        functools.partial(attn_grad_body, tok),
        [((height + 8, D), bf16)] * n_lo,
        (me, lo) + sends + misc,
        scratch=(
            pltpu.VMEM((n_shard * tok, D), bf16), pltpu.VMEM((n_shard * tok, D), bf16),
            pltpu.VMEM((n_lo, height + 8, D), bf16),
        ),
        smem=(0, 1),
    )
    feed_near = after(feed_near, attn_chunks[0])
    feed_far = trade(feed_near, "y")
    attn_got = [attn_chunks[0]] + [pass_on(attn_chunks[k], LO, n_lo, k) for k in range(1, n_lo)]
    (attn_sum,) = call(
        add_pieces_body, [((height + 8, D), bf16)], tuple(attn_got), hold=(finished,)
    )
    attn_other = trade(attn_sum, "hi")
    results = lax.ppermute(finished, ALL, moves)
    output, input_grad = call(widen_body, [((D, tok), f32)] * 2, (results,), hold=(attn_sum,))
    attn_slots, gain_rows = call(
        add_second_body,
        [((n_lo, height, D), bf16), ((8, D), f32)],
        (attn_sum, attn_other),
        hold=(output, olds[3]),
    )
    feed_same, feed_other = call(
        feed_ns_body,
        [((2 * D + 8, part), bf16)] * 2,
        (flags, feed_near, feed_far) + olds,
        scratch=(
            pltpu.VMEM((D, FF), f32), pltpu.VMEM((D, FF), bf16), pltpu.VMEM((D, FF), bf16),
            pltpu.VMEM((D, D), f32), pltpu.VMEM((D, D), bf16), pltpu.VMEM((D, D), bf16),
        ),
        smem=(0,),
        hold=(attn_slots,),
    )
    feed_back = (
        feed_same, trade(feed_other, "core"),
        lax.ppermute(feed_same, OWNER, [(0, 2), (2, 0)]),
        lax.ppermute(feed_other, OWNER, [(0, 3), (2, 1)]),
    )
    attn_full = deal(attn_slots, LO)
    attn_rows_back = deal(attn_full.reshape(n_shard, rows, D), SHARD)
    (attn_ortho,) = call(
        attn_ns_body,
        [((n_shard, rows + 8, D), bf16)],
        (me, attn_full) + attn_olds,
        scratch=[pltpu.VMEM((D, D), kind) for kind in (f32, bf16, f32, bf16, bf16)]
        + [pltpu.VMEM((KV_WIDTH, KV_WIDTH), kind) for kind in (f32, bf16, bf16)],
        smem=(0,),
        hold=(feed_same,),
    )
    attn_ortho = after(attn_ortho, feed_back[2])
    attn_back = deal(attn_ortho, SHARD)
    two = [((2, rows, FF), f32), ((D, part), f32)]
    grad_gate_up, grad_down, moment_gate_up, moment_down, new_gate_up, new_down, feed_norm = call(
        feed_new_body,
        two * 3 + [((3, 8, part), f32)],
        (flags,) + feed_back + (mom_gate_up, mom_down.T, w_gate_up, w_down.T),
        smem=(0,),
        hold=(attn_ortho,),
    )
    three = [((rows, D), f32), ((2, rows, KV_WIDTH), f32), ((rows, D), f32)]
    (
        grad_query, grad_kv, grad_out, moment_query, moment_kv, moment_out,
        grad_gains, moment_gains, new_gains,
    ) = call(
        functools.partial(attn_moment_body, tok * n_ctx * n_shard),
        three * 2 + [((2, rows), f32)] * 3,
        (attn_rows_back, mom_query, mom_kv, mom_out, gain_rows, mom_gains, norm_gains),
        hold=(attn_ortho,),
    )
    new_query, new_kv, new_out, momentum_norms = call(
        attn_new_body,
        three + [((7,), f32)],
        (attn_back, feed_norm, w_query, w_kv, w_out),
    )
    return (
        output.T[None], input_grad.T[None],
        grad_gains, grad_query, grad_kv, grad_out, grad_gate_up, grad_down.T,
        moment_gains, moment_query, moment_kv, moment_out, moment_gate_up, moment_down.T,
        momentum_norms,
        new_gains, new_query, new_kv, new_out, new_gate_up, new_down.T,
    )


def solution(mesh):
    n_ctx = mesh.shape["ctx"]
    split = Mesh(mesh.devices.reshape(2, n_ctx // 4, 2, 2, 2), ALL)
    tokens = P(SHARD, CTX, None)
    first, second, gains = P(SHARD, None), P(None, SHARD, None), P(None, SHARD)
    weights = (gains, first, second, first, second, first)
    return jax.shard_map(
        functools.partial(on_device, 2, n_ctx // 2),
        mesh=split,
        in_specs=(tokens, tokens, P(CTX)) + weights + weights,
        out_specs=(tokens, tokens) + weights + weights + (P(),) + weights,
        check_vma=False,
    )
```

```python
import functools
import math

import jax
import jax.numpy as jnp
from jax import lax
from jax.experimental import pallas as pl
from jax.experimental.pallas import tpu as pltpu
from jax.sharding import Mesh
from jax.sharding import PartitionSpec as P

D = 576
FF = 1536
HEAD_DIM = 64
HEADS = 9
KV_HEADS = 3
GROUPS = 3
KV_WIDTH = 192
NS_STEPS = 5
NS_A = 3.4445
NS_B = -4.775
NS_C = 2.0315
NORM_EPS = 1e-05
MOMENTUM = 0.95
RATE = 0.2
SHAPE_SCALE = 0.2
GAIN_RATE = 0.02
NEG_LARGE = -1e30

bf16 = jnp.bfloat16
f32 = jnp.float32
SHARD = ("y", "core")
LO = ("lh", "lx")
OWNER = ("lx", "core")
CTX = ("hi", "lh", "lx")
ALL = ("hi", "lh", "lx", "y", "core")
TRADE = ((0, 1), (1, 0))


def dot(left, right):
    return jnp.dot(left, right, preferred_element_type=f32)


def dot_cols(left, right):
    return lax.dot_general(left, right, (((1,), (1,)), ((), ())), preferred_element_type=f32)


def dot_rows(left, right):
    return lax.dot_general(left, right, (((0,), (0,)), ((), ())), preferred_element_type=f32)


def call(body, outs, args, scratch=(), smem=(), hold=(), limit=64):
    count = len(args)
    spaces = [pltpu.SMEM if i in smem else pltpu.VMEM for i in range(count)]
    spaces += [pl.ANY] * len(hold)

    def run(*refs):
        body(*refs[:count], *refs[count + len(hold) :])

    return pl.pallas_call(
        run,
        name=getattr(body, "func", body).__name__,
        out_shape=[jax.ShapeDtypeStruct(s, d) for s, d in outs],
        in_specs=[pl.BlockSpec(memory_space=space) for space in spaces],
        out_specs=[
            pl.BlockSpec(memory_space=pltpu.SMEM if len(s) == 1 else pltpu.VMEM) for s, _ in outs
        ],
        scratch_shapes=list(scratch),
        compiler_params=pltpu.CompilerParams(vmem_limit_bytes=limit * 2**20),
        cost_estimate=pl.CostEstimate(flops=0, bytes_accessed=1024, transcendentals=0),
    )(*args, *hold)


def after(x, *hold):
    return pl.pallas_call(
        lambda *refs: None,
        name="after",
        out_shape=jax.ShapeDtypeStruct(x.shape, x.dtype),
        in_specs=[pl.BlockSpec(memory_space=pl.ANY)] * (1 + len(hold)),
        out_specs=pl.BlockSpec(memory_space=pl.ANY),
        input_output_aliases={0: 0},
        cost_estimate=pl.CostEstimate(flops=0, bytes_accessed=1024, transcendentals=0),
    )(x, *hold)


def turn(chunk, cosine, sine):
    lane = lax.broadcasted_iota(jnp.int32, chunk.shape, 1)
    other = jnp.where(lane % 64 < 32, pltpu.roll(chunk, 96, 1), pltpu.roll(chunk, 32, 1))
    return chunk * cosine + other * sine


def turn_wide(rows, cosine, sine):
    width = rows.shape[1]
    parts = []
    for at in range(0, width, 128):
        if at + 128 <= width:
            parts.append(turn(rows[:, at : at + 128], cosine, sine))
        else:
            tail = rows[:, at:]
            parts.append(turn(jnp.concatenate([tail, tail], axis=1), cosine, sine)[:, :64])
    return jnp.concatenate(parts, axis=1)


def inverse_rms(rows):
    return lax.rsqrt(jnp.mean(rows * rows, axis=1, keepdims=True) + NORM_EPS)


def pack_body(tok, pos_ref, x_ref, gains_ref, wq_ref, wkv_ref, xs_ref, packed_ref):
    rows = wq_ref.shape[0]
    xs_ref[0:tok, :] = x_ref[...].T
    base = (pos_ref[0] // tok).astype(f32)
    xs_ref[tok:, :] = jnp.full((8, D), base, f32).astype(bf16)
    packed_ref[0:rows, 0:KV_WIDTH] = wkv_ref[0]
    packed_ref[0:rows, KV_WIDTH : 2 * KV_WIDTH] = wkv_ref[1]
    packed_ref[0:rows, 2 * KV_WIDTH :] = wq_ref[...]
    packed_ref[rows:, :] = jnp.zeros((8, packed_ref.shape[1]), bf16)
    packed_ref[rows : rows + 2, 0:rows] = gains_ref[...]


def pack_wide_body(me_ref, wgu_ref, *out_refs):
    me = me_ref[0]
    part = wgu_ref.shape[2] // len(out_refs)
    for j, out_ref in enumerate(out_refs):
        at = pl.multiple_of((me ^ j) * part, 128)
        out_ref[:, 0:part] = wgu_ref[0, :, pl.ds(at, part)]
        out_ref[:, part : 2 * part] = wgu_ref[1, :, pl.ds(at, part)]


def project_body(
    tok, me_ref, xs_ref, p0, p1, p2, p3, cos_ref, sin_ref,
    attn_in_ref, q_ref, kv_ref, w_ref, gains_ref, pieces,
):
    me = me_ref[0]
    rows = p0.shape[0] - 8
    for j, piece in enumerate((p0, p1, p2, p3)):
        at = me ^ j
        w_ref[pl.ds(pl.multiple_of(at * rows, 16), rows), :] = piece[0:rows, :]
        pieces[at] = piece[rows:, 0:256].astype(f32)
    gains = jnp.concatenate([pieces[t, :, 0:rows] for t in range(4)], axis=1)
    gains_ref[...] = gains
    x = xs_ref[0:tok, :].astype(f32)
    attn_in = (x * inverse_rms(x) * gains[0:1, :]).astype(bf16)
    attn_in_ref[...] = attn_in
    cosine, sine = cos_ref[...], sin_ref[...]
    keys_values = dot(attn_in, w_ref[:, 0 : 2 * KV_WIDTH])
    key = turn_wide(keys_values[:, 0:KV_WIDTH], cosine, sine).astype(bf16)
    value = keys_values[:, KV_WIDTH:].astype(bf16)
    for t in range(kv_ref.shape[0]):
        kv_ref[t, 0:tok, 0:KV_WIDTH] = key
        kv_ref[t, 0:tok, KV_WIDTH:] = value
        kv_ref[t, tok:, :] = xs_ref[tok:, 0 : 2 * KV_WIDTH]
    query = dot(attn_in, w_ref[:, 2 * KV_WIDTH :])
    q_ref[...] = turn_wide(query, cosine, sine).astype(bf16) * jnp.asarray(0.125, bf16)


def group_rows(rows, group):
    return jnp.concatenate(
        [
            rows[:, (GROUPS * group + i) * HEAD_DIM : (GROUPS * group + i + 1) * HEAD_DIM]
            for i in range(GROUPS)
        ],
        axis=0,
    )


def ungroup(groups, tok):
    return jnp.concatenate(
        [g[i * tok : (i + 1) * tok, :] for g in groups for i in range(GROUPS)], axis=1
    )


def kv_block(kv_refs, j):
    half = kv_refs[0].shape[0]
    return kv_refs[j // half].at[j % half]


def head_rows(kv_refs, tok, first, count, group):
    return tuple(
        jnp.concatenate(
            [
                kv_block(kv_refs, j)[0:tok, at : at + HEAD_DIM]
                for j in range(first, first + count)
            ],
            axis=0,
        )
        for at in (group * HEAD_DIM, KV_WIDTH + group * HEAD_DIM)
    )


def attend_body(
    tok, blocks, me_ref, xg_ref, q_ref, near_ref, far_ref, p0, p1, p2, p3, gains_ref,
    wo_ref, attn_f_ref, ffn_ref, rows_ref, middle_ref, lse_ref, scores_ref, peak_ref, total_ref, mixed_ref,
):
    wide = GROUPS * tok
    kv_refs = (near_ref, far_ref)
    for j, piece in enumerate((p0, p1, p2, p3)):
        rows = piece.shape[0]
        wo_ref[pl.ds(pl.multiple_of((me_ref[0] ^ j) * rows, 16), rows), :] = piece[...]
    x = xg_ref[0:tok, :].astype(f32)
    query_base = xg_ref[tok : tok + 1, 0:1].astype(f32) * tok
    row = lax.broadcasted_iota(jnp.int32, (tok, wide), 0)
    col = lax.broadcasted_iota(jnp.int32, (tok, wide), 1) % tok
    ahead = (row - col).astype(f32)
    q = q_ref[...]
    queries = [group_rows(q, g) for g in range(KV_HEADS)]
    peak_ref[...] = jnp.full(peak_ref.shape, NEG_LARGE, f32)
    total_ref[...] = jnp.zeros(total_ref.shape, f32)
    mixed_ref[...] = jnp.zeros(mixed_ref.shape, f32)

    for j in range(blocks):
        block_ref = kv_block(kv_refs, j)
        allowed = ahead <= query_base - block_ref[tok : tok + 1, 0:1].astype(f32) * tok
        for g in range(KV_HEADS):
            s = dot_cols(block_ref[0:tok, g * HEAD_DIM : (g + 1) * HEAD_DIM], queries[g])
            s = jnp.where(allowed, s, NEG_LARGE)
            scores_ref[g, j] = s
            peak_ref[g : g + 1, :] = jnp.maximum(
                peak_ref[g : g + 1, :], jnp.max(s, axis=0, keepdims=True)
            )

    for j in range(blocks):
        block_ref = kv_block(kv_refs, j)
        for g in range(KV_HEADS):
            p = jnp.exp(scores_ref[g, j] - peak_ref[g : g + 1, :])
            total_ref[g : g + 1, :] += jnp.sum(p, axis=0, keepdims=True)
            at = KV_WIDTH + g * HEAD_DIM
            mixed_ref[g] += dot_rows(block_ref[0:tok, at : at + HEAD_DIM], p.astype(bf16))

    lse_ref[...] = peak_ref[...] + jnp.log(total_ref[...])
    attn_f = ungroup(
        [(mixed_ref[g] / total_ref[g : g + 1, :]).T for g in range(KV_HEADS)], tok
    )
    attn_f_ref[...] = attn_f
    attn_rows = attn_f.astype(bf16)
    middle = x + dot(attn_rows, wo_ref[...])
    middle_ref[...] = middle
    ffn_ref[...] = (middle * inverse_rms(middle) * gains_ref[1:2, :]).astype(bf16)
    rows_ref[...] = attn_rows


def feed_body(
    me_ref, lo_ref, ffn_ref, g0, g1, g2, g3, p0, p1, p2, p3, wd_ref, in_ref, rows_ref,
    m0, m1, m2, m3, dffn_ref, *rest,
):
    grad_refs, (cot_ref, wgu_ref, whole_ref, out_ref) = rest[:-4], rest[-4:]
    part = wd_ref.shape[1]
    tok = g0.shape[1]
    me, lo = me_ref[0], lo_ref[0]
    for j, piece in enumerate((g0, g1, g2, g3)):
        cot_ref[:, pl.ds(pl.multiple_of((me ^ j) * tok, 128), tok)] = piece[...]
    for j, piece in enumerate((p0, p1, p2, p3)):
        rows = piece.shape[0]
        wgu_ref[pl.ds(pl.multiple_of((me ^ j) * rows, 16), rows), :] = piece[...]
    ffn_in = ffn_ref[...]
    cotangent = cot_ref[...]
    wgu = wgu_ref[...]
    wd = wd_ref[...]
    gate_up = dot(ffn_in, wgu)
    gate, up = gate_up[:, :part], gate_up[:, part:]
    sigma = jax.nn.sigmoid(gate)
    swish = gate * sigma
    hidden = (swish * up).astype(bf16)
    d_hidden = dot_rows(cotangent, wd)
    d_gate = (d_hidden * up * sigma * (1.0 + gate * (1.0 - sigma))).astype(bf16)
    d_up = (d_hidden * swish).astype(bf16)
    both = jnp.concatenate([d_gate, d_up], axis=1)
    dffn = dot_cols(both, wgu).astype(bf16)
    out = dot_cols(hidden, wd).astype(bf16)
    for s in range(4):
        dffn_ref[s, 0:tok, :] = dffn[s * tok : (s + 1) * tok, :]
        out_ref[s] = out[s * tok : (s + 1) * tok, :]
    for j, send in enumerate((m0, m1, m2, m3)):
        send[0:tok, :] = out_ref[me ^ j]
        send[tok : 2 * tok, :] = jnp.where((me ^ j) == 2, rows_ref[...], in_ref[...])
    gu_grad = dot_rows(ffn_in, both).astype(bf16)
    down_grad = dot(cotangent, hidden).astype(bf16)
    height = whole_ref.shape[1]
    for t in range(whole_ref.shape[0]):
        whole_ref[t, :, 0 : 2 * part] = gu_grad[t * height : (t + 1) * height, :]
        whole_ref[t, :, 2 * part :] = down_grad[t * height : (t + 1) * height, :]
    for k, grad_ref in enumerate(grad_refs):
        grad_ref[...] = whole_ref[lo ^ k]


def old_body(
    me_ref, flags_ref, mq_ref, mkv_ref, mo_ref, mgu_ref, md_ref, q0, q1, q2, q3, same_ref, other_ref
):
    me, lx, core = me_ref[0], flags_ref[0], flags_ref[1]
    rows = mq_ref.shape[0]
    blank = jnp.zeros((rows, D - KV_WIDTH), f32)
    key = jnp.concatenate([mkv_ref[0], blank], axis=1).astype(bf16)
    value = jnp.concatenate([mkv_ref[1], blank], axis=1).astype(bf16)
    query, out = mq_ref[...].astype(bf16), mo_ref[...].astype(bf16)
    for j, old in enumerate((q0, q1, q2, q3)):
        to = me ^ j
        old[...] = jnp.where(
            to == 0, query, jnp.where(to == 1, key, jnp.where(to == 2, out, value))
        )
    part = md_ref.shape[1]

    @pl.when(lx == 0)
    def _():
        for b in range(4):
            at = slice(b * part, (b + 1) * part)
            gate, up = mgu_ref[0, :, at].astype(bf16), mgu_ref[1, :, at].astype(bf16)
            same_ref[b * rows : (b + 1) * rows, :] = jnp.where(core == 0, gate, up)
            other_ref[b * rows : (b + 1) * rows, :] = jnp.where(core == 0, up, gate)

    @pl.when(lx != 0)
    def _():
        down = md_ref[...].astype(bf16)
        up = jnp.concatenate(
            [mgu_ref[1, :, b * part : (b + 1) * part].astype(bf16) for b in range(4)], axis=0
        )
        same_ref[...] = jnp.where(core == 0, down, up)
        other_ref[...] = jnp.where(core == 0, up, down)


def add_pieces_body(*refs):
    total = refs[0][...].astype(f32)
    for piece in refs[1:-1]:
        total = total + piece[...].astype(f32)
    refs[-1][...] = total.astype(bf16)


def add_slots_body(part, total_ref, got_ref, slots_ref):
    total = (total_ref[...].astype(f32) + got_ref[...].astype(f32)).astype(bf16)
    for lx in range(2):
        for core in range(2):
            number = 1 if core == 1 else 2 * lx
            piece = total[:, number * part : (number + 1) * part]
            for lh in range(slots_ref.shape[0]):
                slots_ref[lh, lx, core] = piece


def back_body(
    tok, blocks, flags_ref, dffn_ref, xg_ref, g_ref, middle_ref, gains_ref, wo_ref, attn_f_ref, q_ref, near_ref,
    far_ref, lse_ref, cos_ref, sin_ref,
    dmid_ref, dq_ref, dbranch_ref, dkv_ref, gain_ref, dq_acc,
):
    wide = GROUPS * tok
    core, kv_refs = flags_ref[1], (near_ref, far_ref)
    query_base = xg_ref[tok : tok + 1, 0:1].astype(f32) * tok
    middle = middle_ref[...]
    inverse = inverse_rms(middle)
    normed = middle * inverse
    d_in = dffn_ref[0, 0:tok, :].astype(f32)
    for i in range(1, dffn_ref.shape[0]):
        d_in = d_in + dffn_ref[i, 0:tok, :].astype(f32)
    gain_ref[...] = jnp.sum(d_in * normed, axis=0, keepdims=True)
    scaled = d_in * gains_ref[1:2, :]
    d_middle = g_ref[...].astype(f32).T + inverse * (
        scaled - normed * jnp.mean(scaled * normed, axis=1, keepdims=True)
    )
    dmid_ref[...] = d_middle
    d_branch = d_middle.astype(bf16)
    dbranch_ref[...] = d_branch
    d_attn = dot_cols(d_branch, wo_ref[...]).astype(bf16)
    attn_f = attn_f_ref[...]
    row = lax.broadcasted_iota(jnp.int32, (tok, wide), 0)
    col = lax.broadcasted_iota(jnp.int32, (tok, wide), 1) % tok
    ahead = (row - col).astype(f32)
    q = q_ref[...]
    queries = [group_rows(q, g) for g in range(KV_HEADS)]
    outs = [group_rows(d_attn, g) for g in range(KV_HEADS)]
    product = d_attn.astype(f32) * attn_f
    deltas = [
        jnp.sum(group_rows(product, g).T, axis=0, keepdims=True) for g in range(KV_HEADS)
    ]
    dq_acc[...] = jnp.zeros(dq_acc.shape, f32)
    count = min(blocks, 8)
    for first in range(0, blocks, count):
        masked = jnp.concatenate(
            [
                jnp.where(
                    ahead
                    <= query_base - kv_block(kv_refs, j)[tok : tok + 1, 0:1].astype(f32) * tok,
                    0.0,
                    NEG_LARGE,
                )
                for j in range(first, first + count)
            ],
            axis=0,
        )
        d_keys, d_values = [], []
        for g in range(KV_HEADS):
            key, value = head_rows(kv_refs, tok, first, count, g)
            p = jnp.exp(dot_cols(key, queries[g]) + (masked - lse_ref[g : g + 1, :]))
            d_weight = dot_cols(value, outs[g])
            ds = (p * (d_weight - deltas[g])).astype(bf16)
            d_values.append(dot(p.astype(bf16), outs[g]).astype(bf16))
            d_keys.append(dot(ds, queries[g]).astype(bf16))
            dq_acc[g] += dot_rows(key, ds)
        both = jnp.concatenate(d_keys + d_values, axis=1)
        for j in range(count):
            dkv_ref[(core * (blocks // 2) + first + j) % blocks] = both[j * tok : (j + 1) * tok, :]
    d_query = ungroup([dq_acc[g].T * 0.125 for g in range(KV_HEADS)], tok)
    dq_ref[...] = turn_wide(d_query, cos_ref[...], -sin_ref[...]).astype(bf16)


def input_body(
    tok, rows, me_ref, dkv_ref, xg_ref, dmid_ref, gains_ref, w_ref, dq_ref, dbranch_ref, gain_two_ref,
    cos_ref, sin_ref, dx_ref, s0, s1, s2, s3, send_ref,
):
    total = dkv_ref[0].astype(f32)
    for i in range(1, dkv_ref.shape[0]):
        total = total + dkv_ref[i].astype(f32)
    d_key = turn_wide(total[:, :KV_WIDTH], cos_ref[...], -sin_ref[...]).astype(bf16)
    d_value = total[:, KV_WIDTH:].astype(bf16)
    cat = jnp.concatenate([d_key, d_value, dq_ref[...]], axis=1)
    d_in = dot_cols(cat, w_ref[...])
    x = xg_ref[0:tok, :].astype(f32)
    inverse = inverse_rms(x)
    normed = x * inverse
    gain_one = jnp.sum(d_in * normed, axis=0, keepdims=True)
    scaled = d_in * gains_ref[0:1, :]
    dx_ref[...] = dmid_ref[...] + inverse * (
        scaled - normed * jnp.mean(scaled * normed, axis=1, keepdims=True)
    )
    gain_two = gain_two_ref[...]
    blank = jnp.zeros((tok, D - KV_WIDTH), bf16)
    columns = (
        dq_ref[...], jnp.concatenate([d_key, blank], axis=1), dbranch_ref[...],
        jnp.concatenate([d_value, blank], axis=1),
    )
    for s, column in enumerate(columns):
        send_ref[s, 0:tok, :] = column
        pair = jnp.concatenate(
            [
                gain_one[:, s * rows : (s + 1) * rows],
                gain_two[:, s * rows : (s + 1) * rows],
                jnp.zeros((6, rows), f32),
            ],
            axis=0,
        )
        send_ref[s, tok:, :] = jnp.concatenate(
            [pair, jnp.zeros((8, D - rows), f32)], axis=1
        ).astype(bf16)
    for j, out_ref in enumerate((s0, s1, s2, s3)):
        out_ref[...] = send_ref[me_ref[0] ^ j]


def finish_body(tok, middle_ref, dx_ref, m0, m1, m2, m3, out_ref):
    output = middle_ref[...]
    for piece in (m0, m1, m2, m3):
        output = output + piece[0:tok, :].astype(f32)
    out_ref[0] = output.T.astype(bf16)
    out_ref[1] = dx_ref[...].T.astype(bf16)


def attn_grad_body(tok, me_ref, lo_ref, r0, r1, r2, r3, m0, m1, m2, m3, *rest):
    out_refs, (rows_ref, cols_ref, whole_ref) = rest[:-3], rest[-3:]
    me, lo = me_ref[0], lo_ref[0]
    gain = jnp.zeros((8, D), f32)
    for j, (cols, piece) in enumerate(((r0, m0), (r1, m1), (r2, m2), (r3, m3))):
        rows_ref[j * tok : (j + 1) * tok, :] = piece[tok : 2 * tok, :]
        cols_ref[j * tok : (j + 1) * tok, :] = cols[0:tok, :]
        gain = gain + cols[tok:, :].astype(f32)
    grad = dot_rows(rows_ref[...], cols_ref[...]).astype(bf16)
    gain = gain.astype(bf16)
    height = whole_ref.shape[1] - 8
    for t in range(whole_ref.shape[0]):
        whole_ref[t, 0:height, :] = grad[t * height : (t + 1) * height, :]
        whole_ref[t, height:, :] = gain
    for k, out_ref in enumerate(out_refs):
        out_ref[...] = whole_ref[lo ^ k]


def add_second_body(total_ref, got_ref, slots_ref, gain_ref):
    total = total_ref[...].astype(f32) + got_ref[...].astype(f32)
    height = slots_ref.shape[1]
    piece = total[0:height, :].astype(bf16)
    for t in range(slots_ref.shape[0]):
        slots_ref[t] = piece
    gain_ref[...] = total[height:, :]


def each_rows(n, block, visit, carry):
    def step(i, value):
        at = pl.multiple_of(i * block, 16)
        return visit(at, pl.ds(at, block), value)

    return lax.fori_loop(0, n // block, step, carry)


def sum_all(rows):
    return jnp.sum(jnp.sum(rows, axis=0, keepdims=True), axis=1, keepdims=True)


def sweeps(z_ref, zb_ref, rest_ref, rest_b_ref, poly_ref, squares, block, steps, unroll=1):
    n = z_ref.shape[0]
    row = lax.broadcasted_iota(jnp.int32, (block, n), 0)
    col = lax.broadcasted_iota(jnp.int32, (block, n), 1)

    def sweep(_, squares):
        center = squares / float(n)
        slope = NS_B + 2.0 * NS_C * center
        lead = NS_A + NS_B * center + NS_C * center * center

        def first(at, here):
            gram = dot_cols(zb_ref[here, :], zb_ref[...])
            rest = jnp.where(row + at == col, gram - center, gram)
            rest_ref[here, :] = rest
            rest_b_ref[here, :] = rest.astype(bf16)

        def second(at, here):
            square = dot(rest_b_ref[here, :], rest_b_ref[...])
            poly_ref[here, :] = (NS_C * square + slope * rest_ref[here, :]).astype(bf16)

        def third(at, here, total):
            z = lead * z_ref[here, :] + dot(poly_ref[here, :], zb_ref[...])
            z_ref[here, :] = z
            return total + sum_all(z * z)

        for at in range(0, n, block):
            first(at, slice(at, at + block))
        for at in range(0, n, block):
            second(at, slice(at, at + block))
        total = jnp.zeros((1, 1), f32)
        for at in range(0, n, block):
            total = third(at, slice(at, at + block), total)
        zb_ref[...] = z_ref[...].astype(bf16)
        return total

    return lax.fori_loop(0, steps, sweep, squares, unroll=unroll)


def normalize(z_ref, zb_ref):
    n = z_ref.shape[0]
    total = each_rows(
        n, 48, lambda at, here, total: total + sum_all(z_ref[here, :] * z_ref[here, :]),
        jnp.zeros((1, 1), f32),
    )
    scale = 1.0 / (jnp.sqrt(total) + 1e-07)

    def visit(at, here, carry):
        z = z_ref[here, :] * scale
        z_ref[here, :] = z
        zb_ref[here, :] = z.astype(bf16)
        return carry

    each_rows(n, 48, visit, 0)
    return total, total * scale * scale


def norm_rows(total, entries, shape):
    value = jnp.broadcast_to(jnp.sqrt(total / entries), shape)
    high = value.astype(bf16).astype(f32)
    row = lax.broadcasted_iota(jnp.int32, shape, 0)
    return jnp.where(row == 0, high, value - high).astype(bf16)


def feed_ns_body(
    flags_ref, near_ref, far_ref, o0, o1, o2, o3, same_ref, other_ref,
    z_ref, g_ref, zb_ref, rest_ref, rest_b_ref, poly_ref,
):
    core, y, rowwise, me = flags_ref[1], flags_ref[2], flags_ref[3] == 1, flags_ref[4]
    n_lo, _, height, part = near_ref.shape
    parts = 4
    rows = D // parts
    for t in range(n_lo):
        for c in range(2):
            here = slice(t * height, (t + 1) * height)
            near = pl.ds(pl.multiple_of((2 * y + c) * part, 128), part)
            far = pl.ds(pl.multiple_of((2 * (1 - y) + c) * part, 128), part)
            g_ref[here, near] = near_ref[t, c]
            g_ref[here, far] = far_ref[t, c]
    for j, old_ref in enumerate((o0, o1, o2, o3)):
        s = me ^ j

        @pl.when(rowwise)
        def _():
            for b in range(parts):
                z_ref[pl.ds(pl.multiple_of(s * rows, 16), rows), b * part : (b + 1) * part] = (
                    MOMENTUM * old_ref[b * rows : (b + 1) * rows, :].astype(f32)
                )

        @pl.when(jnp.logical_not(rowwise))
        def _():
            z_ref[:, pl.ds(pl.multiple_of(s * part, 128), part)] = MOMENTUM * old_ref[...].astype(f32)


    def add(at, here, carry):
        z_ref[here, :] += g_ref[here, :].astype(f32)
        return carry

    each_rows(D, 48, add, 0)
    total, squares = normalize(z_ref, zb_ref)
    sweeps(
        z_ref, zb_ref, rest_ref, rest_b_ref, poly_ref, squares, D // 2, NS_STEPS, NS_STEPS
    )
    norm = norm_rows(total, jnp.float32(D * parts * part), (8, part))
    for out_ref, to in ((same_ref, core), (other_ref, 1 - core)):
        s = 2 * y + to
        out_ref[D : D + 8, :] = norm
        for first, source in ((0, zb_ref), (D + 8, g_ref)):

            @pl.when(rowwise)
            def _():
                for b in range(parts):
                    out_ref[first + b * rows : first + (b + 1) * rows, :] = source[
                        pl.ds(pl.multiple_of(s * rows, 16), rows), b * part : (b + 1) * part
                    ]

            @pl.when(jnp.logical_not(rowwise))
            def _():
                out_ref[first : first + D, :] = source[
                    :, pl.ds(pl.multiple_of(s * part, 128), part)
                ]


def attn_ns_body(
    me_ref, grad_ref, m0, m1, m2, m3, out_ref, z_ref, zb_ref, rest_ref, rest_b_ref, poly_ref,
    *narrow_refs,
):
    me = me_ref[0]
    narrow = me % 2 == 1
    n_lo, height, _ = grad_ref.shape
    rows = D // 4
    for t in range(n_lo):
        z_ref[t * height : (t + 1) * height, :] = grad_ref[t].astype(f32)
    for j, piece in enumerate((m0, m1, m2, m3)):
        here = pl.ds(pl.multiple_of((me ^ j) * rows, 16), rows)
        z_ref[here, :] += MOMENTUM * piece[...].astype(f32)
    total, squares = normalize(z_ref, zb_ref)

    @pl.when(narrow)
    def _():
        z_ref[...] = z_ref[...].T
        zb_ref[...] = zb_ref[...].T
        part = slice(0, KV_WIDTH)
        sweeps(z_ref.at[part], zb_ref.at[part], *narrow_refs, squares, KV_WIDTH, NS_STEPS)
        zb_ref[...] = zb_ref[...].T

    @pl.when(jnp.logical_not(narrow))
    def _():
        sweeps(z_ref, zb_ref, rest_ref, rest_b_ref, poly_ref, squares, D, NS_STEPS, NS_STEPS)

    count = jnp.where(narrow, float(KV_WIDTH), float(D))
    norm = norm_rows(total, count * D, (8, D))
    for s in range(4):
        out_ref[s, 0:rows, :] = zb_ref[s * rows : (s + 1) * rows, :]
        out_ref[s, rows:, :] = norm


def feed_new_body(
    flags_ref, own, core_ref, even, odd, mgu_ref, md_ref, wgu_ref, wd_ref,
    ggu_ref, gd_ref, ngu_ref, nd_ref, ugu_ref, ud_ref, norm_ref,
):
    lx, core = flags_ref[0], flags_ref[1]
    rate = -RATE * SHAPE_SCALE * math.sqrt(FF)
    rows = mgu_ref.shape[1]
    part = md_ref.shape[1]

    def pick(number, piece):
        if number == 1:
            return jnp.where(core == 1, own[piece, :], core_ref[piece, :]).astype(f32)
        near = jnp.where(core == 0, own[piece, :], core_ref[piece, :])
        far = jnp.where(core == 0, even[piece, :], odd[piece, :])
        return jnp.where(lx == number // 2, near, far).astype(f32)

    for number in range(2):
        for b in range(4):
            at = slice(b * part, (b + 1) * part)
            ortho = pick(number, slice(b * rows, (b + 1) * rows))
            grad = pick(number, slice(D + 8 + b * rows, D + 8 + (b + 1) * rows))
            ggu_ref[number, :, at] = grad
            ngu_ref[number, :, at] = MOMENTUM * mgu_ref[number, :, at] + grad
            ugu_ref[number, :, at] = wgu_ref[number, :, at].astype(f32) + rate * ortho
    grad = pick(2, slice(D + 8, 2 * D + 8))
    gd_ref[...] = grad
    nd_ref[...] = MOMENTUM * md_ref[...] + grad
    ud_ref[...] = wd_ref[...].astype(f32) + rate * pick(2, slice(0, D))
    for number in range(3):
        norm_ref[number] = pick(number, slice(D, D + 8))


def widen_body(results_ref, output_ref, dx_ref):
    output_ref[...] = results_ref[0].astype(f32)
    dx_ref[...] = results_ref[1].astype(f32)


def attn_moment_body(
    tokens, grad_ref, mq_ref, mkv_ref, mo_ref, rows_ref, mg_ref, gains_ref,
    gq, gkv, go, nq, nkv, no, gg, ng, ug,
):
    grad = rows_ref[0:2, 0 : mg_ref.shape[1]]
    moment = MOMENTUM * mg_ref[...] + grad
    gg[...] = grad
    ng[...] = moment
    ug[...] = gains_ref[...].astype(f32) + -GAIN_RATE / math.sqrt(tokens) * moment
    for number, old_ref, grad_out, new_out in ((0, mq_ref, gq, nq), (2, mo_ref, go, no)):
        grad = grad_ref[number].astype(f32)
        grad_out[...] = grad
        new_out[...] = MOMENTUM * old_ref[...] + grad
    for i, number in enumerate((1, 3)):
        grad = grad_ref[number, :, 0:KV_WIDTH].astype(f32)
        gkv[i] = grad
        nkv[i] = MOMENTUM * mkv_ref[i] + grad


def attn_new_body(
    back_ref, feed_norm_ref, wq_ref, wkv_ref, wo_ref, uq, ukv, uo, norm_ref
):
    rate = -RATE * SHAPE_SCALE * math.sqrt(D)
    rows = wq_ref.shape[0]
    uq[...] = wq_ref[...].astype(f32) + rate * back_ref[0, 0:rows, :].astype(f32)
    uo[...] = wo_ref[...].astype(f32) + rate * back_ref[2, 0:rows, :].astype(f32)
    for i, number in enumerate((1, 3)):
        ukv[i] = wkv_ref[i].astype(f32) + rate * back_ref[number, 0:rows, 0:KV_WIDTH].astype(f32)
    for i, number in enumerate((0, 1, 3, 2)):
        norm_ref[i] = jnp.sum(back_ref[number, rows : rows + 2, 0:1].astype(f32))
    for i in range(3):
        norm_ref[4 + i] = jnp.sum(feed_norm_ref[i, 0:2, 0:1])


def trade(x, axis):
    return lax.ppermute(x, axis, TRADE)


def pass_on(x, axis, size, j):
    return lax.ppermute(x, axis, [(i, i ^ j) for i in range(size)])


def spread(x, axis, size):
    return deal(jnp.broadcast_to(x[None], (size,) + x.shape), axis)


def deal(x, axis):
    return lax.all_to_all(x, axis, 0, 0, tiled=True)


def on_device(
    n_hi, n_lo, block_input, out_grad, positions, norm_gains, w_query, w_kv, w_out, w_gate_up,
    w_down, mom_gains, mom_query, mom_kv, mom_out, mom_gate_up, mom_down,
):
    tok = block_input.shape[1]
    rows = w_query.shape[0]
    part = w_down.shape[0]
    n_shard = 4
    n_ctx = n_hi * n_lo
    blocks = 2 * n_lo
    wide = GROUPS * tok
    height = D // n_lo
    at_lx, at_y, at_core = lax.axis_index("lx"), lax.axis_index("y"), lax.axis_index("core")
    me = (at_y * 2 + at_core).astype(jnp.int32)
    lo = lax.axis_index(LO).astype(jnp.int32)[None]
    rowwise = jnp.where(jnp.logical_and(at_lx == 1, at_core == 0), 0, 1)
    flags = jnp.stack([at_lx, at_core, at_y, rowwise, me]).astype(jnp.int32)
    me = me[None]

    moves = []
    for hi in range(2):
        for at in range(n_lo):
            for y in range(2):
                for core in range(2):
                    moves.append(
                        (
                            ((hi * n_lo + at) * 2 + y) * 2 + core,
                            ((core * n_lo + at) * 2 + y) * 2 + hi,
                        )
                    )

    xs, packed = call(
        functools.partial(pack_body, tok),
        [((tok + 8, D), bf16), ((rows + 8, 2 * KV_WIDTH + D), bf16)],
        (positions, block_input[0].T, norm_gains, w_query, w_kv),
        smem=(0,),
    )
    xs = lax.ppermute(xs, ALL, moves)

    def gathered(x):
        far = trade(x, "y")
        return (x, trade(x, "core"), far, trade(far, "core"))

    def pass_shard(pieces):
        return (pieces[0],) + tuple(pass_on(pieces[j], SHARD, n_shard, j) for j in (1, 2, 3))

    attn_weights = gathered(packed)
    wide_parts = call(
        pack_wide_body, [((rows, 2 * part), bf16)] * n_shard, (me, w_gate_up), smem=(0,)
    )
    out_weights = gathered(w_out)
    wide_pieces = pass_shard(wide_parts)
    cot = lax.ppermute(out_grad[0].T, ALL, moves)
    cots = pass_shard((cot,) * n_shard)

    pos = xs[tok, 0].astype(f32) * tok + jnp.arange(tok, dtype=f32)
    half = HEAD_DIM // 2
    lane = jnp.arange(128)
    inverse = 1.0 / 10000.0 ** ((lane % half).astype(f32) * 2.0 / HEAD_DIM)
    angles = pos[:, None] * inverse[None, :]
    cosine = jnp.cos(angles)
    sine = jnp.sin(angles) * jnp.where(lane % HEAD_DIM < half, -1.0, 1.0)[None, :]

    attn_in, query, kv, w_kvq, gains = call(
        functools.partial(project_body, tok),
        [
            ((tok, D), bf16), ((tok, D), bf16), ((n_lo, tok + 8, 2 * KV_WIDTH), bf16),
            ((D, 2 * KV_WIDTH + D), bf16), ((8, D), f32),
        ],
        (me, xs) + attn_weights + (cosine, sine),
        scratch=(pltpu.VMEM((n_shard, 8, 256), f32),),
        smem=(0,),
        hold=(wide_parts[0],) + out_weights[1:],
    )
    kv = deal(kv, LO)
    *attn_old, old_same, old_other = call(
        old_body,
        [((rows, D), bf16)] * n_shard + [((D, part), bf16)] * 2,
        (me, flags, mom_query, mom_kv, mom_out, mom_gate_up, mom_down.T),
        smem=(0, 1),
    )
    kv = after(kv, old_same, cot, *wide_pieces[1:3])
    kv_pair = (kv, trade(kv, "core"))
    w_o, attn_f, ffn_in, attn_rows, middle, lse = call(
        functools.partial(attend_body, tok, blocks),
        [
            ((D, D), bf16), ((tok, D), f32), ((tok, D), bf16), ((tok, D), bf16),
            ((tok, D), f32), ((KV_HEADS, wide), f32),
        ],
        (me, xs, query) + kv_pair + out_weights + (gains,),
        scratch=(
            pltpu.VMEM((KV_HEADS, blocks, tok, wide), f32),
            pltpu.VMEM((KV_HEADS, wide), f32),
            pltpu.VMEM((KV_HEADS, wide), f32),
            pltpu.VMEM((KV_HEADS, HEAD_DIM, wide), f32),
        ),
        smem=(0,),
        limit=64,
    )
    ffn_all = lax.all_gather(after(ffn_in, wide_pieces[3]), SHARD, axis=0, tiled=True)
    old_same, old_other = after(old_same, ffn_all), after(old_other, ffn_all)
    attn_olds = pass_shard([attn_old[0]] + [after(old, ffn_all) for old in attn_old[1:]])
    olds = pass_shard((old_same, old_other, old_same, old_other))
    misc_0, misc_1, misc_2, misc_3, dffn_part, *feed_grads = call(
        feed_body,
        [((2 * tok + 48, D), bf16)] * n_shard + [((n_shard, tok + 8, D), bf16)]
        + [((height, 3 * part), bf16)] * n_lo,
        (me, lo, ffn_all) + cots + wide_pieces + (w_down.T, attn_in, attn_rows),
        scratch=(
            pltpu.VMEM((D, n_shard * tok), bf16), pltpu.VMEM((D, 2 * part), bf16),
            pltpu.VMEM((n_lo, height, 3 * part), bf16), pltpu.VMEM((n_shard, tok, D), bf16),
        ),
        smem=(0, 1),
    )
    dffn = deal(dffn_part, SHARD)
    feed_got = [feed_grads[0]] + [pass_on(feed_grads[k], LO, n_lo, k) for k in range(1, n_lo)]

    misc = pass_shard((misc_0, misc_1, misc_2, misc_3))

    d_middle, d_query, d_branch, dkv, gain_two = call(
        functools.partial(back_body, tok, blocks),
        [
            ((tok, D), f32), ((tok, D), bf16), ((tok, D), bf16),
            ((blocks, tok, 2 * KV_WIDTH), bf16), ((1, D), f32),
        ],
        (flags, dffn, xs, cot, middle, gains, w_o, attn_f, query) + kv_pair + (lse, cosine, sine),
        scratch=(pltpu.VMEM((KV_HEADS, HEAD_DIM, wide), f32),),
        smem=(0,),
    )
    (feed_sum,) = call(
        add_pieces_body, [((height, 3 * part), bf16)], tuple(feed_got), hold=(gain_two,)
    )
    dkv = deal(after(dkv, *feed_got[1:], *olds[1:3], *attn_olds[1:]), ("core",) + LO)
    feed_other = trade(feed_sum, "hi")
    d_input, *sends = call(
        functools.partial(input_body, tok, rows),
        [((tok, D), f32)] + [((tok + 8, D), bf16)] * n_shard,
        (me, dkv, xs, d_middle, gains, w_kvq, d_query, d_branch, gain_two, cosine, sine),
        scratch=(pltpu.VMEM((n_shard, tok + 8, D), bf16),),
        smem=(0,),
        hold=misc[1:],
    )
    sends = pass_shard(sends)
    (feed_slots,) = call(
        functools.partial(add_slots_body, part),
        [((n_lo // 2, 2, 2, height, part), bf16)],
        (feed_sum, feed_other),
        hold=(d_input,),
    )
    feed_near = deal(feed_slots.reshape(n_lo * 2, height, part), LO + ("core",))
    feed_near = feed_near.reshape(n_lo, 2, height, part)
    (finished,) = call(
        functools.partial(finish_body, tok),
        [((2, D, tok), bf16)],
        (middle, d_input) + misc,
    )

    attn_chunks = call(
        functools.partial(attn_grad_body, tok),
        [((height + 8, D), bf16)] * n_lo,
        (me, lo) + sends + misc,
        scratch=(
            pltpu.VMEM((n_shard * tok, D), bf16), pltpu.VMEM((n_shard * tok, D), bf16),
            pltpu.VMEM((n_lo, height + 8, D), bf16),
        ),
        smem=(0, 1),
    )
    feed_near = after(feed_near, attn_chunks[0])
    feed_far = trade(feed_near, "y")
    attn_got = [attn_chunks[0]] + [pass_on(attn_chunks[k], LO, n_lo, k) for k in range(1, n_lo)]
    (attn_sum,) = call(
        add_pieces_body, [((height + 8, D), bf16)], tuple(attn_got), hold=(finished,)
    )
    attn_other = trade(attn_sum, "hi")
    results = lax.ppermute(finished, ALL, moves)
    output, input_grad = call(widen_body, [((D, tok), f32)] * 2, (results,), hold=(attn_sum,))
    attn_slots, gain_rows = call(
        add_second_body,
        [((n_lo, height, D), bf16), ((8, D), f32)],
        (attn_sum, attn_other),
        hold=(output, olds[3]),
    )
    feed_same, feed_other = call(
        feed_ns_body,
        [((2 * D + 8, part), bf16)] * 2,
        (flags, feed_near, feed_far) + olds,
        scratch=(
            pltpu.VMEM((D, FF), f32), pltpu.VMEM((D, FF), bf16), pltpu.VMEM((D, FF), bf16),
            pltpu.VMEM((D, D), f32), pltpu.VMEM((D, D), bf16), pltpu.VMEM((D, D), bf16),
        ),
        smem=(0,),
        hold=(attn_slots,),
    )
    feed_back = (
        feed_same, trade(feed_other, "core"),
        lax.ppermute(feed_same, OWNER, [(0, 2), (2, 0)]),
        lax.ppermute(feed_other, OWNER, [(0, 3), (2, 1)]),
    )
    attn_full = deal(attn_slots, LO)
    attn_rows_back = deal(attn_full.reshape(n_shard, rows, D), SHARD)
    (attn_ortho,) = call(
        attn_ns_body,
        [((n_shard, rows + 8, D), bf16)],
        (me, attn_full) + attn_olds,
        scratch=[pltpu.VMEM((D, D), kind) for kind in (f32, bf16, f32, bf16, bf16)]
        + [pltpu.VMEM((KV_WIDTH, KV_WIDTH), kind) for kind in (f32, bf16, bf16)],
        smem=(0,),
        hold=(feed_same,),
    )
    attn_ortho = after(attn_ortho, feed_back[2])
    attn_back = deal(attn_ortho, SHARD)
    two = [((2, rows, FF), f32), ((D, part), f32)]
    grad_gate_up, grad_down, moment_gate_up, moment_down, new_gate_up, new_down, feed_norm = call(
        feed_new_body,
        two * 3 + [((3, 8, part), f32)],
        (flags,) + feed_back + (mom_gate_up, mom_down.T, w_gate_up, w_down.T),
        smem=(0,),
        hold=(attn_ortho,),
    )
    three = [((rows, D), f32), ((2, rows, KV_WIDTH), f32), ((rows, D), f32)]
    (
        grad_query, grad_kv, grad_out, moment_query, moment_kv, moment_out,
        grad_gains, moment_gains, new_gains,
    ) = call(
        functools.partial(attn_moment_body, tok * n_ctx * n_shard),
        three * 2 + [((2, rows), f32)] * 3,
        (attn_rows_back, mom_query, mom_kv, mom_out, gain_rows, mom_gains, norm_gains),
        hold=(attn_ortho,),
    )
    new_query, new_kv, new_out, momentum_norms = call(
        attn_new_body,
        three + [((7,), f32)],
        (attn_back, feed_norm, w_query, w_kv, w_out),
    )
    return (
        output.T[None], input_grad.T[None],
        grad_gains, grad_query, grad_kv, grad_out, grad_gate_up, grad_down.T,
        moment_gains, moment_query, moment_kv, moment_out, moment_gate_up, moment_down.T,
        momentum_norms,
        new_gains, new_query, new_kv, new_out, new_gate_up, new_down.T,
    )


def solution(mesh):
    n_ctx = mesh.shape["ctx"]
    split = Mesh(mesh.devices.reshape(2, n_ctx // 4, 2, 2, 2), ALL)
    tokens = P(SHARD, CTX, None)
    first, second, gains = P(SHARD, None), P(None, SHARD, None), P(None, SHARD)
    weights = (gains, first, second, first, second, first)
    return jax.shard_map(
        functools.partial(on_device, 2, n_ctx // 2),
        mesh=split,
        in_specs=(tokens, tokens, P(CTX)) + weights + weights,
        out_specs=(tokens, tokens) + weights + weights + (P(),) + weights,
        check_vma=False,
    )
```
